256 devices in a mesh: fsdp: 32 (over z, y_hi, core), tp: 8 (over x, y_lo).
Axes of the slice: x: 4, y: 4 (y_hi: 2, y_lo: 2; y = y_hi * 2 + y_lo), z: 8, core: 2. Of those that a mesh axis runs over, the one named last changes fastest.
Arguments:
- patches: bfloat16 [14336, 3072], P('fsdp'), may hold values from -500 to 500
- cotangent: bfloat16 [14336, 3072], P('fsdp'), may hold values from -6 to 6
- counts: int32 [32, 4], replicated, may hold values from 32 to 112, as said below
- masks: int32 [4], replicated, may hold values from 0 to 31, as said below
- norm_gain: float32 [3072], replicated, may hold values from 0.25 to 1.75
- qk_gain: float32 [2, 128], replicated, may hold values from 0.25 to 1.75
- qkv_weight: bfloat16 [3072, 9216], P('fsdp', 'tp'), may hold values from -0.109375 to 0.109375
- out_weight: bfloat16 [3072, 3072], P('fsdp', 'tp'), may hold values from -0.109375 to 0.109375
Outputs:
- attended: bfloat16 [14336, 3072], P('fsdp', 'tp')
- grad_rows: bfloat16 [14336, 3072], P('fsdp', 'tp')
- grad_qkv_weight: float32 [3072, 9216], P('fsdp', 'tp')
- grad_out_weight: float32 [3072, 3072], P('fsdp', 'tp')
The draws below stay inside these ranges and needn't reach their ends.
Inputs may be any that keep to these rules, and one draw needn't show every extreme that they name: `masks`: in every draw some slot's mask is 31. `counts`: in every draw some run block holds 112 patches in each of its slots.
All inputs are finite; a program needn't handle non-finite values.
Results may differ from the reference program's by a relative error of at most 0.02.
Values may be sent and summed in bfloat16 or wider, within the bound.
A program may use at most 128 MiB of HBM per device.

```python
import math
import jax
import jax.numpy as jnp
from jax import lax

D = 3072
HEADS = 24
HD = 128
CAP = 112
IMGS = 4
PMIN = 32
TOK = 448
TOKENS = 14336
N_FSDP = 32
N_TP = 8


def plan_helper(key):
    masks = jax.random.randint(jax.random.fold_in(key, 11), (IMGS,), 0, N_FSDP).astype(jnp.int32)
    widest = jax.random.randint(jax.random.fold_in(key, 17), (), 0, IMGS)
    masks = jnp.where(jnp.arange(IMGS, dtype=jnp.int32) == widest, N_FSDP - 1, masks).astype(jnp.int32)
    full_replica = jax.random.randint(jax.random.fold_in(key, 14), (), 0, N_FSDP)
    return (masks, full_replica)


def draw_masks(key, part):
    masks, full_replica = plan_helper(key)
    return masks


def draw_counts(key, part):
    masks, full_replica = plan_helper(key)
    key = jax.random.fold_in(key, 3)
    counts = jax.random.randint(key, (N_FSDP, IMGS), PMIN, CAP + 1)
    full_sources = jnp.bitwise_xor(full_replica, masks)
    replica_ids = jnp.arange(N_FSDP, dtype=jnp.int32)
    is_full = replica_ids[:, None] == full_sources[None, :]
    return jnp.where(is_full, CAP, counts).astype(jnp.int32)


def draw_patches(key, part):
    key = jax.random.fold_in(key, 5)
    base_key, row_key, col_key = jax.random.split(key, 3)
    row_scale = jnp.exp(jax.random.uniform(row_key, (TOKENS, 1), jnp.float32, 0.0, math.log(10.0)))
    col_scale = jnp.exp(jax.random.uniform(col_key, (1, D), jnp.float32, 0.0, math.log(10.0)))
    base = jnp.clip(jax.random.normal(base_key, (TOKENS, D), jnp.float32), -5.0, 5.0)
    return (base * row_scale * col_scale).astype(jnp.bfloat16)


def block_levels(own_key, dims, shards, least, top_value):
    gain = 1.0
    for axis_at, parts in shards:
        heights = jax.random.uniform(jax.random.fold_in(jax.random.fold_in(own_key, 6), axis_at), (parts,), jnp.float32, least / len(shards), top_value / len(shards))
        gain = gain * jnp.repeat(jnp.exp(heights), dims[axis_at] // parts).reshape((-1,) + (1,) * (len(dims) - 1 - axis_at))
    return gain


def gaussian(rng, shape, width, reach, pieces=(), kind=jnp.bfloat16):
    loudness = block_levels(rng, shape, pieces, -0.22, 0.18) if pieces else 1.0
    drawn = jax.random.normal(rng, shape, jnp.float32) * width * loudness
    return jnp.minimum(jnp.maximum(drawn, -reach), reach).astype(kind)


def setup_inputs(seed: int = 0) -> dict:
    key_of = jax.random.split(jax.random.key(seed), 9)
    return {
        "patches": draw_patches(jax.random.fold_in(key_of[8], 71), 0),
        "cotangent": gaussian(key_of[1], (TOKENS, D), 1.0, 6.0, ((0, 32),)),
        "counts": draw_counts(jax.random.fold_in(key_of[8], 71), 0),
        "masks": draw_masks(jax.random.fold_in(key_of[8], 71), 0),
        "norm_gain": jnp.clip(1.0 + 0.15 * jax.random.normal(key_of[4], (D,), jnp.float32), 0.25, 1.75),
        "qk_gain": jnp.clip(1.0 + 0.15 * jax.random.normal(key_of[5], (2, HD), jnp.float32), 0.25, 1.75),
        "qkv_weight": gaussian(key_of[6], (D, 3 * HEADS * HD), D ** -0.5, 0.109375, ((0, 32), (1, 8))),
        "out_weight": gaussian(key_of[7], (D, HEADS * HD), (HEADS * HD) ** -0.5, 0.109375, ((0, 32), (1, 8))),
    }


epsilon = 1e-06

def norm_rows(values):
    row_mean = lax.optimization_barrier(jnp.mean(values, axis=-1, keepdims=True))
    centred = values - row_mean
    factor = lax.rsqrt(lax.optimization_barrier(jnp.mean(centred * centred, axis=-1, keepdims=True)) + epsilon)
    return (centred * factor, factor)

def norm_back(upstream, normed, factor):
    return factor * (upstream - lax.optimization_barrier(jnp.mean(upstream, axis=-1, keepdims=True)) - normed * lax.optimization_barrier(jnp.mean(upstream * normed, axis=-1, keepdims=True)))

def group_sum(left_rows, right_rows):
    left_groups = left_rows.reshape(left_rows.shape[0], N_TP, -1).astype(jnp.float32)
    right_groups = right_rows.reshape(right_rows.shape[0], N_TP, -1).astype(jnp.float32)
    partial_value = jnp.einsum('tgc,dgc->gtd', left_groups, right_groups)
    rounded = lax.optimization_barrier(partial_value.astype(jnp.bfloat16))
    return lax.optimization_barrier(jnp.sum(rounded.astype(jnp.float32), axis=0))

def one_replica(block_rows, live_slots, upstream_rows, norm_gain, qk_gain, qkv_weight, out_weight):
    is_live = live_slots.reshape(TOK)
    allowed = live_slots[:, :, None] & live_slots[:, None, :] | jnp.eye(CAP, dtype=bool)[None]
    centred_rows, row_factor = norm_rows(block_rows.astype(jnp.float32))
    normed = (centred_rows * norm_gain.astype(jnp.float32)).astype(jnp.bfloat16)
    projected = jnp.dot(normed, qkv_weight, preferred_element_type=jnp.float32).reshape(IMGS, CAP, HEADS, 3, HD)
    query_hat, query_factor = norm_rows(projected[:, :, :, 0])
    key_hat, key_factor = norm_rows(projected[:, :, :, 1])
    query_scale = qk_gain[0].astype(jnp.float32) * HD ** (-0.5)
    key_scale = qk_gain[1].astype(jnp.float32)
    query = (query_hat * query_scale).astype(jnp.bfloat16)
    key_rows = (key_hat * key_scale).astype(jnp.bfloat16)
    values = projected[:, :, :, 2].astype(jnp.bfloat16)
    scores = jnp.einsum('sqhe,skhe->shqk', query.astype(jnp.float32), key_rows.astype(jnp.float32))
    raised = jnp.where(allowed[:, None], jnp.exp(scores), 0.0)
    attention = raised / lax.optimization_barrier(jnp.sum(raised, axis=-1, keepdims=True))
    rounded_attention = attention.astype(jnp.bfloat16)
    mixed = jnp.einsum('shqk,skhe->sqhe', rounded_attention.astype(jnp.float32), values.astype(jnp.float32))
    mixed = mixed.astype(jnp.bfloat16).reshape(TOK, HEADS * HD)
    attended = jnp.where(is_live[:, None], group_sum(mixed, out_weight), 0.0).astype(jnp.bfloat16)
    upstream_rows = jnp.where(is_live[:, None], upstream_rows, jnp.zeros((), jnp.bfloat16))
    grad_mixed = jnp.dot(upstream_rows, out_weight, preferred_element_type=jnp.float32).astype(jnp.bfloat16)
    grad_heads = grad_mixed.reshape(IMGS, CAP, HEADS, HD).astype(jnp.float32)
    grad_value = jnp.einsum('shqk,sqhe->skhe', rounded_attention.astype(jnp.float32), grad_heads)
    grad_attention = jnp.einsum('sqhe,skhe->shqk', grad_heads, values.astype(jnp.float32))
    grad_scores = attention * (grad_attention - lax.optimization_barrier(jnp.sum(attention * grad_attention, axis=-1, keepdims=True)))
    grad_scores = grad_scores.astype(jnp.bfloat16).astype(jnp.float32)
    grad_query = jnp.einsum('shqk,skhe->sqhe', grad_scores, key_rows.astype(jnp.float32))
    grad_key = jnp.einsum('shqk,sqhe->skhe', grad_scores, query.astype(jnp.float32))
    query_grad = norm_back(grad_query * query_scale, query_hat, query_factor)
    key_grad = norm_back(grad_key * key_scale, key_hat, key_factor)
    grad_qkv = jnp.stack([query_grad, key_grad, grad_value], axis=3).astype(jnp.bfloat16).reshape(TOK, 3 * HEADS * HD)
    qkv_term = lax.dot_general(normed, grad_qkv, (((0,), (0,)), ((), ())), preferred_element_type=jnp.float32).astype(jnp.bfloat16)
    out_term = lax.dot_general(upstream_rows, mixed, (((0,), (0,)), ((), ())), preferred_element_type=jnp.float32).astype(jnp.bfloat16)
    grad_normed = group_sum(grad_qkv, qkv_weight)
    grad_rows = norm_back(grad_normed * norm_gain.astype(jnp.float32), centred_rows, row_factor).astype(jnp.bfloat16)
    return (attended, grad_rows, qkv_term, out_term)

def reference(patches, cotangent, counts, masks, norm_gain, qk_gain, qkv_weight, out_weight):
    slot_ids = jnp.arange(IMGS, dtype=jnp.int32)
    places = jnp.arange(CAP, dtype=jnp.int32)
    replicas = jnp.arange(N_FSDP, dtype=jnp.int32)
    slotted = patches.reshape(N_FSDP, IMGS, CAP, D)

    def replica_step(carry, target):
        sources = jnp.bitwise_xor(target, masks).astype(jnp.int32)
        run_counts = lax.optimization_barrier(jnp.sum(jnp.where(replicas[:, None] == sources[None, :], counts, 0), axis=0)).astype(jnp.int32)
        live_slots = places[None, :] < run_counts[:, None]
        picked = slotted[sources, slot_ids]
        block_rows = jnp.where(live_slots[:, :, None], picked, jnp.zeros((), jnp.bfloat16)).reshape(TOK, D)
        upstream_rows = lax.dynamic_slice_in_dim(cotangent, (target * TOK).astype(jnp.int32), TOK, 0)
        attended, grad_rows, qkv_term, out_term = one_replica(block_rows, live_slots, upstream_rows, norm_gain, qk_gain, qkv_weight, out_weight)
        return ((carry[0] + qkv_term.astype(jnp.float32), carry[1] + out_term.astype(jnp.float32)), (attended, grad_rows))
    initial = (jnp.zeros((D, 3 * HEADS * HD), jnp.float32), jnp.zeros((D, HEADS * HD), jnp.float32))
    (grad_qkv_weight, grad_out_weight), (attended, grad_rows) = lax.scan(replica_step, initial, replicas)
    return (attended.reshape(TOKENS, D), grad_rows.reshape(TOKENS, D), grad_qkv_weight, grad_out_weight)
```

```python
import functools
import jax
import jax.numpy as jnp
from jax import lax
from jax.experimental import pallas as pl
from jax.experimental.pallas import tpu as pltpu
from jax.sharding import PartitionSpec as P

MESH = pl.DeviceIdType.MESH
epsilon = 1e-06
NZ, NX = 8, 4


def coords():
    f = lax.axis_index("fsdp")
    t = lax.axis_index("tp")
    z, yh, c = lax.div(f, 4), lax.rem(lax.div(f, 2), 2), lax.rem(f, 2)
    x, yl = lax.div(t, 2), lax.rem(t, 2)
    return z, yh, c, x, yl


def dev(z, yh, c, x, yl):
    return (z * 4 + yh * 2 + c, x * 2 + yl)


def remote(src, dst, sems, slot, target):
    send, recv = sems
    return pltpu.make_async_remote_copy(
        src_ref=src,
        dst_ref=dst,
        send_sem=send.at[slot],
        recv_sem=recv.at[slot],
        device_id=target,
        device_id_type=MESH,
    )


def greet(partners):
    barrier = pltpu.get_barrier_semaphore()
    for partner in partners:
        pl.semaphore_signal(barrier, inc=1, device_id=partner, device_id_type=MESH)
    pl.semaphore_wait(barrier, len(partners))


def gather_kernel(
    bits_ref, live_ref, patches, qkv_w, out_w, rows, weights,
    hold, got, a_send, a_recv, b_send, b_recv, c_send, c_recv, local_sem,
):
    z, yh, c, x, yl = coords()
    me = dev(z, yh, c, x, yl)
    f, t = me
    slots, slot_rows, share = hold.shape[1], hold.shape[2], hold.shape[3]
    qkv_cols = qkv_w.shape[1]
    z_up, z_down = lax.rem(z + 1, NZ), lax.rem(z + NZ - 1, NZ)
    x_up, x_down = lax.rem(x + 1, NX), lax.rem(x + NX - 1, NX)
    low4, low2 = lax.rem(z, 4), lax.rem(z, 2)
    across = dev(z, 1 - yh, c, x, 1 - yl)
    z7 = dev(7 - z, yh, c, x, yl)
    z3 = dev(z + 3 - 2 * low4, yh, c, x, yl)
    z1 = dev(z + 1 - 2 * low2, yh, c, x, yl)
    sibling = dev(z, yh, 1 - c, x, yl)
    opposite = dev(z, 1 - yh, c, x, yl)
    beside = dev(z, yh, c, x, 1 - yl)
    up, down = dev(z_up, yh, c, x, yl), dev(z_down, yh, c, x, yl)
    right, left = dev(z, yh, c, x_up, yl), dev(z, yh, c, x_down, yl)
    greet([across, z7, z3, z1, sibling, opposite, beside, up, down, right, left])

    sent = []

    def go(copy):
        copy.start()
        sent.append(copy)

    a_sems, b_sems, c_sems = (a_send, a_recv), (b_send, b_recv), (c_send, c_recv)

    def columns(index):
        return pl.ds(pl.multiple_of(index * share, 128), share)

    def slot_at(k):
        return pl.ds(k * slot_rows, slot_rows)

    for k in range(slots):
        go(remote(patches.at[slot_at(k), columns(x * 2 + 1 - yl)], got.at[0, k], a_sems, k, across))
    own = [
        pltpu.make_async_copy(patches.at[slot_at(k), columns(t)], hold.at[0, k], local_sem.at[k])
        for k in range(slots)
    ]
    own_w = [
        pltpu.make_async_copy(qkv_w, weights.at[f, :, pl.ds(0, qkv_cols)], local_sem.at[slots]),
        pltpu.make_async_copy(
            out_w, weights.at[f, :, pl.ds(qkv_cols, weights.shape[2] - qkv_cols)],
            local_sem.at[slots + 1],
        ),
    ]
    for copy in own_w + own:
        copy.start()
    for copy in own_w:
        copy.wait()

    def weight_copy(piece, slot, target):
        return remote(weights.at[piece], weights.at[piece], c_sems, slot, target)

    def fid(zz, kind):
        return zz * 4 + (yh if kind == 0 else 1 - yh) * 2 + c

    def sib_id(zz, kind):
        return zz * 4 + (yh if kind == 0 else 1 - yh) * 2 + 1 - c

    limits = {(0, 0): 4, (0, 1): 3, (1, 0): 3, (1, 1): 4}
    z_slot = {}
    for direction in range(2):
        for kind in range(2):
            for d in range(1, limits[direction, kind] + 1):
                z_slot[direction, kind, d] = 1 + len(z_slot)
    pieces = [(0, 0), (0, 1)]
    core_slot = {}

    def core_index(key):
        if key not in core_slot:
            core_slot[key] = 15 + len(core_slot)
        return core_slot[key]

    def z_at(distance):
        return lax.rem(z + distance + NZ, NZ)

    def share_core(distance, kind):
        go(weight_copy(fid(z_at(distance), kind), core_index((distance, kind)), sibling))

    def z_send(direction, kind, distance_travelled):
        source = z_at(-distance_travelled if direction == 0 else distance_travelled)
        go(
            weight_copy(
                fid(source, kind), z_slot[direction, kind, distance_travelled + 1],
                up if direction == 0 else down,
            )
        )

    def z_receive(direction, kind, d):
        signed = -d if direction == 0 else d
        weight_copy(fid(z_at(signed), kind), z_slot[direction, kind, d], up).wait_recv()
        if d < limits[direction, kind]:
            z_send(direction, kind, d)
        share_core(signed, kind)

    go(weight_copy(f, 0, opposite))
    share_core(0, 0)

    for copy in own:
        copy.wait()

    partner = {3: z3, 7: z7, 1: z1, 0: sibling}
    column = {7: 1, 3: 2, 1: 3, 0: 4}
    order = [[7, 3, 1, 0], [3, 7, 1, 0], [7, 3, 1, 0], [3, 7, 1, 0]]

    def merge(k, step, bit_column):
        remote(got.at[step, k], got.at[step, k], a_sems, step * slots + k, sibling).wait_recv()
        taken = bits_ref[k, bit_column] > 0
        return lax.select_n(taken, hold[step, k], got[step, k])

    for step in range(4):
        for k in range(slots):
            which = order[k][step]
            before = 0 if step == 0 else column[order[k][step - 1]]
            hold[step + 1, k] = merge(k, step, before)
            go(
                remote(
                    hold.at[step + 1, k], got.at[step + 1, k], a_sems,
                    (step + 1) * slots + k, partner[which],
                )
            )
        if step == 0:
            z_send(0, 0, 0)
            z_send(1, 0, 0)
            weight_copy(fid(z, 1), 0, opposite).wait_recv()
            z_send(0, 1, 0)
            z_send(1, 1, 0)
            share_core(0, 1)

    def row_copy(k, xx, y_low, which, target):
        view = rows.at[slot_at(k), columns(xx * 2 + y_low)]
        return remote(view, view, b_sems, k * 7 + which, target)

    for k in range(slots):
        merged = merge(k, 4, column[order[k][3]]).astype(jnp.float32)
        place = lax.broadcasted_iota(jnp.int32, (slot_rows, share), 0)
        live = place < live_ref[k]
        rows[slot_at(k), columns(t)] = jnp.where(live, merged, 0.0).astype(rows.dtype)
        go(row_copy(k, x, yl, 0, beside))
        go(row_copy(k, x, yl, 1, right))
        go(row_copy(k, x, yl, 4, left))

    def rows_second(k):
        row_copy(k, x, 1 - yl, 0, beside).wait_recv()
        go(row_copy(k, x, 1 - yl, 3, right))
        go(row_copy(k, x, 1 - yl, 5, left))

    def rows_third(k):
        row_copy(k, x_down, yl, 1, right).wait_recv()
        go(row_copy(k, x_down, yl, 2, right))
        row_copy(k, x_up, 1 - yl, 5, left).wait_recv()
        go(row_copy(k, x_up, 1 - yl, 6, left))

    for d in range(1, 5):
        for kind in range(2):
            for direction in range(2):
                if d <= limits[direction, kind]:
                    z_receive(direction, kind, d)
        if d == 1:
            for k in range(slots):
                rows_second(k)
                rows_third(k)
    for k in range(slots):
        row_copy(k, lax.rem(x + 2, NX), yl, 2, right).wait_recv()
        row_copy(k, x_down, 1 - yl, 3, right).wait_recv()
        row_copy(k, x_up, yl, 4, left).wait_recv()
        row_copy(k, lax.rem(x + 2, NX), 1 - yl, 6, left).wait_recv()
    for (distance, kind), slot in core_slot.items():
        weight_copy(sib_id(z_at(distance), kind), slot, sibling).wait_recv()
    for copy in sent:
        copy.wait_send()


def gather(bits, live, patches, qkv_w, out_w):
    tok, model = patches.shape
    slots = bits.shape[0]
    share = model // 8
    slot_rows = tok // slots
    bf16 = jnp.bfloat16
    depth, wide = qkv_w.shape[0], qkv_w.shape[1] + out_w.shape[1]
    hbm = pl.BlockSpec(memory_space=pl.ANY)
    smem = pl.BlockSpec(memory_space=pltpu.SMEM)
    return pl.pallas_call(
        gather_kernel,
        out_shape=(
            jax.ShapeDtypeStruct((tok, model), bf16),
            jax.ShapeDtypeStruct((32, depth, wide), bf16),
        ),
        in_specs=[smem, smem, hbm, hbm, hbm],
        out_specs=(pl.BlockSpec(memory_space=pltpu.VMEM), hbm),
        scratch_shapes=[
            pltpu.VMEM((5, slots, slot_rows, share), bf16),
            pltpu.VMEM((5, slots, slot_rows, share), bf16),
            pltpu.SemaphoreType.DMA((5 * slots,)),
            pltpu.SemaphoreType.DMA((5 * slots,)),
            pltpu.SemaphoreType.DMA((7 * slots,)),
            pltpu.SemaphoreType.DMA((7 * slots,)),
            pltpu.SemaphoreType.DMA((31,)),
            pltpu.SemaphoreType.DMA((31,)),
            pltpu.SemaphoreType.DMA((slots + 2,)),
        ],
        compiler_params=pltpu.CompilerParams(
            collective_id=0, has_side_effects=True, vmem_limit_bytes=24 * 2**20
        ),
        cost_estimate=pl.CostEstimate(flops=0, bytes_accessed=24 * 2**20, transcendentals=0),
    )(bits, live, patches, qkv_w, out_w)


def add_into(total, other, rows_at=16):
    @pl.loop(0, total.shape[0] // rows_at)
    def _(i):
        at = pl.ds(pl.multiple_of(i * rows_at, rows_at), rows_at)
        total[at, :] = (
            total[at, :].astype(jnp.float32) + other[at, :].astype(jnp.float32)
        ).astype(total.dtype)


def reduce_kernel(
    qkv_term, out_term, value_part, back_part,
    grad_w, value_sum, back_sum,
    mine, theirs, z_got, y_got, parts, x_got, l_got,
    core_send, core_recv, z_send_sem, z_recv_sem, y_send, y_recv,
    x_send, x_recv, l_send, l_recv, local_sem,
):
    z, yh, c, x, yl = coords()
    qkv_cols, out_cols = qkv_term.shape[-1], out_term.shape[-1]
    share = value_sum.shape[1]
    z_up, z_down = lax.rem(z + 1, NZ), lax.rem(z + NZ - 1, NZ)
    x_up, x_down = lax.rem(x + 1, NX), lax.rem(x + NX - 1, NX)
    sibling = dev(z, yh, 1 - c, x, yl)
    opposite = dev(z, 1 - yh, c, x, yl)
    beside = dev(z, yh, c, x, 1 - yl)
    up, down = dev(z_up, yh, c, x, yl), dev(z_down, yh, c, x, yl)
    right, left = dev(z, yh, c, x_up, yl), dev(z, yh, c, x_down, yl)
    greet([sibling, opposite, beside, up, down, right, left])
    sent = []

    def go(copy):
        copy.start()
        sent.append(copy)

    core_sems, z_sems = (core_send, core_recv), (z_send_sem, z_recv_sem)
    y_sems, x_sems, l_sems = (y_send, y_recv), (x_send, x_recv), (l_send, l_recv)
    left_cols, right_cols = pl.ds(0, qkv_cols), pl.ds(qkv_cols, out_cols)

    def z_at(distance):
        return lax.rem(z + distance + NZ, NZ)

    distances = [4, 3, -3, 2, -2, 1, -1, 0]
    local = []
    for i, distance in enumerate(distances):
        zz = z_at(distance)
        for j, (term, cols) in enumerate(((qkv_term, left_cols), (out_term, right_cols))):
            go(
                remote(
                    term.at[zz, :, 1 - c], theirs.at[zz, :, :, cols], core_sems, i * 2 + j, sibling
                )
            )
            copy = pltpu.make_async_copy(
                term.at[zz, :, c], mine.at[zz, :, :, cols], local_sem.at[i * 2 + j]
            )
            copy.start()
            local.append(copy)
        if i == 0:
            for p, part in enumerate((value_part, back_part)):
                for shard in range(8):
                    copy = pltpu.make_async_copy(
                        part.at[:, pl.ds(shard * share, share)],
                        parts.at[p, shard],
                        local_sem.at[16 + p * 8 + shard],
                    )
                    copy.start()
                    local.append(copy)
    part_copies = local[2:18]
    term_copies = local[:2] + local[18:]

    def have(distance):
        i = distances.index(distance)
        zz = z_at(distance)
        for j, (term, cols) in enumerate(((qkv_term, left_cols), (out_term, right_cols))):
            term_copies[i * 2 + j].wait()
            remote(
                term.at[zz, :, c], theirs.at[zz, :, :, cols], core_sems, i * 2 + j, sibling
            ).wait_recv()
        for y in range(2):
            add_into(mine.at[zz, y], theirs.at[zz, y])

    def y_of(kind):
        return yh if kind == 0 else 1 - yh

    limits = {(0, 0): 4, (0, 1): 3, (1, 0): 3, (1, 1): 4}
    z_slot = {}
    for direction in range(2):
        for kind in range(2):
            for d in range(limits[direction, kind], 0, -1):
                z_slot[direction, kind, d] = len(z_slot)

    def z_go(direction, kind, d):
        zz = z_at(d if direction == 0 else -d)
        slot = z_slot[direction, kind, d]
        go(
            remote(
                mine.at[zz, y_of(kind)], z_got.at[slot], z_sems, slot,
                up if direction == 0 else down,
            )
        )

    def z_take(direction, kind, d):
        zz = z_at(d - 1 if direction == 0 else 1 - d)
        slot = z_slot[direction, kind, d]
        remote(mine.at[zz, y_of(kind)], z_got.at[slot], z_sems, slot, up).wait_recv()
        add_into(mine.at[zz, y_of(kind)], z_got.at[slot])

    x_limits = {(0, 0): 2, (0, 1): 1, (1, 0): 1, (1, 1): 2}
    x_slot = {}
    for p in range(2):
        for direction in range(2):
            for kind in range(2):
                for d in range(x_limits[direction, kind], 0, -1):
                    x_slot[p, direction, kind, d] = len(x_slot)

    def x_shard(direction, kind, d):
        xx = lax.rem(x + (d if direction == 0 else NX - d), NX)
        return xx * 2 + (yl if kind == 0 else 1 - yl)

    def x_go(p, direction, kind, d):
        slot = x_slot[p, direction, kind, d]
        go(
            remote(
                parts.at[p, x_shard(direction, kind, d)], x_got.at[slot], x_sems, slot,
                right if direction == 0 else left,
            )
        )

    def x_take(p, direction, kind, d):
        slot = x_slot[p, direction, kind, d]
        shard = x_shard(direction, kind, d - 1)
        remote(parts.at[p, shard], x_got.at[slot], x_sems, slot, right).wait_recv()
        add_into(parts.at[p, shard], x_got.at[slot])

    def x_first(p):
        for shard in range(8):
            part_copies[p * 8 + shard].wait()
        for d in (2, 1):
            for kind in (1, 0):
                for direction in range(2):
                    if d == x_limits[direction, kind]:
                        x_go(p, direction, kind, d)

    def x_second(p):
        x_take(p, 1, 1, 2)
        x_go(p, 1, 1, 1)
        x_take(p, 0, 0, 2)
        x_go(p, 0, 0, 1)

    def x_third(p):
        x_take(p, 0, 1, 1)
        x_take(p, 1, 1, 1)
        go(remote(parts.at[p, x * 2 + 1 - yl], l_got.at[p], l_sems, p, beside))
        x_take(p, 1, 0, 1)
        x_take(p, 0, 0, 1)

    def x_last(p, out):
        remote(parts.at[p, x * 2 + yl], l_got.at[p], l_sems, p, beside).wait_recv()

        @pl.loop(0, out.shape[0] // 16)
        def _(i):
            at = pl.ds(pl.multiple_of(i * 16, 16), 16)
            out[at, :] = parts[p, x * 2 + yl, at, :].astype(jnp.float32) + l_got[
                p, at, :
            ].astype(jnp.float32)

    x_first(0)
    have(4)
    z_go(1, 1, 4)
    z_go(0, 0, 4)
    have(3)
    z_go(0, 1, 3)
    have(-3)
    z_go(1, 0, 3)
    x_first(1)
    have(2)
    have(-2)
    x_second(0)
    z_take(1, 1, 4)
    z_go(1, 1, 3)
    z_take(0, 0, 4)
    z_go(0, 0, 3)
    z_take(0, 1, 3)
    z_go(0, 1, 2)
    z_take(1, 0, 3)
    z_go(1, 0, 2)
    x_third(0)
    have(1)
    have(-1)
    have(0)
    z_take(1, 1, 3)
    z_go(1, 1, 2)
    z_take(0, 0, 3)
    z_go(0, 0, 2)
    x_second(1)
    z_take(0, 1, 2)
    z_go(0, 1, 1)
    z_take(1, 0, 2)
    z_go(1, 0, 1)
    x_last(0, value_sum)
    z_take(1, 1, 2)
    z_go(1, 1, 1)
    z_take(0, 0, 2)
    z_go(0, 0, 1)
    x_third(1)
    z_take(0, 1, 1)
    z_take(1, 1, 1)
    go(remote(mine.at[z, 1 - yh], y_got, y_sems, 0, opposite))
    z_take(1, 0, 1)
    z_take(0, 0, 1)
    x_last(1, back_sum)
    remote(mine.at[z, yh], y_got, y_sems, 0, opposite).wait_recv()

    @pl.loop(0, grad_w.shape[0] // 16)
    def _(i):
        at = pl.ds(pl.multiple_of(i * 16, 16), 16)
        grad_w[at, :] = mine[z, yh, at, :].astype(jnp.float32) + y_got[at, :].astype(jnp.float32)

    for copy in sent:
        copy.wait_send()


def reduce(qkv_term, out_term, value_part, back_part):
    bf16, f32 = jnp.bfloat16, jnp.float32
    model, qkv_cols = qkv_term.shape
    out_cols = out_term.shape[1]
    wide = qkv_cols + out_cols
    depth = model // 32
    tok = value_part.shape[0]
    share = model // 8
    hbm = pl.BlockSpec(memory_space=pl.ANY)
    vmem = pl.BlockSpec(memory_space=pltpu.VMEM)
    dma = pltpu.SemaphoreType.DMA
    return pl.pallas_call(
        reduce_kernel,
        out_shape=(
            jax.ShapeDtypeStruct((depth, wide), f32),
            jax.ShapeDtypeStruct((tok, share), f32),
            jax.ShapeDtypeStruct((tok, share), f32),
        ),
        in_specs=[hbm] * 4,
        out_specs=(vmem,) * 3,
        scratch_shapes=[
            pltpu.VMEM((NZ, 2, depth, wide), bf16),
            pltpu.VMEM((NZ, 2, depth, wide), bf16),
            pltpu.VMEM((14, depth, wide), bf16),
            pltpu.VMEM((depth, wide), bf16),
            pltpu.VMEM((2, 8, tok, share), bf16),
            pltpu.VMEM((12, tok, share), bf16),
            pltpu.VMEM((2, tok, share), bf16),
            dma((16,)), dma((16,)), dma((14,)), dma((14,)), dma((1,)), dma((1,)),
            dma((12,)), dma((12,)), dma((2,)), dma((2,)), dma((32,)),
        ],
        compiler_params=pltpu.CompilerParams(
            collective_id=1, has_side_effects=True, vmem_limit_bytes=40 * 2**20
        ),
        cost_estimate=pl.CostEstimate(flops=0, bytes_accessed=30 * 2**20, transcendentals=0),
    )(
        qkv_term.reshape(NZ, 2, 2, depth, qkv_cols),
        out_term.reshape(NZ, 2, 2, depth, out_cols),
        value_part,
        back_part,
    )


def norm_rows(values):
    row_mean = jnp.mean(values, axis=-1, keepdims=True)
    centred = values - row_mean
    factor = lax.rsqrt(jnp.mean(centred * centred, axis=-1, keepdims=True) + epsilon)
    return (centred * factor, factor)


def norm_back(upstream, normed, factor):
    return factor * (
        upstream
        - jnp.mean(upstream, axis=-1, keepdims=True)
        - normed * jnp.mean(upstream * normed, axis=-1, keepdims=True)
    )


def per_device(patches, cotangent, counts, masks, norm_gain, qk_gain, qkv_weight, out_weight):
    replicas = lax.axis_size("fsdp")
    groups = lax.axis_size("tp")
    my_replica = lax.axis_index("fsdp")
    my_group = lax.axis_index("tp")
    tok_rows = patches.shape[0]
    images = counts.shape[1]
    slot_rows = tok_rows // images
    model_width = norm_gain.shape[0]
    share_width = model_width // groups
    head_dim = qk_gain.shape[1]
    qkv_cols = qkv_weight.shape[1]
    out_cols = out_weight.shape[1]
    local_heads = out_cols // head_dim
    bit = [jnp.bitwise_and(jnp.right_shift(masks, place), 1) for place in range(5)]
    bits = jnp.stack(
        [bit[1], bit[4], bit[3] ^ bit[4], bit[2] ^ bit[3], bit[0]], axis=1
    ).astype(jnp.int32)
    replica_ids = jnp.arange(replicas, dtype=jnp.int32)
    sources = jnp.bitwise_xor(my_replica, masks)
    run_counts = jnp.sum(jnp.where(replica_ids[:, None] == sources[None, :], counts, 0), axis=0)
    places = jnp.arange(slot_rows, dtype=jnp.int32)
    live_slots = places[None, :] < run_counts[:, None]
    is_live = live_slots.reshape(tok_rows)
    allowed = live_slots[:, :, None] & live_slots[:, None, :] | jnp.eye(slot_rows, dtype=bool)[None]
    block_rows, weights = gather(
        bits, run_counts.astype(jnp.int32), patches, qkv_weight, out_weight
    )
    weights = weights.reshape(model_width, qkv_cols + out_cols)
    qkv_full, out_full = weights[:, :qkv_cols], weights[:, qkv_cols:]
    centred_rows, row_factor = norm_rows(block_rows.astype(jnp.float32))
    normed = (centred_rows * norm_gain).astype(jnp.bfloat16)
    projected = jnp.dot(normed, qkv_full, preferred_element_type=jnp.float32).reshape(
        images, slot_rows, local_heads, 3, head_dim
    )
    query_hat, query_factor = norm_rows(projected[:, :, :, 0])
    key_hat, key_factor = norm_rows(projected[:, :, :, 1])
    query_scale = qk_gain[0] * head_dim ** (-0.5)
    key_scale = qk_gain[1]
    query = (query_hat * query_scale).astype(jnp.bfloat16)
    key_rows = (key_hat * key_scale).astype(jnp.bfloat16)
    values = projected[:, :, :, 2].astype(jnp.bfloat16)
    scores = jnp.einsum("sqhe,skhe->shqk", query, key_rows, preferred_element_type=jnp.float32)
    raised = jnp.where(allowed[:, None], jnp.exp(scores), 0.0)
    attention = raised / jnp.sum(raised, axis=-1, keepdims=True)
    rounded_attention = attention.astype(jnp.bfloat16)
    mixed = jnp.einsum(
        "shqk,skhe->sqhe", rounded_attention, values, preferred_element_type=jnp.float32
    )
    mixed = mixed.astype(jnp.bfloat16).reshape(tok_rows, out_cols)
    partial_value = lax.dot_general(
        mixed, out_full, (((1,), (1,)), ((), ())), preferred_element_type=jnp.float32
    )
    upstream_rows = jnp.where(is_live[:, None], cotangent, jnp.zeros((), cotangent.dtype))
    grad_mixed = jnp.dot(upstream_rows, out_full, preferred_element_type=jnp.float32).astype(
        jnp.bfloat16
    )
    grad_heads = grad_mixed.reshape(images, slot_rows, local_heads, head_dim)
    grad_value = jnp.einsum(
        "shqk,sqhe->skhe", rounded_attention, grad_heads, preferred_element_type=jnp.float32
    )
    grad_attention = jnp.einsum(
        "sqhe,skhe->shqk", grad_heads, values, preferred_element_type=jnp.float32
    )
    grad_scores = attention * (
        grad_attention - jnp.sum(attention * grad_attention, axis=-1, keepdims=True)
    )
    grad_scores = grad_scores.astype(jnp.bfloat16)
    grad_query = jnp.einsum(
        "shqk,skhe->sqhe", grad_scores, key_rows, preferred_element_type=jnp.float32
    )
    grad_key = jnp.einsum("shqk,sqhe->skhe", grad_scores, query, preferred_element_type=jnp.float32)
    query_grad = norm_back(grad_query * query_scale, query_hat, query_factor)
    key_grad = norm_back(grad_key * key_scale, key_hat, key_factor)
    grad_qkv = (
        jnp.stack([query_grad, key_grad, grad_value], axis=3)
        .astype(jnp.bfloat16)
        .reshape(tok_rows, qkv_cols)
    )
    qkv_term = lax.dot_general(
        normed, grad_qkv, (((0,), (0,)), ((), ())), preferred_element_type=jnp.float32
    )
    out_term = lax.dot_general(
        upstream_rows, mixed, (((0,), (0,)), ((), ())), preferred_element_type=jnp.float32
    )
    partial_back = lax.dot_general(
        grad_qkv, qkv_full, (((1,), (1,)), ((), ())), preferred_element_type=jnp.float32
    )
    partial_back = partial_back.astype(jnp.bfloat16)
    scaled = partial_back.astype(jnp.float32) * norm_gain
    sums = jnp.stack([jnp.sum(scaled, -1), jnp.sum(scaled * centred_rows, -1)])
    sums = lax.psum(sums, "tp") / model_width
    grad_w, value_sum, back_sum = reduce(
        qkv_term.astype(jnp.bfloat16),
        out_term.astype(jnp.bfloat16),
        partial_value.astype(jnp.bfloat16),
        partial_back,
    )
    attended = jnp.where(is_live[:, None], value_sum, 0.0).astype(jnp.bfloat16)
    gain_share = lax.dynamic_slice_in_dim(norm_gain, my_group * share_width, share_width, 0)
    centred_share = lax.dynamic_slice_in_dim(
        centred_rows, my_group * share_width, share_width, 1
    )
    grad_rows = row_factor * (
        back_sum * gain_share - sums[0][:, None] - centred_share * sums[1][:, None]
    )
    grad_rows = grad_rows.astype(jnp.bfloat16)
    return (attended, grad_rows, grad_w[:, :qkv_cols], grad_w[:, qkv_cols:])


def solution(mesh):
    in_specs = (
        P("fsdp", None),
        P("fsdp", None),
        P(),
        P(),
        P(),
        P(),
        P("fsdp", "tp"),
        P("fsdp", "tp"),
    )
    out_specs = (P("fsdp", "tp"), P("fsdp", "tp"), P("fsdp", "tp"), P("fsdp", "tp"))
    return jax.shard_map(
        per_device, mesh=mesh, in_specs=in_specs, out_specs=out_specs, check_vma=False
    )
```

```python
import functools
import jax
import jax.numpy as jnp
from jax import lax
from jax.experimental import pallas as pl
from jax.experimental.pallas import tpu as pltpu
from jax.sharding import PartitionSpec as P

MESH = pl.DeviceIdType.MESH
epsilon = 1e-06
NZ, NX = 8, 4


def coords():
    f = lax.axis_index("fsdp")
    t = lax.axis_index("tp")
    z, yh, c = lax.div(f, 4), lax.rem(lax.div(f, 2), 2), lax.rem(f, 2)
    x, yl = lax.div(t, 2), lax.rem(t, 2)
    return z, yh, c, x, yl


def dev(z, yh, c, x, yl):
    return (z * 4 + yh * 2 + c, x * 2 + yl)


def remote(src, dst, sems, slot, target):
    send, recv = sems
    return pltpu.make_async_remote_copy(
        src_ref=src,
        dst_ref=dst,
        send_sem=send.at[slot],
        recv_sem=recv.at[slot],
        device_id=target,
        device_id_type=MESH,
    )


def greet(partners):
    barrier = pltpu.get_barrier_semaphore()
    for partner in partners:
        pl.semaphore_signal(barrier, inc=1, device_id=partner, device_id_type=MESH)
    pl.semaphore_wait(barrier, len(partners))


def gather_kernel(
    bits_ref, live_ref, patches, qkv_w, out_w, rows, weights,
    hold, got, a_send, a_recv, b_send, b_recv, c_send, c_recv, local_sem,
):
    z, yh, c, x, yl = coords()
    me = dev(z, yh, c, x, yl)
    f, t = me
    slots, slot_rows, share = hold.shape[1], hold.shape[2], hold.shape[3]
    qkv_cols = qkv_w.shape[1]
    z_up, z_down = lax.rem(z + 1, NZ), lax.rem(z + NZ - 1, NZ)
    x_up, x_down = lax.rem(x + 1, NX), lax.rem(x + NX - 1, NX)
    low4, low2 = lax.rem(z, 4), lax.rem(z, 2)
    across = dev(z, 1 - yh, c, x, 1 - yl)
    z7 = dev(7 - z, yh, c, x, yl)
    z3 = dev(z + 3 - 2 * low4, yh, c, x, yl)
    z1 = dev(z + 1 - 2 * low2, yh, c, x, yl)
    sibling = dev(z, yh, 1 - c, x, yl)
    opposite = dev(z, 1 - yh, c, x, yl)
    beside = dev(z, yh, c, x, 1 - yl)
    up, down = dev(z_up, yh, c, x, yl), dev(z_down, yh, c, x, yl)
    right, left = dev(z, yh, c, x_up, yl), dev(z, yh, c, x_down, yl)
    greet([across, z7, z3, z1, sibling, opposite, beside, up, down, right, left])

    sent = []

    def go(copy):
        copy.start()
        sent.append(copy)

    a_sems, b_sems, c_sems = (a_send, a_recv), (b_send, b_recv), (c_send, c_recv)

    def columns(index):
        return pl.ds(pl.multiple_of(index * share, 128), share)

    def slot_at(k):
        return pl.ds(k * slot_rows, slot_rows)

    for k in range(slots):
        go(remote(patches.at[slot_at(k), columns(x * 2 + 1 - yl)], got.at[0, k], a_sems, k, across))
    own = [
        pltpu.make_async_copy(patches.at[slot_at(k), columns(t)], hold.at[0, k], local_sem.at[k])
        for k in range(slots)
    ]
    own_w = [
        pltpu.make_async_copy(qkv_w, weights.at[f, :, pl.ds(0, qkv_cols)], local_sem.at[slots]),
        pltpu.make_async_copy(
            out_w, weights.at[f, :, pl.ds(qkv_cols, weights.shape[2] - qkv_cols)],
            local_sem.at[slots + 1],
        ),
    ]
    for copy in own_w + own:
        copy.start()
    for copy in own_w:
        copy.wait()

    def weight_copy(piece, slot, target):
        return remote(weights.at[piece], weights.at[piece], c_sems, slot, target)

    def fid(zz, kind):
        return zz * 4 + (yh if kind == 0 else 1 - yh) * 2 + c

    def sib_id(zz, kind):
        return zz * 4 + (yh if kind == 0 else 1 - yh) * 2 + 1 - c

    limits = {(0, 0): 4, (0, 1): 3, (1, 0): 3, (1, 1): 4}
    z_slot = {}
    for direction in range(2):
        for kind in range(2):
            for d in range(1, limits[direction, kind] + 1):
                z_slot[direction, kind, d] = 1 + len(z_slot)
    pieces = [(0, 0), (0, 1)]
    core_slot = {}

    def core_index(key):
        if key not in core_slot:
            core_slot[key] = 15 + len(core_slot)
        return core_slot[key]

    def z_at(distance):
        return lax.rem(z + distance + NZ, NZ)

    def share_core(distance, kind):
        go(weight_copy(fid(z_at(distance), kind), core_index((distance, kind)), sibling))

    def z_send(direction, kind, distance_travelled):
        source = z_at(-distance_travelled if direction == 0 else distance_travelled)
        go(
            weight_copy(
                fid(source, kind), z_slot[direction, kind, distance_travelled + 1],
                up if direction == 0 else down,
            )
        )

    def z_receive(direction, kind, d):
        signed = -d if direction == 0 else d
        weight_copy(fid(z_at(signed), kind), z_slot[direction, kind, d], up).wait_recv()
        if d < limits[direction, kind]:
            z_send(direction, kind, d)
        share_core(signed, kind)

    go(weight_copy(f, 0, opposite))
    share_core(0, 0)

    for copy in own:
        copy.wait()

    partner = {3: z3, 7: z7, 1: z1, 0: sibling}
    column = {7: 1, 3: 2, 1: 3, 0: 4}
    order = [[7, 3, 1, 0], [3, 7, 1, 0], [7, 3, 1, 0], [3, 7, 1, 0]]

    def merge(k, step, bit_column):
        remote(got.at[step, k], got.at[step, k], a_sems, step * slots + k, sibling).wait_recv()
        taken = bits_ref[k, bit_column] > 0
        return lax.select_n(taken, hold[step, k], got[step, k])

    for step in range(4):
        for k in range(slots):
            which = order[k][step]
            before = 0 if step == 0 else column[order[k][step - 1]]
            hold[step + 1, k] = merge(k, step, before)
            go(
                remote(
                    hold.at[step + 1, k], got.at[step + 1, k], a_sems,
                    (step + 1) * slots + k, partner[which],
                )
            )
        if step == 0:
            z_send(0, 0, 0)
            z_send(1, 0, 0)
            weight_copy(fid(z, 1), 0, opposite).wait_recv()
            z_send(0, 1, 0)
            z_send(1, 1, 0)
            share_core(0, 1)

    def row_copy(k, xx, y_low, which, target):
        view = rows.at[slot_at(k), columns(xx * 2 + y_low)]
        return remote(view, view, b_sems, k * 7 + which, target)

    for k in range(slots):
        merged = merge(k, 4, column[order[k][3]]).astype(jnp.float32)
        place = lax.broadcasted_iota(jnp.int32, (slot_rows, share), 0)
        live = place < live_ref[k]
        rows[slot_at(k), columns(t)] = jnp.where(live, merged, 0.0).astype(rows.dtype)
        go(row_copy(k, x, yl, 0, beside))
        go(row_copy(k, x, yl, 1, right))
        go(row_copy(k, x, yl, 4, left))

    def rows_second(k):
        row_copy(k, x, 1 - yl, 0, beside).wait_recv()
        go(row_copy(k, x, 1 - yl, 3, right))
        go(row_copy(k, x, 1 - yl, 5, left))

    def rows_third(k):
        row_copy(k, x_down, yl, 1, right).wait_recv()
        go(row_copy(k, x_down, yl, 2, right))
        row_copy(k, x_up, 1 - yl, 5, left).wait_recv()
        go(row_copy(k, x_up, 1 - yl, 6, left))

    for d in range(1, 5):
        for kind in range(2):
            for direction in range(2):
                if d <= limits[direction, kind]:
                    z_receive(direction, kind, d)
        if d == 1:
            for k in range(slots):
                rows_second(k)
                rows_third(k)
    for k in range(slots):
        row_copy(k, lax.rem(x + 2, NX), yl, 2, right).wait_recv()
        row_copy(k, x_down, 1 - yl, 3, right).wait_recv()
        row_copy(k, x_up, yl, 4, left).wait_recv()
        row_copy(k, lax.rem(x + 2, NX), 1 - yl, 6, left).wait_recv()
    for (distance, kind), slot in core_slot.items():
        weight_copy(sib_id(z_at(distance), kind), slot, sibling).wait_recv()
    for copy in sent:
        copy.wait_send()


def gather(bits, live, patches, qkv_w, out_w):
    tok, model = patches.shape
    slots = bits.shape[0]
    share = model // 8
    slot_rows = tok // slots
    bf16 = jnp.bfloat16
    depth, wide = qkv_w.shape[0], qkv_w.shape[1] + out_w.shape[1]
    hbm = pl.BlockSpec(memory_space=pl.ANY)
    smem = pl.BlockSpec(memory_space=pltpu.SMEM)
    return pl.pallas_call(
        gather_kernel,
        out_shape=(
            jax.ShapeDtypeStruct((tok, model), bf16),
            jax.ShapeDtypeStruct((32, depth, wide), bf16),
        ),
        in_specs=[smem, smem, hbm, hbm, hbm],
        out_specs=(pl.BlockSpec(memory_space=pltpu.VMEM), hbm),
        scratch_shapes=[
            pltpu.VMEM((5, slots, slot_rows, share), bf16),
            pltpu.VMEM((5, slots, slot_rows, share), bf16),
            pltpu.SemaphoreType.DMA((5 * slots,)),
            pltpu.SemaphoreType.DMA((5 * slots,)),
            pltpu.SemaphoreType.DMA((7 * slots,)),
            pltpu.SemaphoreType.DMA((7 * slots,)),
            pltpu.SemaphoreType.DMA((31,)),
            pltpu.SemaphoreType.DMA((31,)),
            pltpu.SemaphoreType.DMA((slots + 2,)),
        ],
        compiler_params=pltpu.CompilerParams(
            collective_id=0, has_side_effects=True, vmem_limit_bytes=24 * 2**20
        ),
        cost_estimate=pl.CostEstimate(flops=0, bytes_accessed=24 * 2**20, transcendentals=0),
    )(bits, live, patches, qkv_w, out_w)


def head_norm(values):
    centred = values - jnp.mean(values, axis=-1, keepdims=True)
    factor = lax.rsqrt(jnp.mean(centred * centred, axis=-1, keepdims=True) + epsilon)
    return centred * factor, factor


def head_norm_back(upstream, normed, factor):
    return factor * (
        upstream
        - jnp.mean(upstream, axis=-1, keepdims=True)
        - normed * jnp.mean(upstream * normed, axis=-1, keepdims=True)
    )


def dot_nn(a, b):
    return jnp.dot(a, b, preferred_element_type=jnp.float32)


def dot_nt(a, b):
    return lax.dot_general(a, b, (((1,), (1,)), ((), ())), preferred_element_type=jnp.float32)


def dot_tn(a, b):
    return lax.dot_general(a, b, (((0,), (0,)), ((), ())), preferred_element_type=jnp.float32)


def exact_dot(a, b, dims):
    return lax.dot_general(
        a, b, (dims, ((), ())),
        precision=lax.Precision.HIGHEST, preferred_element_type=jnp.float32,
    )


def add_into(total, other, rows_at=32):
    @pl.loop(0, total.shape[0] // rows_at)
    def _(i):
        at = pl.ds(pl.multiple_of(i * rows_at, rows_at), rows_at)
        total[at, :] = (
            total[at, :].astype(jnp.float32) + other[at, :].astype(jnp.float32)
        ).astype(total.dtype)


def branch_kernel(
    live_ref, gain, qk_gain, rows_in, weights_in, cotangent,
    attended, grad_rows, grad_qkv_w, grad_out_w,
    rows, weights, upstream, normed, row_mean, row_factor, projected, attention,
    mixed, grad_mixed, grad_qkv, terms, theirs, z_got, y_got, parts, x_got, l_got,
    partial_sums, sums, sums_got,
    core_send, core_recv, z_send_sem, z_recv_sem, y_send, y_recv,
    x_send, x_recv, l_send, l_recv, s_send, s_recv, local_sem,
):
    f32, bf16 = jnp.float32, jnp.bfloat16
    z, yh, c, x, yl = coords()
    me_t = x * 2 + yl
    tok, model = rows.shape
    share = attended.shape[1]
    heads = attention.shape[0]
    slots, slot_rows = attention.shape[1], attention.shape[2]
    head_dim = qk_gain.shape[1]
    qkv_cols, out_cols = grad_qkv_w.shape[1], grad_out_w.shape[1]
    depth = grad_qkv_w.shape[0]
    band = 4 * depth
    z_up, z_down = lax.rem(z + 1, NZ), lax.rem(z + NZ - 1, NZ)
    x_up, x_down = lax.rem(x + 1, NX), lax.rem(x + NX - 1, NX)
    sibling = dev(z, yh, 1 - c, x, yl)
    opposite = dev(z, 1 - yh, c, x, yl)
    beside = dev(z, yh, c, x, 1 - yl)
    up, down = dev(z_up, yh, c, x, yl), dev(z_down, yh, c, x, yl)
    right, left = dev(z, yh, c, x_up, yl), dev(z, yh, c, x_down, yl)
    my_f = z * 4 + yh * 2 + c
    peers = [(my_f, lax.rem(me_t + o, 8)) for o in range(1, 8)]

    loads = [
        pltpu.make_async_copy(rows_in, rows, local_sem.at[0]),
        pltpu.make_async_copy(weights_in, weights, local_sem.at[1]),
        pltpu.make_async_copy(cotangent, upstream, local_sem.at[2]),
    ]
    for copy in loads:
        copy.start()
    greet([sibling, opposite, up, down] + peers)
    sent = []

    def go(copy):
        copy.start()
        sent.append(copy)

    core_sems, z_sems = (core_send, core_recv), (z_send_sem, z_recv_sem)
    y_sems, x_sems, l_sems = (y_send, y_recv), (x_send, x_recv), (l_send, l_recv)
    s_sems = (s_send, s_recv)
    step_rows = 16
    per_slot = slot_rows // step_rows
    qkv_part, out_part = pl.ds(0, qkv_cols), pl.ds(qkv_cols, out_cols)

    def live_rows(i, shape):
        place = lax.broadcasted_iota(jnp.int32, shape, 0) + lax.rem(i, per_slot) * step_rows
        return place < live_ref[lax.div(i, per_slot)]

    loads[0].wait()

    @pl.loop(0, tok // step_rows)
    def _(i):
        at = pl.ds(pl.multiple_of(i * step_rows, step_rows), step_rows)
        values = rows[at, :].astype(f32)
        mean = jnp.mean(values, axis=-1, keepdims=True)
        centred = values - mean
        factor = lax.rsqrt(jnp.mean(centred * centred, axis=-1, keepdims=True) + epsilon)
        normed[at, :] = (centred * factor * gain[...]).astype(bf16)
        row_mean[at, :] = jnp.broadcast_to(mean, (step_rows, 128))
        row_factor[at, :] = jnp.broadcast_to(factor, (step_rows, 128))

    loads[1].wait()
    piece = model // 4

    @pl.loop(0, 4)
    def _(i):
        at = pl.ds(pl.multiple_of(i * piece, piece), piece)
        part = dot_nn(normed[:, at], weights[at, qkv_part])

        @pl.when(i == 0)
        def _():
            projected[...] = part

        @pl.when(i > 0)
        def _():
            projected[...] += part

    query_scale = qk_gain[0:1, :] * head_dim ** (-0.5)
    key_scale = qk_gain[1:2, :]

    def slot_at(s):
        return pl.ds(s * slot_rows, slot_rows)

    def head_at(h, which):
        return pl.ds(pl.multiple_of((h * 3 + which) * head_dim, head_dim), head_dim)

    def mixed_at(h):
        return pl.ds(pl.multiple_of(h * head_dim, head_dim), head_dim)

    def head_rows(h, s):
        query_hat, query_factor = head_norm(projected[slot_at(s), head_at(h, 0)])
        key_hat, key_factor = head_norm(projected[slot_at(s), head_at(h, 1)])
        values = projected[slot_at(s), head_at(h, 2)].astype(bf16)
        return (
            (query_hat, query_factor, (query_hat * query_scale).astype(bf16)),
            (key_hat, key_factor, (key_hat * key_scale).astype(bf16)),
            values,
        )

    @pl.loop(0, heads)
    def _(h):
        i = lax.broadcasted_iota(jnp.int32, (slot_rows, slot_rows), 0)
        j = lax.broadcasted_iota(jnp.int32, (slot_rows, slot_rows), 1)
        for s in range(slots):
            (_, _, query), (_, _, key_rows), values = head_rows(h, s)
            count = live_ref[s]
            allowed = (jnp.maximum(i, j) < count) | (i == j)
            raised = jnp.where(allowed, jnp.exp(dot_nt(query, key_rows)), 0.0)
            weight = raised / jnp.sum(raised, axis=-1, keepdims=True)
            attention[h, s] = weight
            mixed[slot_at(s), mixed_at(h)] = dot_nn(weight.astype(bf16), values).astype(bf16)

    x_limits = {(0, 0): 2, (0, 1): 1, (1, 0): 1, (1, 1): 2}
    x_slot = {}
    for p in range(2):
        for direction in range(2):
            for kind in range(2):
                for d in range(x_limits[direction, kind], 0, -1):
                    x_slot[p, direction, kind, d] = len(x_slot)

    def x_shard(direction, kind, d):
        xx = lax.rem(x + (d if direction == 0 else NX - d), NX)
        return xx * 2 + (yl if kind == 0 else 1 - yl)

    def x_go(p, direction, kind, d):
        slot = x_slot[p, direction, kind, d]
        go(
            remote(
                parts.at[p, x_shard(direction, kind, d)], x_got.at[slot], x_sems, slot,
                right if direction == 0 else left,
            )
        )

    def x_take(p, direction, kind, d):
        slot = x_slot[p, direction, kind, d]
        shard = x_shard(direction, kind, d - 1)
        remote(parts.at[p, shard], x_got.at[slot], x_sems, slot, right).wait_recv()
        add_into(parts.at[p, shard], x_got.at[slot])

    def x_first(p):
        for d in (2, 1):
            for kind in (1, 0):
                for direction in range(2):
                    if d == x_limits[direction, kind]:
                        x_go(p, direction, kind, d)

    def x_second(p):
        x_take(p, 1, 1, 2)
        x_go(p, 1, 1, 1)
        x_take(p, 0, 0, 2)
        x_go(p, 0, 0, 1)

    def x_third(p):
        x_take(p, 0, 1, 1)
        x_take(p, 1, 1, 1)
        go(remote(parts.at[p, x * 2 + 1 - yl], l_got.at[p], l_sems, p, beside))
        x_take(p, 1, 0, 1)
        x_take(p, 0, 0, 1)

    def l_take(p):
        remote(parts.at[p, me_t], l_got.at[p], l_sems, p, beside).wait_recv()

    def shard_rows(shard):
        return pl.ds(pl.multiple_of(shard * share, share), share)

    @pl.loop(0, 8)
    def _(shard):
        parts[0, shard] = dot_nt(mixed[...], weights[shard_rows(shard), out_part]).astype(bf16)

    x_first(0)

    loads[2].wait()

    @pl.loop(0, tok // step_rows)
    def _(i):
        at = pl.ds(pl.multiple_of(i * step_rows, step_rows), step_rows)
        values = upstream[at, :].astype(f32)
        upstream[at, :] = jnp.where(live_rows(i, values.shape), values, 0.0).astype(bf16)

    grad_mixed[...] = dot_nn(upstream[...], weights[:, out_part]).astype(bf16)

    @pl.loop(0, heads)
    def _(h):
        for s in range(slots):
            (query_hat, query_factor, query), (key_hat, key_factor, key_rows), values = head_rows(
                h, s
            )
            weight = attention[h, s]
            rounded = weight.astype(bf16)
            above = grad_mixed[slot_at(s), mixed_at(h)]
            grad_value = dot_tn(rounded, above)
            grad_weight = dot_nt(above, values)
            grad_scores = weight * (
                grad_weight - jnp.sum(weight * grad_weight, axis=-1, keepdims=True)
            )
            grad_scores = grad_scores.astype(bf16)
            grad_query = dot_nn(grad_scores, key_rows)
            grad_key = dot_tn(grad_scores, query)
            grad_qkv[slot_at(s), head_at(h, 0)] = head_norm_back(
                grad_query * query_scale, query_hat, query_factor
            ).astype(bf16)
            grad_qkv[slot_at(s), head_at(h, 1)] = head_norm_back(
                grad_key * key_scale, key_hat, key_factor
            ).astype(bf16)
            grad_qkv[slot_at(s), head_at(h, 2)] = grad_value.astype(bf16)

    def z_at(distance):
        return lax.rem(z + distance + NZ, NZ)

    distances = [4, 3, -3, 2, -2, 1, -1, 0]

    def compute(distance):
        zz = z_at(distance)
        at = pl.ds(pl.multiple_of(zz * band, band), band)
        left_term = dot_tn(normed[:, at], grad_qkv[...]).astype(bf16)
        for q in range(4):
            terms[zz, q // 2, q % 2, :, 0:qkv_cols] = left_term[q * depth : (q + 1) * depth]
        right_term = dot_tn(upstream[:, at], mixed[...]).astype(bf16)
        for q in range(4):
            terms[zz, q // 2, q % 2, :, qkv_cols:] = right_term[q * depth : (q + 1) * depth]
        go(
            remote(
                terms.at[zz, :, 1 - c], theirs.at[zz], core_sems, distances.index(distance), sibling
            )
        )

    def have(distance):
        zz = z_at(distance)
        remote(
            terms.at[zz, :, c], theirs.at[zz], core_sems, distances.index(distance), sibling
        ).wait_recv()
        for y in range(2):
            add_into(terms.at[zz, y, c], theirs.at[zz, y])

    def y_of(kind):
        return yh if kind == 0 else 1 - yh

    limits = {(0, 0): 4, (0, 1): 3, (1, 0): 3, (1, 1): 4}
    z_slot = {}
    for direction in range(2):
        for kind in range(2):
            for d in range(limits[direction, kind], 0, -1):
                z_slot[direction, kind, d] = len(z_slot)

    def z_go(direction, kind, d):
        zz = z_at(d if direction == 0 else -d)
        slot = z_slot[direction, kind, d]
        go(
            remote(
                terms.at[zz, y_of(kind), c], z_got.at[slot], z_sems, slot,
                up if direction == 0 else down,
            )
        )

    def z_take(direction, kind, d):
        zz = z_at(d - 1 if direction == 0 else 1 - d)
        slot = z_slot[direction, kind, d]
        remote(terms.at[zz, y_of(kind), c], z_got.at[slot], z_sems, slot, up).wait_recv()
        add_into(terms.at[zz, y_of(kind), c], z_got.at[slot])

    def z_pass(direction, kind, d):
        z_take(direction, kind, d)
        z_go(direction, kind, d - 1)

    compute(4)
    compute(3)
    have(4)
    z_go(1, 1, 4)
    z_go(0, 0, 4)
    compute(-3)
    have(3)
    z_go(0, 1, 3)
    compute(2)
    have(-3)
    z_go(1, 0, 3)
    x_second(0)

    partial_sums[...] = jnp.zeros(partial_sums.shape, f32)

    @pl.loop(0, 8)
    def _(shard):
        at = shard_rows(shard)
        part = dot_nt(grad_qkv[...], weights[at, qkv_part]).astype(bf16)
        parts[1, shard] = part
        scaled = part.astype(f32) * gain[:, at]
        for q in range(share // 128):
            lanes = slice(q * 128, (q + 1) * 128)
            own = pl.ds(pl.multiple_of(shard * share + q * 128, 128), 128)
            centred = (rows[:, own].astype(f32) - row_mean[...]) * row_factor[...]
            partial_sums[0] += scaled[:, lanes]
            partial_sums[1] += scaled[:, lanes] * centred

    x_first(1)
    ones = jnp.ones((8, 128), f32)
    upper = lax.broadcasted_iota(jnp.int32, (8, tok), 0) < 4
    sums[...] = jnp.where(
        upper,
        exact_dot(ones, partial_sums[0], ((1,), (1,))),
        exact_dot(ones, partial_sums[1], ((1,), (1,))),
    )
    for o, peer in enumerate(peers):
        go(remote(sums, sums_got.at[o], s_sems, o, peer))

    z_pass(1, 1, 4)
    z_pass(0, 0, 4)
    compute(-2)
    have(2)
    z_pass(0, 1, 3)
    compute(1)
    have(-2)
    z_pass(1, 0, 3)
    x_third(0)
    compute(-1)
    compute(0)
    have(1)
    z_pass(1, 1, 3)
    z_pass(0, 0, 3)
    have(-1)
    have(0)
    x_second(1)
    z_pass(0, 1, 2)
    z_pass(1, 0, 2)
    l_take(0)

    @pl.loop(0, tok // step_rows)
    def _(i):
        at = pl.ds(pl.multiple_of(i * step_rows, step_rows), step_rows)
        total = parts[0, me_t, at, :].astype(f32) + l_got[0, at, :].astype(f32)
        attended[at, :] = jnp.where(live_rows(i, total.shape), total, 0.0).astype(bf16)

    z_pass(1, 1, 2)
    z_pass(0, 0, 2)
    x_third(1)
    total_sums = sums[...]
    for o, peer in enumerate(peers):
        remote(sums, sums_got.at[o], s_sems, o, peer).wait_recv()
        total_sums += sums_got[o]
    pick = lax.broadcasted_iota(jnp.int32, (8, 128), 0)
    partial_sums[0] = exact_dot(
        total_sums, jnp.where(pick == 0, 1.0 / model, 0.0).astype(f32), ((0,), (0,))
    )
    partial_sums[1] = exact_dot(
        total_sums, jnp.where(pick == 4, 1.0 / model, 0.0).astype(f32), ((0,), (0,))
    )
    z_take(0, 1, 1)
    z_take(1, 1, 1)
    go(remote(terms.at[z, 1 - yh, c], y_got, y_sems, 0, opposite))
    l_take(1)

    @pl.loop(0, tok // step_rows)
    def _(i):
        at = pl.ds(pl.multiple_of(i * step_rows, step_rows), step_rows)
        for q in range(share // 128):
            lanes = slice(q * 128, (q + 1) * 128)
            own = pl.ds(pl.multiple_of(me_t * share + q * 128, 128), 128)
            total = parts[1, me_t, at, lanes].astype(f32) + l_got[1, at, lanes].astype(f32)
            centred = (rows[at, own].astype(f32) - row_mean[at, :]) * row_factor[at, :]
            grad_rows[at, lanes] = (
                row_factor[at, :]
                * (total * gain[:, own] - partial_sums[0, at, :] - centred * partial_sums[1, at, :])
            ).astype(bf16)

    z_take(1, 0, 1)
    z_take(0, 0, 1)
    remote(terms.at[z, yh, c], y_got, y_sems, 0, opposite).wait_recv()

    @pl.loop(0, depth // step_rows)
    def _(i):
        at = pl.ds(pl.multiple_of(i * step_rows, step_rows), step_rows)
        total = terms[z, yh, c, at, :].astype(f32) + y_got[at, :].astype(f32)
        grad_qkv_w[at, :] = total[:, :qkv_cols]
        grad_out_w[at, :] = total[:, qkv_cols:]

    for copy in sent:
        copy.wait_send()


def branch(live, gain, qk_gain, rows, weights, cotangent, qkv_cols):
    bf16, f32 = jnp.bfloat16, jnp.float32
    tok, model = rows.shape
    wide = weights.shape[1]
    out_cols = wide - qkv_cols
    depth = model // 32
    share = model // 8
    head_dim = qk_gain.shape[1]
    heads = out_cols // head_dim
    slots = live.shape[0]
    slot_rows = tok // slots
    hbm = pl.BlockSpec(memory_space=pl.ANY)
    vmem = pl.BlockSpec(memory_space=pltpu.VMEM)
    smem = pl.BlockSpec(memory_space=pltpu.SMEM)
    dma = pltpu.SemaphoreType.DMA
    sems = []
    for n in (8, 14, 1, 12, 2, 7):
        sems += [dma((n,)), dma((n,))]
    return pl.pallas_call(
        branch_kernel,
        out_shape=(
            jax.ShapeDtypeStruct((tok, share), bf16),
            jax.ShapeDtypeStruct((tok, share), bf16),
            jax.ShapeDtypeStruct((depth, qkv_cols), f32),
            jax.ShapeDtypeStruct((depth, out_cols), f32),
        ),
        in_specs=[smem, vmem, vmem, hbm, hbm, hbm],
        out_specs=(vmem,) * 4,
        scratch_shapes=[
            pltpu.VMEM((tok, model), bf16),
            pltpu.VMEM((model, wide), bf16),
            pltpu.VMEM((tok, model), bf16),
            pltpu.VMEM((tok, model), bf16),
            pltpu.VMEM((tok, 128), f32),
            pltpu.VMEM((tok, 128), f32),
            pltpu.VMEM((tok, qkv_cols), f32),
            pltpu.VMEM((heads, slots, slot_rows, slot_rows), f32),
            pltpu.VMEM((tok, out_cols), bf16),
            pltpu.VMEM((tok, out_cols), bf16),
            pltpu.VMEM((tok, qkv_cols), bf16),
            pltpu.VMEM((NZ, 2, 2, depth, wide), bf16),
            pltpu.VMEM((NZ, 2, depth, wide), bf16),
            pltpu.VMEM((14, depth, wide), bf16),
            pltpu.VMEM((depth, wide), bf16),
            pltpu.VMEM((2, 8, tok, share), bf16),
            pltpu.VMEM((12, tok, share), bf16),
            pltpu.VMEM((2, tok, share), bf16),
            pltpu.VMEM((2, tok, 128), f32),
            pltpu.VMEM((8, tok), f32),
            pltpu.VMEM((7, 8, tok), f32),
        ]
        + sems
        + [dma((3,))],
        compiler_params=pltpu.CompilerParams(
            collective_id=1, has_side_effects=True, vmem_limit_bytes=60 * 2**20
        ),
        cost_estimate=pl.CostEstimate(
            flops=13 * 10**9, bytes_accessed=16 * 2**20, transcendentals=150528
        ),
    )(live, gain, qk_gain, rows, weights, cotangent)


def per_device(patches, cotangent, counts, masks, norm_gain, qk_gain, qkv_weight, out_weight):
    replicas = lax.axis_size("fsdp")
    my_replica = lax.axis_index("fsdp")
    qkv_cols = qkv_weight.shape[1]
    bit = [jnp.bitwise_and(jnp.right_shift(masks, place), 1) for place in range(5)]
    bits = jnp.stack(
        [bit[1], bit[4], bit[3] ^ bit[4], bit[2] ^ bit[3], bit[0]], axis=1
    ).astype(jnp.int32)
    replica_ids = jnp.arange(replicas, dtype=jnp.int32)
    sources = jnp.bitwise_xor(my_replica, masks)
    run_counts = jnp.sum(jnp.where(replica_ids[:, None] == sources[None, :], counts, 0), axis=0)
    run_counts = run_counts.astype(jnp.int32)
    block_rows, weights = gather(bits, run_counts, patches, qkv_weight, out_weight)
    weights = weights.reshape(norm_gain.shape[0], qkv_cols + out_weight.shape[1])
    return branch(
        run_counts, norm_gain[None, :], qk_gain, block_rows, weights, cotangent, qkv_cols
    )


def solution(mesh):
    in_specs = (
        P("fsdp", None),
        P("fsdp", None),
        P(),
        P(),
        P(),
        P(),
        P("fsdp", "tp"),
        P("fsdp", "tp"),
    )
    out_specs = (P("fsdp", "tp"), P("fsdp", "tp"), P("fsdp", "tp"), P("fsdp", "tp"))
    return jax.shard_map(
        per_device, mesh=mesh, in_specs=in_specs, out_specs=out_specs, check_vma=False
    )
```

```python
import functools
import jax
import jax.numpy as jnp
from jax import lax
from jax.experimental import pallas as pl
from jax.experimental.pallas import tpu as pltpu
from jax.sharding import PartitionSpec as P

MESH = pl.DeviceIdType.MESH
epsilon = 1e-06
NZ, NX = 8, 4
W_ROWS, G_ROWS = 32, 48


def coords():
    f = lax.axis_index("fsdp")
    t = lax.axis_index("tp")
    z, yh, c = lax.div(f, 4), lax.rem(lax.div(f, 2), 2), lax.rem(f, 2)
    x, yl = lax.div(t, 2), lax.rem(t, 2)
    return z, yh, c, x, yl


def dev(z, yh, c, x, yl):
    return (z * 4 + yh * 2 + c, x * 2 + yl)


def remote(src, dst, sems, slot, target):
    send, recv = sems
    return pltpu.make_async_remote_copy(
        src_ref=src,
        dst_ref=dst,
        send_sem=send.at[slot],
        recv_sem=recv.at[slot],
        device_id=target,
        device_id_type=MESH,
    )


def greet(partners):
    barrier = pltpu.get_barrier_semaphore()
    for partner in partners:
        pl.semaphore_signal(barrier, inc=1, device_id=partner, device_id_type=MESH)
    pl.semaphore_wait(barrier, len(partners))


def head_norm(values):
    centred = values - jnp.mean(values, axis=-1, keepdims=True)
    factor = lax.rsqrt(jnp.mean(centred * centred, axis=-1, keepdims=True) + epsilon)
    return centred * factor, factor


def head_norm_back(upstream, normed, factor):
    return factor * (
        upstream
        - jnp.mean(upstream, axis=-1, keepdims=True)
        - normed * jnp.mean(upstream * normed, axis=-1, keepdims=True)
    )


def dot_nn(a, b):
    return jnp.dot(a, b, preferred_element_type=jnp.float32)


def dot_nt(a, b):
    return lax.dot_general(a, b, (((1,), (1,)), ((), ())), preferred_element_type=jnp.float32)


def dot_tn(a, b):
    return lax.dot_general(a, b, (((0,), (0,)), ((), ())), preferred_element_type=jnp.float32)


def exact_dot(a, b, dims):
    return lax.dot_general(
        a, b, (dims, ((), ())),
        precision=lax.Precision.HIGHEST, preferred_element_type=jnp.float32,
    )


def add_into(total, other, rows_at=32):
    @pl.loop(0, total.shape[0] // rows_at)
    def _(i):
        at = pl.ds(pl.multiple_of(i * rows_at, rows_at), rows_at)
        total[at, :] = (
            total[at, :].astype(jnp.float32) + other[at, :].astype(jnp.float32)
        ).astype(total.dtype)


def branch_kernel(
    bits_ref, live_ref, gain, qk_gain, patches, cotangent, qkv_w, out_w,
    attended, grad_rows, grad_qkv_w, grad_out_w,
    hold, got, rows, weights, upstream, normed, row_mean, row_factor, projected, attention,
    mixed, grad_mixed, grad_qkv, terms, theirs, y_part, z_got, y_got, parts, x_got, l_got,
    partial_sums, sums, sums_got,
    a_send, a_recv, b_send, b_recv, c_send, c_recv,
    core_send, core_recv, z_send_sem, z_recv_sem, y_send, y_recv,
    x_send, x_recv, l_send, l_recv, s_send, s_recv, local_sem,
):
    f32, bf16 = jnp.float32, jnp.bfloat16
    z, yh, c, x, yl = coords()
    me_t = x * 2 + yl
    tok, model = rows.shape
    share = attended.shape[1]
    heads = attention.shape[0]
    slots, slot_rows = attention.shape[1], attention.shape[2]
    head_dim = qk_gain.shape[1]
    qkv_cols, out_cols = grad_qkv_w.shape[1], grad_out_w.shape[1]
    depth = grad_qkv_w.shape[0]
    band = 4 * depth
    z_up, z_down = lax.rem(z + 1, NZ), lax.rem(z + NZ - 1, NZ)
    x_up, x_down = lax.rem(x + 1, NX), lax.rem(x + NX - 1, NX)
    sibling = dev(z, yh, 1 - c, x, yl)
    opposite = dev(z, 1 - yh, c, x, yl)
    beside = dev(z, yh, c, x, 1 - yl)
    up, down = dev(z_up, yh, c, x, yl), dev(z_down, yh, c, x, yl)
    right, left = dev(z, yh, c, x_up, yl), dev(z, yh, c, x_down, yl)
    across = dev(z, 1 - yh, c, x, 1 - yl)
    z7 = dev(7 - z, yh, c, x, yl)
    z3 = dev(z + 3 - 2 * lax.rem(z, 4), yh, c, x, yl)
    z1 = dev(z + 1 - 2 * lax.rem(z, 2), yh, c, x, yl)
    my_f = z * 4 + yh * 2 + c
    peers = [(my_f, lax.rem(me_t + o, 8)) for o in range(1, 8)]
    f32, bf16 = jnp.float32, jnp.bfloat16

    def slot_at(s):
        return pl.ds(s * slot_rows, slot_rows)

    def columns(index):
        return pl.ds(pl.multiple_of(index * share, 128), share)

    def weight_at(index, first, count):
        return weights.at[pl.ds(pl.multiple_of(index * depth + first, 16), count), :]

    own = [
        pltpu.make_async_copy(patches.at[slot_at(k), columns(me_t)], hold.at[0, k], local_sem.at[k])
        for k in range(slots)
    ]
    mine = pl.ds(pl.multiple_of(my_f * depth, 16), depth)
    own_w = [
        pltpu.make_async_copy(qkv_w, weights.at[mine, pl.ds(0, qkv_cols)], local_sem.at[slots]),
        pltpu.make_async_copy(
            out_w, weights.at[mine, pl.ds(qkv_cols, out_cols)], local_sem.at[slots + 1]
        ),
    ]
    load = pltpu.make_async_copy(cotangent, upstream, local_sem.at[slots + 2])
    for copy in own_w + own + [load]:
        copy.start()
    greet([across, z7, z3, z1, sibling, opposite, up, down] + peers)
    sent = []

    def go(copy):
        copy.start()
        sent.append(copy)

    a_sems, b_sems, c_sems = (a_send, a_recv), (b_send, b_recv), (c_send, c_recv)
    core_sems, z_sems = (core_send, core_recv), (z_send_sem, z_recv_sem)
    y_sems, x_sems, l_sems = (y_send, y_recv), (x_send, x_recv), (l_send, l_recv)
    s_sems = (s_send, s_recv)
    step_rows = 16
    per_slot = slot_rows // step_rows
    qkv_part, out_part = pl.ds(0, qkv_cols), pl.ds(qkv_cols, out_cols)
    limits = {(0, 0): 4, (0, 1): 3, (1, 0): 3, (1, 1): 4}

    def z_at(distance):
        return lax.rem(z + distance + NZ, NZ)

    def y_of(kind):
        return yh if kind == 0 else 1 - yh

    w_slot = {}

    def w_index(key):
        if key not in w_slot:
            w_slot[key] = len(w_slot)
        return w_slot[key]

    def w_copy(route, piece, target, core=0):
        distance, kind, first, count = piece
        owner = z_at(distance) * 4 + y_of(kind) * 2 + (1 - c if core else c)
        view = weight_at(owner, first, count)
        return remote(view, view, c_sems, w_index((route, piece)), target)

    def w_core(piece):
        go(w_copy("core", piece, sibling))

    def w_core_take(piece):
        w_copy("core", piece, sibling, 1).wait_recv()

    def w_rows(kind):
        return (0, depth) if kind == 0 else (0, W_ROWS)

    rest = (W_ROWS, depth - W_ROWS)

    def w_route(direction):
        return "up" if direction == 0 else "down"

    def w_send(direction, kind, travelled):
        signed = -travelled if direction == 0 else travelled
        first, count = w_rows(kind)
        owner = z_at(signed) * 4 + y_of(kind) * 2 + c
        view = weight_at(owner, first, count)
        there = -travelled - 1 if direction == 0 else travelled + 1
        slot = w_index((w_route(direction), (there, kind, first, count)))
        go(remote(view, view, c_sems, slot, up if direction == 0 else down))

    def w_take(direction, kind, d):
        signed = -d if direction == 0 else d
        piece = (signed, kind) + w_rows(kind)
        w_copy(w_route(direction), piece, up).wait_recv()
        if d < limits[direction, kind]:
            w_send(direction, kind, d)
        if kind == 0:
            owner = z_at(signed) * 4 + yh * 2 + c
            view = weight_at(owner, *rest)
            go(remote(view, view, c_sems, w_index(("y", (signed, 1) + rest)), opposite))
        w_core(piece)

    def w_round(d):
        for kind in range(2):
            for direction in range(2):
                if d <= limits[direction, kind]:
                    w_take(direction, kind, d)

    def w_across(signed):
        piece = (signed, 1) + rest
        w_copy("y", piece, opposite).wait_recv()
        w_core(piece)

    for k in range(slots):
        go(remote(patches.at[slot_at(k), columns(x * 2 + 1 - yl)], got.at[0, k], a_sems, k, across))
    for copy in own_w:
        copy.wait()
    whole = (0, depth)
    view = weight_at(my_f, *whole)
    go(remote(view, view, c_sems, w_index(("y", (0, 1) + whole)), opposite))
    w_core((0, 0) + whole)
    w_send(0, 0, 0)
    w_send(1, 0, 0)
    for copy in own:
        copy.wait()

    partner = {3: z3, 7: z7, 1: z1, 0: sibling}
    bit_column = {7: 1, 3: 2, 1: 3, 0: 4}
    order = [[7, 3, 1, 0], [3, 7, 1, 0], [7, 3, 1, 0], [3, 7, 1, 0]]

    def merge(k, step):
        remote(got.at[step, k], got.at[step, k], a_sems, step * slots + k, sibling).wait_recv()
        taken = bits_ref[k, 0 if step == 0 else bit_column[order[k][step - 1]]] > 0
        return lax.select_n(taken, hold[step, k], got[step, k])

    def row_step(step):
        for k in range(slots):
            hold[step + 1, k] = merge(k, step)
            go(
                remote(
                    hold.at[step + 1, k], got.at[step + 1, k], a_sems,
                    (step + 1) * slots + k, partner[order[k][step]],
                )
            )

    def row_copy(k, xx, y_low, which, target):
        view = rows.at[slot_at(k), columns(xx * 2 + y_low)]
        return remote(view, view, b_sems, k * 7 + which, target)

    def rows_first(k):
        merged = merge(k, 4).astype(f32)
        place = lax.broadcasted_iota(jnp.int32, (slot_rows, share), 0)
        live = place < live_ref[k]
        rows[slot_at(k), columns(me_t)] = jnp.where(live, merged, 0.0).astype(bf16)
        go(row_copy(k, x, yl, 0, beside))
        go(row_copy(k, x, yl, 1, right))
        go(row_copy(k, x, yl, 4, left))

    def rows_second(k):
        row_copy(k, x, 1 - yl, 0, beside).wait_recv()
        go(row_copy(k, x, 1 - yl, 3, right))
        go(row_copy(k, x, 1 - yl, 5, left))

    def rows_third(k):
        row_copy(k, x_down, yl, 1, right).wait_recv()
        go(row_copy(k, x_down, yl, 2, right))
        row_copy(k, x_up, 1 - yl, 5, left).wait_recv()
        go(row_copy(k, x_up, 1 - yl, 6, left))

    def rows_last(k):
        row_copy(k, lax.rem(x + 2, NX), yl, 2, right).wait_recv()
        row_copy(k, x_down, 1 - yl, 3, right).wait_recv()
        row_copy(k, x_up, yl, 4, left).wait_recv()
        row_copy(k, lax.rem(x + 2, NX), 1 - yl, 6, left).wait_recv()

    def norm_slot(k):
        @pl.loop(0, per_slot)
        def _(i):
            at = pl.ds(pl.multiple_of(k * slot_rows + i * step_rows, step_rows), step_rows)
            values = rows[at, :].astype(f32)
            mean = jnp.mean(values, axis=-1, keepdims=True)
            centred = values - mean
            factor = lax.rsqrt(jnp.mean(centred * centred, axis=-1, keepdims=True) + epsilon)
            normed[at, :] = (centred * factor * gain[...]).astype(bf16)
            row_mean[at, :] = jnp.broadcast_to(mean, (step_rows, 128))
            row_factor[at, :] = jnp.broadcast_to(factor, (step_rows, 128))

    def project(distance):
        if distance == 0:
            for kind in range(2):
                w_core_take((0, kind) + whole)
        else:
            for kind, part in ((0, whole), (1, (0, W_ROWS)), (1, rest)):
                signed = distance
                if abs(distance) == 4:
                    signed = 4 if (kind, part) == (1, (0, W_ROWS)) else -4
                w_core_take((signed, kind) + part)
        at = pl.ds(pl.multiple_of(z_at(distance) * band, band), band)
        part = dot_nn(normed[:, at], weights[at, qkv_part])
        if distance == 0:
            projected[...] = part
        else:
            projected[...] += part

    def live_rows(i, shape):
        place = lax.broadcasted_iota(jnp.int32, shape, 0) + lax.rem(i, per_slot) * step_rows
        return place < live_ref[lax.div(i, per_slot)]

    row_step(0)
    w_copy("y", (0, 1) + whole, opposite).wait_recv()
    w_send(0, 1, 0)
    w_send(1, 1, 0)
    w_core((0, 1) + whole)
    row_step(1)
    w_round(1)
    row_step(2)
    w_across(-1)
    w_across(1)
    row_step(3)
    w_round(2)
    for k in range(slots):
        rows_first(k)
    for k in range(slots):
        rows_second(k)
    w_across(-2)
    w_across(2)
    for k in range(slots):
        rows_third(k)
    w_round(3)
    load.wait()

    @pl.loop(0, tok // step_rows)
    def _(i):
        at = pl.ds(pl.multiple_of(i * step_rows, step_rows), step_rows)
        values = upstream[at, :].astype(f32)
        upstream[at, :] = jnp.where(live_rows(i, values.shape), values, 0.0).astype(bf16)

    for k in range(slots):
        rows_last(k)
        norm_slot(k)
    project(0)
    project(-1)
    project(1)
    w_across(-3)
    w_across(3)
    project(-2)
    project(2)
    w_round(4)
    project(-3)
    project(3)
    w_across(-4)
    project(4)

    query_scale = qk_gain[0:1, :] * head_dim ** (-0.5)
    key_scale = qk_gain[1:2, :]

    def head_at(h, which):
        return pl.ds(pl.multiple_of((h * 3 + which) * head_dim, head_dim), head_dim)

    def mixed_at(h):
        return pl.ds(pl.multiple_of(h * head_dim, head_dim), head_dim)

    def head_rows(h, s):
        query_hat, query_factor = head_norm(projected[slot_at(s), head_at(h, 0)])
        key_hat, key_factor = head_norm(projected[slot_at(s), head_at(h, 1)])
        values = projected[slot_at(s), head_at(h, 2)].astype(bf16)
        return (
            (query_hat, query_factor, (query_hat * query_scale).astype(bf16)),
            (key_hat, key_factor, (key_hat * key_scale).astype(bf16)),
            values,
        )

    @pl.loop(0, heads)
    def _(h):
        i = lax.broadcasted_iota(jnp.int32, (slot_rows, slot_rows), 0)
        j = lax.broadcasted_iota(jnp.int32, (slot_rows, slot_rows), 1)
        for s in range(slots):
            (_, _, query), (_, _, key_rows), values = head_rows(h, s)
            count = live_ref[s]
            allowed = (jnp.maximum(i, j) < count) | (i == j)
            raised = jnp.where(allowed, jnp.exp(dot_nt(query, key_rows)), 0.0)
            weight = raised / jnp.sum(raised, axis=-1, keepdims=True)
            attention[h, s] = weight
            mixed[slot_at(s), mixed_at(h)] = dot_nn(weight.astype(bf16), values).astype(bf16)

    x_limits = {(0, 0): 2, (0, 1): 1, (1, 0): 1, (1, 1): 2}
    x_slot = {}
    for p in range(2):
        for direction in range(2):
            for kind in range(2):
                for d in range(x_limits[direction, kind], 0, -1):
                    x_slot[p, direction, kind, d] = len(x_slot)

    def x_shard(direction, kind, d):
        xx = lax.rem(x + (d if direction == 0 else NX - d), NX)
        return xx * 2 + (yl if kind == 0 else 1 - yl)

    def x_go(p, direction, kind, d):
        slot = x_slot[p, direction, kind, d]
        go(
            remote(
                parts.at[p, x_shard(direction, kind, d)], x_got.at[slot], x_sems, slot,
                right if direction == 0 else left,
            )
        )

    def x_take(p, direction, kind, d):
        slot = x_slot[p, direction, kind, d]
        shard = x_shard(direction, kind, d - 1)
        remote(parts.at[p, shard], x_got.at[slot], x_sems, slot, right).wait_recv()
        add_into(parts.at[p, shard], x_got.at[slot])

    def x_first(p):
        for d in (2, 1):
            for kind in (1, 0):
                for direction in range(2):
                    if d == x_limits[direction, kind]:
                        x_go(p, direction, kind, d)

    def x_second(p):
        x_take(p, 1, 1, 2)
        x_go(p, 1, 1, 1)
        x_take(p, 0, 0, 2)
        x_go(p, 0, 0, 1)

    def x_third(p):
        x_take(p, 0, 1, 1)
        x_take(p, 1, 1, 1)
        go(remote(parts.at[p, x * 2 + 1 - yl], l_got.at[p], l_sems, p, beside))
        x_take(p, 1, 0, 1)
        x_take(p, 0, 0, 1)

    def l_take(p):
        remote(parts.at[p, me_t], l_got.at[p], l_sems, p, beside).wait_recv()

    def shard_rows(shard):
        return pl.ds(pl.multiple_of(shard * share, share), share)

    @pl.loop(0, 8)
    def _(shard):
        parts[0, shard] = dot_nt(mixed[...], weights[shard_rows(shard), out_part]).astype(bf16)

    x_first(0)

    grad_mixed[...] = dot_nn(upstream[...], weights[:, out_part]).astype(bf16)

    @pl.loop(0, heads)
    def _(h):
        for s in range(slots):
            (query_hat, query_factor, query), (key_hat, key_factor, key_rows), values = head_rows(
                h, s
            )
            weight = attention[h, s]
            rounded = weight.astype(bf16)
            above = grad_mixed[slot_at(s), mixed_at(h)]
            grad_value = dot_tn(rounded, above)
            grad_weight = dot_nt(above, values)
            grad_scores = weight * (
                grad_weight - jnp.sum(weight * grad_weight, axis=-1, keepdims=True)
            )
            grad_scores = grad_scores.astype(bf16)
            grad_query = dot_nn(grad_scores, key_rows)
            grad_key = dot_tn(grad_scores, query)
            grad_qkv[slot_at(s), head_at(h, 0)] = head_norm_back(
                grad_query * query_scale, query_hat, query_factor
            ).astype(bf16)
            grad_qkv[slot_at(s), head_at(h, 1)] = head_norm_back(
                grad_key * key_scale, key_hat, key_factor
            ).astype(bf16)
            grad_qkv[slot_at(s), head_at(h, 2)] = grad_value.astype(bf16)

    distances = [4, 3, -3, 2, -2, 1, -1, 0]
    kept = pl.ds(0, G_ROWS)
    crossing = pl.ds(G_ROWS, depth - G_ROWS)

    def compute(distance):
        zz = z_at(distance)
        at = pl.ds(pl.multiple_of(zz * band, band), band)
        left_term = dot_tn(normed[:, at], grad_qkv[...]).astype(bf16)
        for q in range(4):
            terms[zz, q // 2, q % 2, :, 0:qkv_cols] = left_term[q * depth : (q + 1) * depth]
        right_term = dot_tn(upstream[:, at], mixed[...]).astype(bf16)
        for q in range(4):
            terms[zz, q // 2, q % 2, :, qkv_cols:] = right_term[q * depth : (q + 1) * depth]
        go(
            remote(
                terms.at[zz, :, 1 - c], theirs.at[zz], core_sems, distances.index(distance), sibling
            )
        )

    def have(distance):
        i = distances.index(distance)
        zz = z_at(distance)
        remote(terms.at[zz, :, c], theirs.at[zz], core_sems, i, sibling).wait_recv()
        add_into(terms.at[zz, 1 - yh, c], theirs.at[zz, 1 - yh])
        target = y_got.at[crossing] if distance == 0 else y_part.at[i]
        go(remote(terms.at[zz, 1 - yh, c, crossing], target, y_sems, i, opposite))
        add_into(terms.at[zz, yh, c], theirs.at[zz, yh])

    def y_take(distance):
        i = distances.index(distance)
        zz = z_at(distance)
        remote(terms.at[zz, yh, c, crossing], y_part.at[i], y_sems, i, opposite).wait_recv()
        add_into(terms.at[zz, yh, c, crossing], y_part.at[i], 16)

    z_slot = {}
    for direction in range(2):
        for kind in range(2):
            for d in range(limits[direction, kind], 0, -1):
                z_slot[direction, kind, d] = len(z_slot)

    def z_views(kind, zz, slot):
        if kind == 0:
            return terms.at[zz, yh, c], z_got.at[slot]
        return terms.at[zz, 1 - yh, c, kept], z_got.at[slot, kept]

    def z_go(direction, kind, d):
        zz = z_at(d if direction == 0 else -d)
        slot = z_slot[direction, kind, d]
        here, there = z_views(kind, zz, slot)
        go(remote(here, there, z_sems, slot, up if direction == 0 else down))

    def z_take(direction, kind, d):
        zz = z_at(d - 1 if direction == 0 else 1 - d)
        slot = z_slot[direction, kind, d]
        here, arrived = z_views(kind, zz, slot)
        remote(here, arrived, z_sems, slot, up).wait_recv()
        add_into(here, arrived, 16)

    def z_pass(direction, kind, d):
        z_take(direction, kind, d)
        z_go(direction, kind, d - 1)

    compute(4)
    compute(3)
    have(4)
    z_go(1, 1, 4)
    compute(-3)
    have(3)
    z_go(0, 1, 3)
    y_take(4)
    z_go(0, 0, 4)
    compute(2)
    have(-3)
    compute(-2)
    y_take(-3)
    z_go(1, 0, 3)
    x_second(0)

    partial_sums[...] = jnp.zeros(partial_sums.shape, f32)

    @pl.loop(0, 8)
    def _(shard):
        at = shard_rows(shard)
        part = dot_nt(grad_qkv[...], weights[at, qkv_part]).astype(bf16)
        parts[1, shard] = part
        scaled = part.astype(f32) * gain[:, at]
        for q in range(share // 128):
            lanes = slice(q * 128, (q + 1) * 128)
            own = pl.ds(pl.multiple_of(shard * share + q * 128, 128), 128)
            centred = (rows[:, own].astype(f32) - row_mean[...]) * row_factor[...]
            partial_sums[0] += scaled[:, lanes]
            partial_sums[1] += scaled[:, lanes] * centred

    x_first(1)
    ones = jnp.ones((8, 128), f32)
    upper = lax.broadcasted_iota(jnp.int32, (8, tok), 0) < 4
    sums[...] = jnp.where(
        upper,
        exact_dot(ones, partial_sums[0], ((1,), (1,))),
        exact_dot(ones, partial_sums[1], ((1,), (1,))),
    )
    for o, peer in enumerate(peers):
        go(remote(sums, sums_got.at[o], s_sems, o, peer))

    have(2)
    have(-2)
    z_pass(1, 1, 4)
    y_take(3)
    z_pass(0, 0, 4)
    z_pass(0, 1, 3)
    y_take(-2)
    z_pass(1, 0, 3)
    compute(1)
    compute(-1)
    have(1)
    have(-1)
    x_third(0)
    z_pass(1, 1, 3)
    y_take(2)
    z_pass(0, 0, 3)
    compute(0)
    z_pass(0, 1, 2)
    y_take(-1)
    z_pass(1, 0, 2)
    have(0)
    x_second(1)
    z_pass(1, 1, 2)
    y_take(1)
    z_pass(0, 0, 2)
    l_take(0)

    @pl.loop(0, tok // step_rows)
    def _(i):
        at = pl.ds(pl.multiple_of(i * step_rows, step_rows), step_rows)
        total = parts[0, me_t, at, :].astype(f32) + l_got[0, at, :].astype(f32)
        attended[at, :] = jnp.where(live_rows(i, total.shape), total, 0.0).astype(bf16)

    x_third(1)
    total_sums = sums[...]
    for o, peer in enumerate(peers):
        remote(sums, sums_got.at[o], s_sems, o, peer).wait_recv()
        total_sums += sums_got[o]
    pick = lax.broadcasted_iota(jnp.int32, (8, 128), 0)
    partial_sums[0] = exact_dot(
        total_sums, jnp.where(pick == 0, 1.0 / model, 0.0).astype(f32), ((0,), (0,))
    )
    partial_sums[1] = exact_dot(
        total_sums, jnp.where(pick == 4, 1.0 / model, 0.0).astype(f32), ((0,), (0,))
    )
    z_take(0, 1, 1)
    z_take(1, 1, 1)
    go(remote(terms.at[z, 1 - yh, c, kept], y_got.at[kept], y_sems, 8, opposite))
    l_take(1)

    @pl.loop(0, tok // step_rows)
    def _(i):
        at = pl.ds(pl.multiple_of(i * step_rows, step_rows), step_rows)
        for q in range(share // 128):
            lanes = slice(q * 128, (q + 1) * 128)
            own = pl.ds(pl.multiple_of(me_t * share + q * 128, 128), 128)
            total = parts[1, me_t, at, lanes].astype(f32) + l_got[1, at, lanes].astype(f32)
            centred = (rows[at, own].astype(f32) - row_mean[at, :]) * row_factor[at, :]
            grad_rows[at, lanes] = (
                row_factor[at, :]
                * (total * gain[:, own] - partial_sums[0, at, :] - centred * partial_sums[1, at, :])
            ).astype(bf16)

    z_take(1, 0, 1)
    z_take(0, 0, 1)
    remote(terms.at[z, yh, c, crossing], y_got.at[crossing], y_sems, 7, opposite).wait_recv()
    remote(terms.at[z, yh, c, kept], y_got.at[kept], y_sems, 8, opposite).wait_recv()

    @pl.loop(0, depth // step_rows)
    def _(i):
        at = pl.ds(pl.multiple_of(i * step_rows, step_rows), step_rows)
        total = terms[z, yh, c, at, :].astype(f32) + y_got[at, :].astype(f32)
        grad_qkv_w[at, :] = total[:, :qkv_cols]
        grad_out_w[at, :] = total[:, qkv_cols:]

    for copy in sent:
        copy.wait_send()


def branch(bits, live, gain, qk_gain, patches, cotangent, qkv_weight, out_weight):
    bf16, f32 = jnp.bfloat16, jnp.float32
    tok, model = patches.shape
    qkv_cols, out_cols = qkv_weight.shape[1], out_weight.shape[1]
    wide = qkv_cols + out_cols
    depth = model // 32
    share = model // 8
    head_dim = qk_gain.shape[1]
    heads = out_cols // head_dim
    slots = live.shape[0]
    slot_rows = tok // slots
    hbm = pl.BlockSpec(memory_space=pl.ANY)
    vmem = pl.BlockSpec(memory_space=pltpu.VMEM)
    smem = pl.BlockSpec(memory_space=pltpu.SMEM)
    dma = pltpu.SemaphoreType.DMA
    sems = []
    for n in (5 * slots, 7 * slots, 45, 8, 14, 9, 12, 2, 7):
        sems += [dma((n,)), dma((n,))]
    return pl.pallas_call(
        branch_kernel,
        out_shape=(
            jax.ShapeDtypeStruct((tok, share), bf16),
            jax.ShapeDtypeStruct((tok, share), bf16),
            jax.ShapeDtypeStruct((depth, qkv_cols), f32),
            jax.ShapeDtypeStruct((depth, out_cols), f32),
        ),
        in_specs=[smem, smem, vmem, vmem, hbm, hbm, hbm, hbm],
        out_specs=(vmem,) * 4,
        scratch_shapes=[
            pltpu.VMEM((5, slots, slot_rows, share), bf16),
            pltpu.VMEM((5, slots, slot_rows, share), bf16),
            pltpu.VMEM((tok, model), bf16),
            pltpu.VMEM((model, wide), bf16),
            pltpu.VMEM((tok, model), bf16),
            pltpu.VMEM((tok, model), bf16),
            pltpu.VMEM((tok, 128), f32),
            pltpu.VMEM((tok, 128), f32),
            pltpu.VMEM((tok, qkv_cols), f32),
            pltpu.VMEM((heads, slots, slot_rows, slot_rows), f32),
            pltpu.VMEM((tok, out_cols), bf16),
            pltpu.VMEM((tok, out_cols), bf16),
            pltpu.VMEM((tok, qkv_cols), bf16),
            pltpu.VMEM((NZ, 2, 2, depth, wide), bf16),
            pltpu.VMEM((NZ, 2, depth, wide), bf16),
            pltpu.VMEM((7, depth - G_ROWS, wide), bf16),
            pltpu.VMEM((14, depth, wide), bf16),
            pltpu.VMEM((depth, wide), bf16),
            pltpu.VMEM((2, 8, tok, share), bf16),
            pltpu.VMEM((12, tok, share), bf16),
            pltpu.VMEM((2, tok, share), bf16),
            pltpu.VMEM((2, tok, 128), f32),
            pltpu.VMEM((8, tok), f32),
            pltpu.VMEM((7, 8, tok), f32),
        ]
        + sems
        + [dma((slots + 3,))],
        compiler_params=pltpu.CompilerParams(
            collective_id=0, has_side_effects=True, vmem_limit_bytes=60 * 2**20
        ),
        cost_estimate=pl.CostEstimate(
            flops=13 * 10**9, bytes_accessed=16 * 2**20, transcendentals=150528
        ),
    )(bits, live, gain, qk_gain, patches, cotangent, qkv_weight, out_weight)


def per_device(patches, cotangent, counts, masks, norm_gain, qk_gain, qkv_weight, out_weight):
    replicas = lax.axis_size("fsdp")
    my_replica = lax.axis_index("fsdp")
    bit = [jnp.bitwise_and(jnp.right_shift(masks, place), 1) for place in range(5)]
    bits = jnp.stack(
        [bit[1], bit[4], bit[3] ^ bit[4], bit[2] ^ bit[3], bit[0]], axis=1
    ).astype(jnp.int32)
    replica_ids = jnp.arange(replicas, dtype=jnp.int32)
    sources = jnp.bitwise_xor(my_replica, masks)
    run_counts = jnp.sum(jnp.where(replica_ids[:, None] == sources[None, :], counts, 0), axis=0)
    run_counts = run_counts.astype(jnp.int32)
    return branch(
        bits, run_counts, norm_gain[None, :], qk_gain, patches, cotangent, qkv_weight, out_weight
    )


def solution(mesh):
    in_specs = (
        P("fsdp", None),
        P("fsdp", None),
        P(),
        P(),
        P(),
        P(),
        P("fsdp", "tp"),
        P("fsdp", "tp"),
    )
    out_specs = (P("fsdp", "tp"), P("fsdp", "tp"), P("fsdp", "tp"), P("fsdp", "tp"))
    return jax.shard_map(
        per_device, mesh=mesh, in_specs=in_specs, out_specs=out_specs, check_vma=False
    )
```

```python
import functools
import jax
import jax.numpy as jnp
from jax import lax
from jax.experimental import pallas as pl
from jax.experimental.pallas import tpu as pltpu
from jax.sharding import PartitionSpec as P

MESH = pl.DeviceIdType.MESH
epsilon = 1e-06
NZ, NX = 8, 4
SETTLE_PIECES = 2
W_ROWS, G_ROWS = 48, 48


def coords():
    f = lax.axis_index("fsdp")
    t = lax.axis_index("tp")
    z, yh, c = lax.div(f, 4), lax.rem(lax.div(f, 2), 2), lax.rem(f, 2)
    x, yl = lax.div(t, 2), lax.rem(t, 2)
    return z, yh, c, x, yl


def dev(z, yh, c, x, yl):
    return (z * 4 + yh * 2 + c, x * 2 + yl)


def remote(src, dst, sems, slot, target):
    send, recv = sems
    return pltpu.make_async_remote_copy(
        src_ref=src,
        dst_ref=dst,
        send_sem=send.at[slot],
        recv_sem=recv.at[slot],
        device_id=target,
        device_id_type=MESH,
    )


def greet(partners):
    barrier = pltpu.get_barrier_semaphore()
    for partner in partners:
        pl.semaphore_signal(barrier, inc=1, device_id=partner, device_id_type=MESH)
    pl.semaphore_wait(barrier, len(partners))


def head_norm(values):
    centred = values - jnp.mean(values, axis=-1, keepdims=True)
    factor = lax.rsqrt(jnp.mean(centred * centred, axis=-1, keepdims=True) + epsilon)
    return centred * factor, factor


def head_norm_back(upstream, normed, factor):
    return factor * (
        upstream
        - jnp.mean(upstream, axis=-1, keepdims=True)
        - normed * jnp.mean(upstream * normed, axis=-1, keepdims=True)
    )


def dot_nn(a, b):
    return jnp.dot(a, b, preferred_element_type=jnp.float32)


def dot_nt(a, b):
    return lax.dot_general(a, b, (((1,), (1,)), ((), ())), preferred_element_type=jnp.float32)


def dot_tn(a, b):
    return lax.dot_general(a, b, (((0,), (0,)), ((), ())), preferred_element_type=jnp.float32)


def exact_dot(a, b, dims):
    return lax.dot_general(
        a, b, (dims, ((), ())),
        precision=lax.Precision.HIGHEST, preferred_element_type=jnp.float32,
    )


def add_into(total, other, rows_at=32):
    @pl.loop(0, total.shape[0] // rows_at)
    def _(i):
        at = pl.ds(pl.multiple_of(i * rows_at, rows_at), rows_at)
        total[at, :] = (
            total[at, :].astype(jnp.float32) + other[at, :].astype(jnp.float32)
        ).astype(total.dtype)


def branch_kernel(
    masks_ref, counts_ref, gain, qk_gain, patches, cotangent, qkv_w, out_w,
    attended, grad_rows, grad_qkv_w, grad_out_w,
    hold, got, rows, weights, upstream, normed, row_mean, row_factor, projected, attention,
    mixed, grad_mixed, grad_qkv, terms, theirs, y_part, z_got, y_got, parts, x_got, l_got,
    partial_sums, sums, sums_got,
    a_send, a_recv, b_send, b_recv, c_send, c_recv,
    core_send, core_recv, z_send_sem, z_recv_sem, y_send, y_recv,
    x_send, x_recv, l_send, l_recv, s_send, s_recv, local_sem,
):
    f32, bf16 = jnp.float32, jnp.bfloat16
    z, yh, c, x, yl = coords()
    me_t = x * 2 + yl
    tok, model = rows.shape
    share = attended.shape[1]
    heads = attention.shape[0]
    slots, slot_rows = attention.shape[1], attention.shape[2]
    head_dim = qk_gain.shape[1]
    qkv_cols, out_cols = grad_qkv_w.shape[1], grad_out_w.shape[1]
    depth = grad_qkv_w.shape[0]
    band = 4 * depth
    z_up, z_down = lax.rem(z + 1, NZ), lax.rem(z + NZ - 1, NZ)
    x_up, x_down = lax.rem(x + 1, NX), lax.rem(x + NX - 1, NX)
    sibling = dev(z, yh, 1 - c, x, yl)
    opposite = dev(z, 1 - yh, c, x, yl)
    beside = dev(z, yh, c, x, 1 - yl)
    up, down = dev(z_up, yh, c, x, yl), dev(z_down, yh, c, x, yl)
    right, left = dev(z, yh, c, x_up, yl), dev(z, yh, c, x_down, yl)
    across = dev(z, 1 - yh, c, x, 1 - yl)
    z7 = dev(7 - z, yh, c, x, yl)
    z3 = dev(z + 3 - 2 * lax.rem(z, 4), yh, c, x, yl)
    z1 = dev(z + 1 - 2 * lax.rem(z, 2), yh, c, x, yl)
    my_f = z * 4 + yh * 2 + c
    peers = [(my_f, lax.rem(me_t + o, 8)) for o in range(1, 8)]
    f32, bf16 = jnp.float32, jnp.bfloat16

    def live_count(k):
        return counts_ref[k, jnp.bitwise_xor(my_f, masks_ref[k])]

    def mask_bit(k, place):
        return jnp.bitwise_and(lax.shift_right_logical(masks_ref[k], place), 1)

    def takes(k, step):
        which = -1 if step == 0 else order[k][step - 1]
        if which in (-1, 7, 0):
            return mask_bit(k, {-1: 1, 7: 4, 0: 0}[which]) > 0
        places = (3, 4) if which == 3 else (2, 3)
        return mask_bit(k, places[0]) != mask_bit(k, places[1])

    def slot_at(s):
        return pl.ds(s * slot_rows, slot_rows)

    def columns(index):
        return pl.ds(pl.multiple_of(index * share, 128), share)

    def weight_at(index, first, count):
        return weights.at[pl.ds(pl.multiple_of(index * depth + first, 16), count), :]

    own = [
        pltpu.make_async_copy(patches.at[slot_at(k), columns(me_t)], hold.at[0, k], local_sem.at[k])
        for k in range(slots)
    ]
    mine = pl.ds(pl.multiple_of(my_f * depth, 16), depth)
    own_w = [
        pltpu.make_async_copy(qkv_w, weights.at[mine, pl.ds(0, qkv_cols)], local_sem.at[slots]),
        pltpu.make_async_copy(
            out_w, weights.at[mine, pl.ds(qkv_cols, out_cols)], local_sem.at[slots + 1]
        ),
    ]
    load = pltpu.make_async_copy(cotangent, upstream, local_sem.at[slots + 2])
    for copy in own_w + own + [load]:
        copy.start()
    greet([across, z7, z3, z1, sibling, opposite, up, down] + peers)
    sent = []

    def go(copy):
        copy.start()
        sent.append(copy)

    a_sems, b_sems, c_sems = (a_send, a_recv), (b_send, b_recv), (c_send, c_recv)
    core_sems, z_sems = (core_send, core_recv), (z_send_sem, z_recv_sem)
    y_sems, x_sems, l_sems = (y_send, y_recv), (x_send, x_recv), (l_send, l_recv)
    s_sems = (s_send, s_recv)
    step_rows = 16
    per_slot = slot_rows // step_rows
    qkv_part, out_part = pl.ds(0, qkv_cols), pl.ds(qkv_cols, out_cols)
    limits = {(0, 0): 4, (0, 1): 3, (1, 0): 3, (1, 1): 4}

    def z_at(distance):
        return lax.rem(z + distance + NZ, NZ)

    def y_of(kind):
        return yh if kind == 0 else 1 - yh

    w_slot = {}

    def w_index(key):
        if key not in w_slot:
            w_slot[key] = len(w_slot)
        return w_slot[key]

    def w_copy(route, piece, target, core=0):
        distance, kind, first, count = piece
        owner = z_at(distance) * 4 + y_of(kind) * 2 + (1 - c if core else c)
        view = weight_at(owner, first, count)
        return remote(view, view, c_sems, w_index((route, piece)), target)

    def w_core(piece):
        go(w_copy("core", piece, sibling))

    def w_core_take(piece):
        w_copy("core", piece, sibling, 1).wait_recv()

    def w_rows(kind):
        return (0, depth) if kind == 0 else (0, W_ROWS)

    rest = (W_ROWS, depth - W_ROWS)

    def w_route(direction):
        return "up" if direction == 0 else "down"

    def w_send(direction, kind, travelled):
        signed = -travelled if direction == 0 else travelled
        first, count = w_rows(kind)
        owner = z_at(signed) * 4 + y_of(kind) * 2 + c
        view = weight_at(owner, first, count)
        there = -travelled - 1 if direction == 0 else travelled + 1
        slot = w_index((w_route(direction), (there, kind, first, count)))
        go(remote(view, view, c_sems, slot, up if direction == 0 else down))

    def w_take(kind, d):
        for direction in range(2):
            if d <= limits[direction, kind]:
                signed = -d if direction == 0 else d
                piece = (signed, kind) + w_rows(kind)
                w_copy(w_route(direction), piece, up).wait_recv()
                if kind == 0:
                    owner = z_at(signed) * 4 + yh * 2 + c
                    view = weight_at(owner, *rest)
                    go(remote(view, view, c_sems, w_index(("y", (signed, 1) + rest)), opposite))
                w_core(piece)

    def w_pass(kind, d):
        for direction in range(2):
            if d < limits[direction, kind]:
                w_send(direction, kind, d)

    def w_across(signed):
        piece = (signed, 1) + rest
        w_copy("y", piece, opposite).wait_recv()
        w_core(piece)

    for k in range(slots):
        go(remote(patches.at[slot_at(k), columns(x * 2 + 1 - yl)], got.at[0, k], a_sems, k, across))
    for copy in own_w:
        copy.wait()
    whole = (0, depth)
    w_pass(0, 0)
    for copy in own:
        copy.wait()

    partner = {3: z3, 7: z7, 1: z1, 0: sibling}
    order = [[7, 3, 1, 0], [3, 7, 1, 0], [7, 3, 1, 0], [3, 7, 1, 0]]

    def merge(k, step):
        remote(got.at[step, k], got.at[step, k], a_sems, step * slots + k, sibling).wait_recv()
        taken = takes(k, step)
        return lax.select_n(taken, hold[step, k], got[step, k])

    def row_step(step, which_slots=(0, 1, 2, 3)):
        for k in which_slots:
            hold[step + 1, k] = merge(k, step)
            go(
                remote(
                    hold.at[step + 1, k], got.at[step + 1, k], a_sems,
                    (step + 1) * slots + k, partner[order[k][step]],
                )
            )

    def row_copy(k, xx, y_low, which, target):
        view = rows.at[slot_at(k), columns(xx * 2 + y_low)]
        return remote(view, view, b_sems, k * 7 + which, target)

    def rows_first(k):
        merged = merge(k, 4).astype(f32)
        place = lax.broadcasted_iota(jnp.int32, (slot_rows, share), 0)
        live = place < live_count(k)
        rows[slot_at(k), columns(me_t)] = jnp.where(live, merged, 0.0).astype(bf16)
        go(row_copy(k, x, yl, 0, beside))
        go(row_copy(k, x, yl, 1, right))
        go(row_copy(k, x, yl, 4, left))

    def rows_second(k):
        row_copy(k, x, 1 - yl, 0, beside).wait_recv()
        go(row_copy(k, x, 1 - yl, 3, right))
        go(row_copy(k, x, 1 - yl, 5, left))

    def rows_third(k):
        row_copy(k, x_down, yl, 1, right).wait_recv()
        go(row_copy(k, x_down, yl, 2, right))
        row_copy(k, x_up, 1 - yl, 5, left).wait_recv()
        go(row_copy(k, x_up, 1 - yl, 6, left))

    def rows_last(k):
        row_copy(k, lax.rem(x + 2, NX), yl, 2, right).wait_recv()
        row_copy(k, x_down, 1 - yl, 3, right).wait_recv()
        row_copy(k, x_up, yl, 4, left).wait_recv()
        row_copy(k, lax.rem(x + 2, NX), 1 - yl, 6, left).wait_recv()

    def norm_slot(k):
        @pl.loop(0, per_slot)
        def _(i):
            at = pl.ds(pl.multiple_of(k * slot_rows + i * step_rows, step_rows), step_rows)
            values = rows[at, :].astype(f32)
            mean = jnp.mean(values, axis=-1, keepdims=True)
            centred = values - mean
            factor = lax.rsqrt(jnp.mean(centred * centred, axis=-1, keepdims=True) + epsilon)
            normed[at, :] = (centred * factor * gain[...]).astype(bf16)
            row_mean[at, :] = jnp.broadcast_to(mean, (step_rows, 128))
            row_factor[at, :] = jnp.broadcast_to(factor, (step_rows, 128))

    def project(distance):
        if distance == 0:
            for kind in range(2):
                w_core_take((0, kind) + whole)
        else:
            for kind, part in ((0, whole), (1, (0, W_ROWS)), (1, rest)):
                signed = distance
                if abs(distance) == 4:
                    signed = 4 if (kind, part) == (1, (0, W_ROWS)) else -4
                w_core_take((signed, kind) + part)
        at = pl.ds(pl.multiple_of(z_at(distance) * band, band), band)
        part = dot_nn(normed[:, at], weights[at, qkv_part])
        if distance == 0:
            projected[...] = part
        else:
            projected[...] += part

    def live_rows(i, shape):
        place = lax.broadcasted_iota(jnp.int32, shape, 0) + lax.rem(i, per_slot) * step_rows
        return place < live_count(lax.div(i, per_slot))

    row_step(0, (0, 1, 2, 3))
    view = weight_at(my_f, *whole)
    go(remote(view, view, c_sems, w_index(("y", (0, 1) + whole)), opposite))
    w_core((0, 0) + whole)
    w_take(0, 1)
    row_step(1, (0, 1, 2, 3))
    w_copy("y", (0, 1) + whole, opposite).wait_recv()
    w_core((0, 1) + whole)
    row_step(2, (0, 1, 2, 3))
    w_pass(0, 1)
    w_pass(1, 0)
    w_across(-1)
    w_across(1)
    row_step(3, (0, 1, 2, 3))
    rows_first(0)
    rows_first(1)
    rows_first(2)
    rows_first(3)
    w_take(0, 2)
    w_pass(0, 2)
    rows_second(0)
    rows_second(1)
    rows_second(2)
    rows_second(3)
    w_take(1, 1)
    w_pass(1, 1)
    rows_third(0)
    rows_third(1)
    rows_third(2)
    rows_third(3)
    w_across(-2)
    w_across(2)
    w_take(0, 3)
    w_pass(0, 3)
    w_take(1, 2)
    w_pass(1, 2)
    rows_last(0)
    norm_slot(0)
    rows_last(1)
    norm_slot(1)
    w_across(-3)
    w_across(3)
    rows_last(2)
    norm_slot(2)
    rows_last(3)
    norm_slot(3)
    w_take(0, 4)
    w_take(1, 3)
    w_pass(1, 3)
    project(0)
    project(-1)
    project(1)
    load.wait()

    @pl.loop(0, tok // step_rows)
    def _(i):
        at = pl.ds(pl.multiple_of(i * step_rows, step_rows), step_rows)
        values = upstream[at, :].astype(f32)
        upstream[at, :] = jnp.where(live_rows(i, values.shape), values, 0.0).astype(bf16)
    project(-2)
    project(2)
    w_take(1, 4)
    w_across(-4)
    project(-3)
    project(3)
    project(4)

    query_scale = qk_gain[0:1, :] * head_dim ** (-0.5)
    key_scale = qk_gain[1:2, :]

    def head_at(h, which):
        return pl.ds(pl.multiple_of((h * 3 + which) * head_dim, head_dim), head_dim)

    def mixed_at(h):
        return pl.ds(pl.multiple_of(h * head_dim, head_dim), head_dim)

    def head_rows(h, s):
        query_hat, query_factor = head_norm(projected[slot_at(s), head_at(h, 0)])
        key_hat, key_factor = head_norm(projected[slot_at(s), head_at(h, 1)])
        values = projected[slot_at(s), head_at(h, 2)].astype(bf16)
        return (
            (query_hat, query_factor, (query_hat * query_scale).astype(bf16)),
            (key_hat, key_factor, (key_hat * key_scale).astype(bf16)),
            values,
        )

    @pl.loop(0, heads)
    def _(h):
        i = lax.broadcasted_iota(jnp.int32, (slot_rows, slot_rows), 0)
        j = lax.broadcasted_iota(jnp.int32, (slot_rows, slot_rows), 1)
        for s in range(slots):
            (_, _, query), (_, _, key_rows), values = head_rows(h, s)
            count = live_count(s)
            allowed = (jnp.maximum(i, j) < count) | (i == j)
            raised = jnp.where(allowed, jnp.exp(dot_nt(query, key_rows)), 0.0)
            weight = raised / jnp.sum(raised, axis=-1, keepdims=True)
            attention[h, s] = weight
            mixed[slot_at(s), mixed_at(h)] = dot_nn(weight.astype(bf16), values).astype(bf16)

    x_limits = {(0, 0): 2, (0, 1): 1, (1, 0): 1, (1, 1): 2}
    x_slot = {}
    for p in range(2):
        for direction in range(2):
            for kind in range(2):
                for d in range(x_limits[direction, kind], 0, -1):
                    x_slot[p, direction, kind, d] = len(x_slot)

    def x_shard(direction, kind, d):
        xx = lax.rem(x + (d if direction == 0 else NX - d), NX)
        return xx * 2 + (yl if kind == 0 else 1 - yl)

    def x_go(p, direction, kind, d):
        slot = x_slot[p, direction, kind, d]
        go(
            remote(
                parts.at[p, x_shard(direction, kind, d)], x_got.at[slot], x_sems, slot,
                right if direction == 0 else left,
            )
        )

    def x_take(p, direction, kind, d):
        slot = x_slot[p, direction, kind, d]
        shard = x_shard(direction, kind, d - 1)
        remote(parts.at[p, shard], x_got.at[slot], x_sems, slot, right).wait_recv()
        add_into(parts.at[p, shard], x_got.at[slot])

    def x_first(p):
        x_go(p, 0, 0, 2)
        x_go(p, 1, 1, 2)

    def x_second(p):
        x_take(p, 1, 1, 2)
        x_go(p, 1, 1, 1)
        x_go(p, 0, 1, 1)
        x_take(p, 0, 0, 2)

    def x_third(p):
        x_take(p, 0, 1, 1)
        x_take(p, 1, 1, 1)
        go(remote(parts.at[p, x * 2 + 1 - yl], l_got.at[p], l_sems, p, beside))
        x_go(p, 0, 0, 1)
        x_go(p, 1, 0, 1)

    def x_last(p):
        x_take(p, 1, 0, 1)
        x_take(p, 0, 0, 1)

    def l_take(p):
        remote(parts.at[p, me_t], l_got.at[p], l_sems, p, beside).wait_recv()

    def shard_rows(shard):
        return pl.ds(pl.multiple_of(shard * share, share), share)

    @pl.loop(0, 8)
    def _(shard):
        parts[0, shard] = dot_nt(mixed[...], weights[shard_rows(shard), out_part]).astype(bf16)

    x_first(0)

    grad_mixed[...] = dot_nn(upstream[...], weights[:, out_part]).astype(bf16)

    @pl.loop(0, heads)
    def _(h):
        for s in range(slots):
            (query_hat, query_factor, query), (key_hat, key_factor, key_rows), values = head_rows(
                h, s
            )
            weight = attention[h, s]
            rounded = weight.astype(bf16)
            above = grad_mixed[slot_at(s), mixed_at(h)]
            grad_value = dot_tn(rounded, above)
            grad_weight = dot_nt(above, values)
            grad_scores = weight * (
                grad_weight - jnp.sum(weight * grad_weight, axis=-1, keepdims=True)
            )
            grad_scores = grad_scores.astype(bf16)
            grad_query = dot_nn(grad_scores, key_rows)
            grad_key = dot_tn(grad_scores, query)
            grad_qkv[slot_at(s), head_at(h, 0)] = head_norm_back(
                grad_query * query_scale, query_hat, query_factor
            ).astype(bf16)
            grad_qkv[slot_at(s), head_at(h, 1)] = head_norm_back(
                grad_key * key_scale, key_hat, key_factor
            ).astype(bf16)
            grad_qkv[slot_at(s), head_at(h, 2)] = grad_value.astype(bf16)

    distances = [4, 3, -3, 2, -2, 1, -1, 0]
    kept = pl.ds(0, G_ROWS)
    crossing = pl.ds(G_ROWS, depth - G_ROWS)

    def compute(distance):
        zz = z_at(distance)
        at = pl.ds(pl.multiple_of(zz * band, band), band)
        left_term = dot_tn(normed[:, at], grad_qkv[...]).astype(bf16)
        for q in range(4):
            terms[zz, q // 2, q % 2, :, 0:qkv_cols] = left_term[q * depth : (q + 1) * depth]
        right_term = dot_tn(upstream[:, at], mixed[...]).astype(bf16)
        for q in range(4):
            terms[zz, q // 2, q % 2, :, qkv_cols:] = right_term[q * depth : (q + 1) * depth]
        go(
            remote(
                terms.at[zz, :, 1 - c], theirs.at[zz], core_sems, distances.index(distance), sibling
            )
        )

    def have(distance):
        zz = z_at(distance)
        remote(
            terms.at[zz, :, c], theirs.at[zz], core_sems, distances.index(distance), sibling
        ).wait_recv()
        for y in range(2):
            add_into(terms.at[zz, y, c], theirs.at[zz, y])

    def y_go(distance):
        i = distances.index(distance)
        zz = z_at(distance)
        target = y_got.at[crossing] if distance == 0 else y_part.at[i]
        go(remote(terms.at[zz, 1 - yh, c, crossing], target, y_sems, i, opposite))

    def y_take(distance):
        i = distances.index(distance)
        zz = z_at(distance)
        remote(terms.at[zz, yh, c, crossing], y_part.at[i], y_sems, i, opposite).wait_recv()
        add_into(terms.at[zz, yh, c, crossing], y_part.at[i], 16)

    z_slot = {}
    for direction in range(2):
        for kind in range(2):
            for d in range(limits[direction, kind], 0, -1):
                z_slot[direction, kind, d] = len(z_slot)

    def z_views(kind, zz, slot):
        if kind == 0:
            return terms.at[zz, yh, c], z_got.at[slot]
        return terms.at[zz, 1 - yh, c, kept], z_got.at[slot, kept]

    def z_go(direction, kind, d):
        zz = z_at(d if direction == 0 else -d)
        slot = z_slot[direction, kind, d]
        here, there = z_views(kind, zz, slot)
        go(remote(here, there, z_sems, slot, up if direction == 0 else down))

    def z_take(direction, kind, d):
        zz = z_at(d - 1 if direction == 0 else 1 - d)
        slot = z_slot[direction, kind, d]
        here, arrived = z_views(kind, zz, slot)
        remote(here, arrived, z_sems, slot, up).wait_recv()
        add_into(here, arrived, 16)

    def z_pass(direction, kind, d):
        z_take(direction, kind, d)
        z_go(direction, kind, d - 1)

    compute(4)
    compute(-3)
    have(4)
    y_go(4)
    z_go(1, 1, 4)
    have(-3)
    y_go(-3)
    compute(3)
    have(3)
    z_go(0, 1, 3)
    x_second(0)
    compute(2)
    have(2)
    compute(-2)
    have(-2)
    y_take(4)
    z_go(0, 0, 4)
    y_go(3)
    y_take(-3)
    z_go(1, 0, 3)
    y_go(-2)
    partial_sums[...] = jnp.zeros(partial_sums.shape, f32)

    @pl.loop(0, 8)
    def _(shard):
        at = shard_rows(shard)
        part = dot_nt(grad_qkv[...], weights[at, qkv_part]).astype(bf16)
        parts[1, shard] = part
        scaled = part.astype(f32) * gain[:, at]
        for q in range(share // 128):
            lanes = slice(q * 128, (q + 1) * 128)
            own = pl.ds(pl.multiple_of(shard * share + q * 128, 128), 128)
            centred = (rows[:, own].astype(f32) - row_mean[...]) * row_factor[...]
            partial_sums[0] += scaled[:, lanes]
            partial_sums[1] += scaled[:, lanes] * centred
    x_first(1)
    ones = jnp.ones((8, 128), f32)
    upper = lax.broadcasted_iota(jnp.int32, (8, tok), 0) < 4
    sums[...] = jnp.where(
        upper,
        exact_dot(ones, partial_sums[0], ((1,), (1,))),
        exact_dot(ones, partial_sums[1], ((1,), (1,))),
    )
    for o, peer in enumerate(peers):
        go(remote(sums, sums_got.at[o], s_sems, o, peer))
    z_pass(1, 1, 4)
    z_pass(0, 1, 3)
    x_third(0)
    compute(1)
    have(1)
    compute(-1)
    have(-1)
    y_take(3)
    z_pass(0, 0, 4)
    y_go(2)
    y_take(-2)
    z_pass(1, 0, 3)
    y_go(-1)
    compute(0)
    have(0)
    x_second(1)
    z_pass(1, 1, 3)
    z_pass(0, 1, 2)
    y_take(2)
    z_pass(0, 0, 3)
    y_go(1)
    y_take(-1)
    z_pass(1, 0, 2)
    y_go(0)
    x_last(0)
    l_take(0)

    @pl.loop(0, tok // step_rows)
    def _(i):
        at = pl.ds(pl.multiple_of(i * step_rows, step_rows), step_rows)
        total = parts[0, me_t, at, :].astype(f32) + l_got[0, at, :].astype(f32)
        attended[at, :] = jnp.where(live_rows(i, total.shape), total, 0.0).astype(bf16)
    z_pass(1, 1, 2)
    y_take(1)
    z_pass(0, 0, 2)
    x_third(1)
    z_take(0, 1, 1)
    z_take(1, 1, 1)
    go(remote(terms.at[z, 1 - yh, c, kept], y_got.at[kept], y_sems, 8, opposite))
    total_sums = sums[...]
    for o, peer in enumerate(peers):
        remote(sums, sums_got.at[o], s_sems, o, peer).wait_recv()
        total_sums += sums_got[o]
    pick = lax.broadcasted_iota(jnp.int32, (8, 128), 0)
    partial_sums[0] = exact_dot(
        total_sums, jnp.where(pick == 0, 1.0 / model, 0.0).astype(f32), ((0,), (0,))
    )
    partial_sums[1] = exact_dot(
        total_sums, jnp.where(pick == 4, 1.0 / model, 0.0).astype(f32), ((0,), (0,))
    )
    x_last(1)
    l_take(1)

    @pl.loop(0, tok // step_rows)
    def _(i):
        at = pl.ds(pl.multiple_of(i * step_rows, step_rows), step_rows)
        for q in range(share // 128):
            lanes = slice(q * 128, (q + 1) * 128)
            own = pl.ds(pl.multiple_of(me_t * share + q * 128, 128), 128)
            total = parts[1, me_t, at, lanes].astype(f32) + l_got[1, at, lanes].astype(f32)
            centred = (rows[at, own].astype(f32) - row_mean[at, :]) * row_factor[at, :]
            grad_rows[at, lanes] = (
                row_factor[at, :]
                * (total * gain[:, own] - partial_sums[0, at, :] - centred * partial_sums[1, at, :])
            ).astype(bf16)
    z_take(1, 0, 1)
    z_take(0, 0, 1)
    remote(terms.at[z, yh, c, crossing], y_got.at[crossing], y_sems, 7, opposite).wait_recv()
    remote(terms.at[z, yh, c, kept], y_got.at[kept], y_sems, 8, opposite).wait_recv()

    @pl.loop(0, depth // step_rows)
    def _(i):
        at = pl.ds(pl.multiple_of(i * step_rows, step_rows), step_rows)
        total = terms[z, yh, c, at, :].astype(f32) + y_got[at, :].astype(f32)
        grad_qkv_w[at, :] = total[:, :qkv_cols]
        grad_out_w[at, :] = total[:, qkv_cols:]

    for copy in sent:
        copy.wait_send()


def branch(masks, counts, gain, qk_gain, patches, cotangent, qkv_weight, out_weight):
    bf16, f32 = jnp.bfloat16, jnp.float32
    tok, model = patches.shape
    qkv_cols, out_cols = qkv_weight.shape[1], out_weight.shape[1]
    wide = qkv_cols + out_cols
    depth = model // 32
    share = model // 8
    head_dim = qk_gain.shape[1]
    heads = out_cols // head_dim
    slots = masks.shape[0]
    slot_rows = tok // slots
    hbm = pl.BlockSpec(memory_space=pl.ANY)
    vmem = pl.BlockSpec(memory_space=pltpu.VMEM)
    smem = pl.BlockSpec(memory_space=pltpu.SMEM)
    dma = pltpu.SemaphoreType.DMA
    sems = []
    for n in (5 * slots, 7 * slots, 45, 8, 14, 9, 12, 2, 7):
        sems += [dma((n,)), dma((n,))]
    return pl.pallas_call(
        branch_kernel,
        out_shape=(
            jax.ShapeDtypeStruct((tok, share), bf16),
            jax.ShapeDtypeStruct((tok, share), bf16),
            jax.ShapeDtypeStruct((depth, qkv_cols), f32),
            jax.ShapeDtypeStruct((depth, out_cols), f32),
        ),
        in_specs=[smem, smem, vmem, vmem, hbm, hbm, hbm, hbm],
        out_specs=(vmem,) * 4,
        scratch_shapes=[
            pltpu.VMEM((5, slots, slot_rows, share), bf16),
            pltpu.VMEM((5, slots, slot_rows, share), bf16),
            pltpu.VMEM((tok, model), bf16),
            pltpu.VMEM((model, wide), bf16),
            pltpu.VMEM((tok, model), bf16),
            pltpu.VMEM((tok, model), bf16),
            pltpu.VMEM((tok, 128), f32),
            pltpu.VMEM((tok, 128), f32),
            pltpu.VMEM((tok, qkv_cols), f32),
            pltpu.VMEM((heads, slots, slot_rows, slot_rows), f32),
            pltpu.VMEM((tok, out_cols), bf16),
            pltpu.VMEM((tok, out_cols), bf16),
            pltpu.VMEM((tok, qkv_cols), bf16),
            pltpu.VMEM((NZ, 2, 2, depth, wide), bf16),
            pltpu.VMEM((NZ, 2, depth, wide), bf16),
            pltpu.VMEM((7, depth - G_ROWS, wide), bf16),
            pltpu.VMEM((14, depth, wide), bf16),
            pltpu.VMEM((depth, wide), bf16),
            pltpu.VMEM((2, 8, tok, share), bf16),
            pltpu.VMEM((12, tok, share), bf16),
            pltpu.VMEM((2, tok, share), bf16),
            pltpu.VMEM((2, tok, 128), f32),
            pltpu.VMEM((8, tok), f32),
            pltpu.VMEM((7, 8, tok), f32),
        ]
        + sems
        + [dma((slots + 3,))],
        compiler_params=pltpu.CompilerParams(
            collective_id=0, has_side_effects=True, vmem_limit_bytes=60 * 2**20
        ),
        cost_estimate=pl.CostEstimate(
            flops=13 * 10**9, bytes_accessed=16 * 2**20, transcendentals=150528
        ),
    )(masks, counts, gain, qk_gain, patches, cotangent, qkv_weight, out_weight)


def settle_kernel(*refs):
    sem = refs[-1]
    half = len(refs) // 2
    copies = []
    for source, target in zip(refs[:half], refs[half:-1]):
        part = source.shape[0] // SETTLE_PIECES
        for i in range(SETTLE_PIECES):
            at = pl.ds(i * part, part)
            copies.append(
                pltpu.make_async_copy(source.at[at], target.at[at], sem.at[len(copies)])
            )
    for copy in copies:
        copy.start()
    for copy in copies:
        copy.wait()


def settle(arrays):
    hbm = pl.BlockSpec(memory_space=pltpu.HBM)
    return pl.pallas_call(
        settle_kernel,
        out_shape=tuple(jax.ShapeDtypeStruct(a.shape, a.dtype) for a in arrays),
        in_specs=[hbm] * len(arrays),
        out_specs=(hbm,) * len(arrays),
        scratch_shapes=[pltpu.SemaphoreType.DMA((SETTLE_PIECES * len(arrays),))],
        compiler_params=pltpu.CompilerParams(vmem_limit_bytes=60 * 2**20),
    )(*arrays)


def per_device(patches, cotangent, counts, masks, norm_gain, qk_gain, qkv_weight, out_weight):
    return settle(
        branch(
            masks, counts.T, norm_gain[None, :], qk_gain, patches, cotangent, qkv_weight, out_weight
        )
    )


def solution(mesh):
    in_specs = (
        P("fsdp", None),
        P("fsdp", None),
        P(),
        P(),
        P(),
        P(),
        P("fsdp", "tp"),
        P("fsdp", "tp"),
    )
    out_specs = (P("fsdp", "tp"), P("fsdp", "tp"), P("fsdp", "tp"), P("fsdp", "tp"))
    return jax.shard_map(
        per_device, mesh=mesh, in_specs=in_specs, out_specs=out_specs, check_vma=False
    )
```

```python
import functools
import jax
import jax.numpy as jnp
from jax import lax
from jax.experimental import pallas as pl
from jax.experimental.pallas import tpu as pltpu
from jax.sharding import PartitionSpec as P

MESH = pl.DeviceIdType.MESH
epsilon = 1e-06
NZ, NX = 8, 4
W_ROWS, G_ROWS = 48, 48


def coords():
    f = lax.axis_index("fsdp")
    t = lax.axis_index("tp")
    z, yh, c = lax.div(f, 4), lax.rem(lax.div(f, 2), 2), lax.rem(f, 2)
    x, yl = lax.div(t, 2), lax.rem(t, 2)
    return z, yh, c, x, yl


def dev(z, yh, c, x, yl):
    return (z * 4 + yh * 2 + c, x * 2 + yl)


def remote(src, dst, sems, slot, target):
    send, recv = sems
    return pltpu.make_async_remote_copy(
        src_ref=src,
        dst_ref=dst,
        send_sem=send.at[slot],
        recv_sem=recv.at[slot],
        device_id=target,
        device_id_type=MESH,
    )


def greet(partners):
    barrier = pltpu.get_barrier_semaphore()
    for partner in partners:
        pl.semaphore_signal(barrier, inc=1, device_id=partner, device_id_type=MESH)
    pl.semaphore_wait(barrier, len(partners))


def head_norm(values):
    centred = values - jnp.mean(values, axis=-1, keepdims=True)
    factor = lax.rsqrt(jnp.mean(centred * centred, axis=-1, keepdims=True) + epsilon)
    return centred * factor, factor


def head_norm_back(upstream, normed, factor):
    return factor * (
        upstream
        - jnp.mean(upstream, axis=-1, keepdims=True)
        - normed * jnp.mean(upstream * normed, axis=-1, keepdims=True)
    )


def dot_nn(a, b):
    return jnp.dot(a, b, preferred_element_type=jnp.float32)


def dot_nt(a, b):
    return lax.dot_general(a, b, (((1,), (1,)), ((), ())), preferred_element_type=jnp.float32)


def dot_tn(a, b):
    return lax.dot_general(a, b, (((0,), (0,)), ((), ())), preferred_element_type=jnp.float32)


def exact_dot(a, b, dims):
    return lax.dot_general(
        a, b, (dims, ((), ())),
        precision=lax.Precision.HIGHEST, preferred_element_type=jnp.float32,
    )


def add_into(total, other, rows_at=32):
    @pl.loop(0, total.shape[0] // rows_at)
    def _(i):
        at = pl.ds(pl.multiple_of(i * rows_at, rows_at), rows_at)
        total[at, :] = (
            total[at, :].astype(jnp.float32) + other[at, :].astype(jnp.float32)
        ).astype(total.dtype)


def branch_kernel(
    masks_ref, counts_ref, gain, qk_gain, patches, cotangent, qkv_w, out_w,
    attended, grad_rows, grad_qkv_w, grad_out_w,
    hold, got, rows, weights, upstream, normed, row_mean, row_factor, projected, attention,
    mixed, grad_mixed, grad_qkv, terms, theirs, y_part, z_got, y_got, parts, x_got, l_got,
    partial_sums, sums, sums_got,
    a_send, a_recv, b_send, b_recv, c_send, c_recv,
    core_send, core_recv, z_send_sem, z_recv_sem, y_send, y_recv,
    x_send, x_recv, l_send, l_recv, s_send, s_recv, local_sem,
):
    f32, bf16 = jnp.float32, jnp.bfloat16
    z, yh, c, x, yl = coords()
    me_t = x * 2 + yl
    tok, model = rows.shape
    share = attended.shape[1]
    heads = attention.shape[0]
    slots, slot_rows = attention.shape[1], attention.shape[2]
    head_dim = qk_gain.shape[1]
    qkv_cols, out_cols = grad_qkv_w.shape[1], grad_out_w.shape[1]
    depth = grad_qkv_w.shape[0]
    band = 4 * depth
    z_up, z_down = lax.rem(z + 1, NZ), lax.rem(z + NZ - 1, NZ)
    x_up, x_down = lax.rem(x + 1, NX), lax.rem(x + NX - 1, NX)
    sibling = dev(z, yh, 1 - c, x, yl)
    opposite = dev(z, 1 - yh, c, x, yl)
    beside = dev(z, yh, c, x, 1 - yl)
    up, down = dev(z_up, yh, c, x, yl), dev(z_down, yh, c, x, yl)
    right, left = dev(z, yh, c, x_up, yl), dev(z, yh, c, x_down, yl)
    across = dev(z, 1 - yh, c, x, 1 - yl)
    z7 = dev(7 - z, yh, c, x, yl)
    z3 = dev(z + 3 - 2 * lax.rem(z, 4), yh, c, x, yl)
    z1 = dev(z + 1 - 2 * lax.rem(z, 2), yh, c, x, yl)
    my_f = z * 4 + yh * 2 + c
    peers = [(my_f, lax.rem(me_t + o, 8)) for o in range(1, 8)]
    f32, bf16 = jnp.float32, jnp.bfloat16

    def live_count(k):
        return counts_ref[k, jnp.bitwise_xor(my_f, masks_ref[k])]

    def mask_bit(k, place):
        return jnp.bitwise_and(lax.shift_right_logical(masks_ref[k], place), 1)

    def takes(k, step):
        which = -1 if step == 0 else order[k][step - 1]
        if which in (-1, 7, 0):
            return mask_bit(k, {-1: 1, 7: 4, 0: 0}[which]) > 0
        places = (3, 4) if which == 3 else (2, 3)
        return mask_bit(k, places[0]) != mask_bit(k, places[1])

    def slot_at(s):
        return pl.ds(s * slot_rows, slot_rows)

    def columns(index):
        return pl.ds(pl.multiple_of(index * share, 128), share)

    def weight_at(index, first, count):
        return weights.at[pl.ds(pl.multiple_of(index * depth + first, 16), count), :]

    own = [
        pltpu.make_async_copy(patches.at[slot_at(k), columns(me_t)], hold.at[0, k], local_sem.at[k])
        for k in range(slots)
    ]
    mine = pl.ds(pl.multiple_of(my_f * depth, 16), depth)
    own_w = [
        pltpu.make_async_copy(qkv_w, weights.at[mine, pl.ds(0, qkv_cols)], local_sem.at[slots]),
        pltpu.make_async_copy(
            out_w, weights.at[mine, pl.ds(qkv_cols, out_cols)], local_sem.at[slots + 1]
        ),
    ]
    load = pltpu.make_async_copy(cotangent, upstream, local_sem.at[slots + 2])
    for copy in own_w + own + [load]:
        copy.start()
    greet([across, z7, z3, z1, sibling, opposite, up, down] + peers)
    sent = []

    def go(copy):
        copy.start()
        sent.append(copy)

    a_sems, b_sems, c_sems = (a_send, a_recv), (b_send, b_recv), (c_send, c_recv)
    core_sems, z_sems = (core_send, core_recv), (z_send_sem, z_recv_sem)
    y_sems, x_sems, l_sems = (y_send, y_recv), (x_send, x_recv), (l_send, l_recv)
    s_sems = (s_send, s_recv)
    step_rows = 16
    per_slot = slot_rows // step_rows
    qkv_part, out_part = pl.ds(0, qkv_cols), pl.ds(qkv_cols, out_cols)
    limits = {(0, 0): 4, (0, 1): 3, (1, 0): 3, (1, 1): 4}

    def z_at(distance):
        return lax.rem(z + distance + NZ, NZ)

    def y_of(kind):
        return yh if kind == 0 else 1 - yh

    w_slot = {}

    def w_index(key):
        if key not in w_slot:
            w_slot[key] = len(w_slot)
        return w_slot[key]

    def w_copy(route, piece, target, core=0):
        distance, kind, first, count = piece
        owner = z_at(distance) * 4 + y_of(kind) * 2 + (1 - c if core else c)
        view = weight_at(owner, first, count)
        return remote(view, view, c_sems, w_index((route, piece)), target)

    def w_core(piece):
        go(w_copy("core", piece, sibling))

    def w_core_take(piece):
        w_copy("core", piece, sibling, 1).wait_recv()

    def w_rows(kind):
        return (0, depth) if kind == 0 else (0, W_ROWS)

    rest = (W_ROWS, depth - W_ROWS)

    def w_route(direction):
        return "up" if direction == 0 else "down"

    def w_send(direction, kind, travelled):
        signed = -travelled if direction == 0 else travelled
        first, count = w_rows(kind)
        owner = z_at(signed) * 4 + y_of(kind) * 2 + c
        view = weight_at(owner, first, count)
        there = -travelled - 1 if direction == 0 else travelled + 1
        slot = w_index((w_route(direction), (there, kind, first, count)))
        go(remote(view, view, c_sems, slot, up if direction == 0 else down))

    def w_take(kind, d):
        for direction in range(2):
            if d <= limits[direction, kind]:
                signed = -d if direction == 0 else d
                piece = (signed, kind) + w_rows(kind)
                w_copy(w_route(direction), piece, up).wait_recv()
                if kind == 0:
                    owner = z_at(signed) * 4 + yh * 2 + c
                    view = weight_at(owner, *rest)
                    go(remote(view, view, c_sems, w_index(("y", (signed, 1) + rest)), opposite))
                w_core(piece)

    def w_pass(kind, d):
        for direction in range(2):
            if d < limits[direction, kind]:
                w_send(direction, kind, d)

    def w_across(signed):
        piece = (signed, 1) + rest
        w_copy("y", piece, opposite).wait_recv()
        w_core(piece)

    for k in range(slots):
        go(remote(patches.at[slot_at(k), columns(x * 2 + 1 - yl)], got.at[0, k], a_sems, k, across))
    for copy in own_w:
        copy.wait()
    whole = (0, depth)
    w_pass(0, 0)
    for copy in own:
        copy.wait()

    partner = {3: z3, 7: z7, 1: z1, 0: sibling}
    order = [[7, 3, 1, 0], [3, 7, 1, 0], [7, 3, 1, 0], [3, 7, 1, 0]]

    def merge(k, step):
        remote(got.at[step, k], got.at[step, k], a_sems, step * slots + k, sibling).wait_recv()
        taken = takes(k, step)
        return lax.select_n(taken, hold[step, k], got[step, k])

    def row_step(step, which_slots=(0, 1, 2, 3)):
        for k in which_slots:
            hold[step + 1, k] = merge(k, step)
            go(
                remote(
                    hold.at[step + 1, k], got.at[step + 1, k], a_sems,
                    (step + 1) * slots + k, partner[order[k][step]],
                )
            )

    def row_copy(k, xx, y_low, which, target):
        view = rows.at[slot_at(k), columns(xx * 2 + y_low)]
        return remote(view, view, b_sems, k * 7 + which, target)

    def rows_first(k):
        merged = merge(k, 4).astype(f32)
        place = lax.broadcasted_iota(jnp.int32, (slot_rows, share), 0)
        live = place < live_count(k)
        rows[slot_at(k), columns(me_t)] = jnp.where(live, merged, 0.0).astype(bf16)
        go(row_copy(k, x, yl, 0, beside))
        go(row_copy(k, x, yl, 1, right))
        go(row_copy(k, x, yl, 4, left))

    def rows_second(k):
        row_copy(k, x, 1 - yl, 0, beside).wait_recv()
        go(row_copy(k, x, 1 - yl, 3, right))
        go(row_copy(k, x, 1 - yl, 5, left))

    def rows_third(k):
        row_copy(k, x_down, yl, 1, right).wait_recv()
        go(row_copy(k, x_down, yl, 2, right))
        row_copy(k, x_up, 1 - yl, 5, left).wait_recv()
        go(row_copy(k, x_up, 1 - yl, 6, left))

    def rows_last(k):
        row_copy(k, lax.rem(x + 2, NX), yl, 2, right).wait_recv()
        row_copy(k, x_down, 1 - yl, 3, right).wait_recv()
        row_copy(k, x_up, yl, 4, left).wait_recv()
        row_copy(k, lax.rem(x + 2, NX), 1 - yl, 6, left).wait_recv()

    def norm_slot(k):
        @pl.loop(0, per_slot)
        def _(i):
            at = pl.ds(pl.multiple_of(k * slot_rows + i * step_rows, step_rows), step_rows)
            values = rows[at, :].astype(f32)
            mean = jnp.mean(values, axis=-1, keepdims=True)
            centred = values - mean
            factor = lax.rsqrt(jnp.mean(centred * centred, axis=-1, keepdims=True) + epsilon)
            normed[at, :] = (centred * factor * gain[...]).astype(bf16)
            row_mean[at, :] = jnp.broadcast_to(mean, (step_rows, 128))
            row_factor[at, :] = jnp.broadcast_to(factor, (step_rows, 128))

    def project(distance):
        if distance == 0:
            for kind in range(2):
                w_core_take((0, kind) + whole)
        else:
            for kind, part in ((0, whole), (1, (0, W_ROWS)), (1, rest)):
                signed = distance
                if abs(distance) == 4:
                    signed = 4 if (kind, part) == (1, (0, W_ROWS)) else -4
                w_core_take((signed, kind) + part)
        at = pl.ds(pl.multiple_of(z_at(distance) * band, band), band)
        part = dot_nn(normed[:, at], weights[at, qkv_part])
        if distance == 0:
            projected[...] = part
        else:
            projected[...] += part

    def live_rows(i, shape):
        place = lax.broadcasted_iota(jnp.int32, shape, 0) + lax.rem(i, per_slot) * step_rows
        return place < live_count(lax.div(i, per_slot))

    row_step(0, (0, 1, 2, 3))
    view = weight_at(my_f, *whole)
    go(remote(view, view, c_sems, w_index(("y", (0, 1) + whole)), opposite))
    w_core((0, 0) + whole)
    w_take(0, 1)
    row_step(1, (0, 1, 2, 3))
    w_copy("y", (0, 1) + whole, opposite).wait_recv()
    w_core((0, 1) + whole)
    row_step(2, (0, 1, 2, 3))
    w_pass(0, 1)
    w_pass(1, 0)
    w_across(-1)
    w_across(1)
    row_step(3, (0, 1, 2, 3))
    rows_first(0)
    rows_first(1)
    rows_first(2)
    rows_first(3)
    w_take(0, 2)
    w_pass(0, 2)
    rows_second(0)
    rows_second(1)
    rows_second(2)
    rows_second(3)
    w_take(1, 1)
    w_pass(1, 1)
    rows_third(0)
    rows_third(1)
    rows_third(2)
    rows_third(3)
    w_across(-2)
    w_across(2)
    w_take(0, 3)
    w_pass(0, 3)
    w_take(1, 2)
    w_pass(1, 2)
    rows_last(0)
    norm_slot(0)
    rows_last(1)
    norm_slot(1)
    w_across(-3)
    w_across(3)
    rows_last(2)
    norm_slot(2)
    rows_last(3)
    norm_slot(3)
    w_take(0, 4)
    w_take(1, 3)
    w_pass(1, 3)
    project(0)
    project(-1)
    project(1)
    load.wait()

    @pl.loop(0, tok // step_rows)
    def _(i):
        at = pl.ds(pl.multiple_of(i * step_rows, step_rows), step_rows)
        values = upstream[at, :].astype(f32)
        upstream[at, :] = jnp.where(live_rows(i, values.shape), values, 0.0).astype(bf16)
    project(-2)
    project(2)
    w_take(1, 4)
    w_across(-4)
    project(-3)
    project(3)
    project(4)

    query_scale = qk_gain[0:1, :] * head_dim ** (-0.5)
    key_scale = qk_gain[1:2, :]

    def head_at(h, which):
        return pl.ds(pl.multiple_of((h * 3 + which) * head_dim, head_dim), head_dim)

    def mixed_at(h):
        return pl.ds(pl.multiple_of(h * head_dim, head_dim), head_dim)

    def head_rows(h, s):
        query_hat, query_factor = head_norm(projected[slot_at(s), head_at(h, 0)])
        key_hat, key_factor = head_norm(projected[slot_at(s), head_at(h, 1)])
        values = projected[slot_at(s), head_at(h, 2)].astype(bf16)
        return (
            (query_hat, query_factor, (query_hat * query_scale).astype(bf16)),
            (key_hat, key_factor, (key_hat * key_scale).astype(bf16)),
            values,
        )

    @pl.loop(0, heads)
    def _(h):
        i = lax.broadcasted_iota(jnp.int32, (slot_rows, slot_rows), 0)
        j = lax.broadcasted_iota(jnp.int32, (slot_rows, slot_rows), 1)
        for s in range(slots):
            (_, _, query), (_, _, key_rows), values = head_rows(h, s)
            count = live_count(s)
            allowed = (jnp.maximum(i, j) < count) | (i == j)
            raised = jnp.where(allowed, jnp.exp(dot_nt(query, key_rows)), 0.0)
            weight = raised / jnp.sum(raised, axis=-1, keepdims=True)
            attention[h, s] = weight
            mixed[slot_at(s), mixed_at(h)] = dot_nn(weight.astype(bf16), values).astype(bf16)

    x_limits = {(0, 0): 2, (0, 1): 1, (1, 0): 1, (1, 1): 2}
    x_slot = {}
    for p in range(2):
        for direction in range(2):
            for kind in range(2):
                for d in range(x_limits[direction, kind], 0, -1):
                    x_slot[p, direction, kind, d] = len(x_slot)

    def x_shard(direction, kind, d):
        xx = lax.rem(x + (d if direction == 0 else NX - d), NX)
        return xx * 2 + (yl if kind == 0 else 1 - yl)

    def x_go(p, direction, kind, d):
        slot = x_slot[p, direction, kind, d]
        go(
            remote(
                parts.at[p, x_shard(direction, kind, d)], x_got.at[slot], x_sems, slot,
                right if direction == 0 else left,
            )
        )

    def x_take(p, direction, kind, d):
        slot = x_slot[p, direction, kind, d]
        shard = x_shard(direction, kind, d - 1)
        remote(parts.at[p, shard], x_got.at[slot], x_sems, slot, right).wait_recv()
        add_into(parts.at[p, shard], x_got.at[slot])

    def x_first(p):
        x_go(p, 0, 0, 2)
        x_go(p, 1, 1, 2)

    def x_second(p):
        x_take(p, 1, 1, 2)
        x_go(p, 1, 1, 1)
        x_go(p, 0, 1, 1)
        x_take(p, 0, 0, 2)

    def x_third(p):
        x_take(p, 0, 1, 1)
        x_take(p, 1, 1, 1)
        go(remote(parts.at[p, x * 2 + 1 - yl], l_got.at[p], l_sems, p, beside))
        x_go(p, 0, 0, 1)
        x_go(p, 1, 0, 1)

    def x_last(p):
        x_take(p, 1, 0, 1)
        x_take(p, 0, 0, 1)

    def l_take(p):
        remote(parts.at[p, me_t], l_got.at[p], l_sems, p, beside).wait_recv()

    def shard_rows(shard):
        return pl.ds(pl.multiple_of(shard * share, share), share)

    @pl.loop(0, 8)
    def _(shard):
        parts[0, shard] = dot_nt(mixed[...], weights[shard_rows(shard), out_part]).astype(bf16)

    x_first(0)

    grad_mixed[...] = dot_nn(upstream[...], weights[:, out_part]).astype(bf16)

    @pl.loop(0, heads)
    def _(h):
        for s in range(slots):
            (query_hat, query_factor, query), (key_hat, key_factor, key_rows), values = head_rows(
                h, s
            )
            weight = attention[h, s]
            rounded = weight.astype(bf16)
            above = grad_mixed[slot_at(s), mixed_at(h)]
            grad_value = dot_tn(rounded, above)
            grad_weight = dot_nt(above, values)
            grad_scores = weight * (
                grad_weight - jnp.sum(weight * grad_weight, axis=-1, keepdims=True)
            )
            grad_scores = grad_scores.astype(bf16)
            grad_query = dot_nn(grad_scores, key_rows)
            grad_key = dot_tn(grad_scores, query)
            grad_qkv[slot_at(s), head_at(h, 0)] = head_norm_back(
                grad_query * query_scale, query_hat, query_factor
            ).astype(bf16)
            grad_qkv[slot_at(s), head_at(h, 1)] = head_norm_back(
                grad_key * key_scale, key_hat, key_factor
            ).astype(bf16)
            grad_qkv[slot_at(s), head_at(h, 2)] = grad_value.astype(bf16)

    distances = [4, 3, -3, 2, -2, 1, -1, 0]
    kept = pl.ds(0, G_ROWS)
    crossing = pl.ds(G_ROWS, depth - G_ROWS)

    def compute(distance):
        zz = z_at(distance)
        at = pl.ds(pl.multiple_of(zz * band, band), band)
        left_term = dot_tn(normed[:, at], grad_qkv[...]).astype(bf16)
        for q in range(4):
            terms[zz, q // 2, q % 2, :, 0:qkv_cols] = left_term[q * depth : (q + 1) * depth]
        right_term = dot_tn(upstream[:, at], mixed[...]).astype(bf16)
        for q in range(4):
            terms[zz, q // 2, q % 2, :, qkv_cols:] = right_term[q * depth : (q + 1) * depth]
        go(
            remote(
                terms.at[zz, :, 1 - c], theirs.at[zz], core_sems, distances.index(distance), sibling
            )
        )

    def have(distance):
        zz = z_at(distance)
        remote(
            terms.at[zz, :, c], theirs.at[zz], core_sems, distances.index(distance), sibling
        ).wait_recv()
        for y in range(2):
            add_into(terms.at[zz, y, c], theirs.at[zz, y])

    def y_go(distance):
        i = distances.index(distance)
        zz = z_at(distance)
        target = y_got.at[crossing] if distance == 0 else y_part.at[i]
        go(remote(terms.at[zz, 1 - yh, c, crossing], target, y_sems, i, opposite))

    def y_take(distance):
        i = distances.index(distance)
        zz = z_at(distance)
        remote(terms.at[zz, yh, c, crossing], y_part.at[i], y_sems, i, opposite).wait_recv()
        add_into(terms.at[zz, yh, c, crossing], y_part.at[i], 16)

    z_slot = {}
    for direction in range(2):
        for kind in range(2):
            for d in range(limits[direction, kind], 0, -1):
                z_slot[direction, kind, d] = len(z_slot)

    def z_views(kind, zz, slot):
        if kind == 0:
            return terms.at[zz, yh, c], z_got.at[slot]
        return terms.at[zz, 1 - yh, c, kept], z_got.at[slot, kept]

    def z_go(direction, kind, d):
        zz = z_at(d if direction == 0 else -d)
        slot = z_slot[direction, kind, d]
        here, there = z_views(kind, zz, slot)
        go(remote(here, there, z_sems, slot, up if direction == 0 else down))

    def z_take(direction, kind, d):
        zz = z_at(d - 1 if direction == 0 else 1 - d)
        slot = z_slot[direction, kind, d]
        here, arrived = z_views(kind, zz, slot)
        remote(here, arrived, z_sems, slot, up).wait_recv()
        add_into(here, arrived, 16)

    def z_pass(direction, kind, d):
        z_take(direction, kind, d)
        z_go(direction, kind, d - 1)

    compute(4)
    compute(-3)
    have(4)
    y_go(4)
    z_go(1, 1, 4)
    have(-3)
    y_go(-3)
    compute(3)
    have(3)
    z_go(0, 1, 3)
    x_second(0)
    compute(2)
    have(2)
    compute(-2)
    have(-2)
    y_take(4)
    z_go(0, 0, 4)
    y_go(3)
    y_take(-3)
    z_go(1, 0, 3)
    y_go(-2)
    partial_sums[...] = jnp.zeros(partial_sums.shape, f32)

    @pl.loop(0, 8)
    def _(shard):
        at = shard_rows(shard)
        part = dot_nt(grad_qkv[...], weights[at, qkv_part]).astype(bf16)
        parts[1, shard] = part
        scaled = part.astype(f32) * gain[:, at]
        for q in range(share // 128):
            lanes = slice(q * 128, (q + 1) * 128)
            own = pl.ds(pl.multiple_of(shard * share + q * 128, 128), 128)
            centred = (rows[:, own].astype(f32) - row_mean[...]) * row_factor[...]
            partial_sums[0] += scaled[:, lanes]
            partial_sums[1] += scaled[:, lanes] * centred
    x_first(1)
    ones = jnp.ones((8, 128), f32)
    upper = lax.broadcasted_iota(jnp.int32, (8, tok), 0) < 4
    sums[...] = jnp.where(
        upper,
        exact_dot(ones, partial_sums[0], ((1,), (1,))),
        exact_dot(ones, partial_sums[1], ((1,), (1,))),
    )
    for o, peer in enumerate(peers):
        go(remote(sums, sums_got.at[o], s_sems, o, peer))
    z_pass(1, 1, 4)
    z_pass(0, 1, 3)
    x_third(0)
    compute(1)
    have(1)
    compute(-1)
    have(-1)
    y_take(3)
    z_pass(0, 0, 4)
    y_go(2)
    y_take(-2)
    z_pass(1, 0, 3)
    y_go(-1)
    compute(0)
    have(0)
    x_second(1)
    z_pass(1, 1, 3)
    z_pass(0, 1, 2)
    y_take(2)
    z_pass(0, 0, 3)
    y_go(1)
    y_take(-1)
    z_pass(1, 0, 2)
    y_go(0)
    x_last(0)
    l_take(0)

    @pl.loop(0, tok // step_rows)
    def _(i):
        at = pl.ds(pl.multiple_of(i * step_rows, step_rows), step_rows)
        total = parts[0, me_t, at, :].astype(f32) + l_got[0, at, :].astype(f32)
        attended[at, :] = jnp.where(live_rows(i, total.shape), total, 0.0).astype(bf16)
    z_pass(1, 1, 2)
    y_take(1)
    z_pass(0, 0, 2)
    x_third(1)
    z_take(0, 1, 1)
    z_take(1, 1, 1)
    go(remote(terms.at[z, 1 - yh, c, kept], y_got.at[kept], y_sems, 8, opposite))
    total_sums = sums[...]
    for o, peer in enumerate(peers):
        remote(sums, sums_got.at[o], s_sems, o, peer).wait_recv()
        total_sums += sums_got[o]
    pick = lax.broadcasted_iota(jnp.int32, (8, 128), 0)
    partial_sums[0] = exact_dot(
        total_sums, jnp.where(pick == 0, 1.0 / model, 0.0).astype(f32), ((0,), (0,))
    )
    partial_sums[1] = exact_dot(
        total_sums, jnp.where(pick == 4, 1.0 / model, 0.0).astype(f32), ((0,), (0,))
    )
    x_last(1)
    l_take(1)

    @pl.loop(0, tok // step_rows)
    def _(i):
        at = pl.ds(pl.multiple_of(i * step_rows, step_rows), step_rows)
        for q in range(share // 128):
            lanes = slice(q * 128, (q + 1) * 128)
            own = pl.ds(pl.multiple_of(me_t * share + q * 128, 128), 128)
            total = parts[1, me_t, at, lanes].astype(f32) + l_got[1, at, lanes].astype(f32)
            centred = (rows[at, own].astype(f32) - row_mean[at, :]) * row_factor[at, :]
            grad_rows[at, lanes] = (
                row_factor[at, :]
                * (total * gain[:, own] - partial_sums[0, at, :] - centred * partial_sums[1, at, :])
            ).astype(bf16)
    z_take(1, 0, 1)
    z_take(0, 0, 1)
    remote(terms.at[z, yh, c, crossing], y_got.at[crossing], y_sems, 7, opposite).wait_recv()
    remote(terms.at[z, yh, c, kept], y_got.at[kept], y_sems, 8, opposite).wait_recv()

    @pl.loop(0, depth // step_rows)
    def _(i):
        at = pl.ds(pl.multiple_of(i * step_rows, step_rows), step_rows)
        total = terms[z, yh, c, at, :].astype(f32) + y_got[at, :].astype(f32)
        grad_qkv_w[at, :] = total[:, :qkv_cols]
        grad_out_w[at, :] = total[:, qkv_cols:]

    for copy in sent:
        copy.wait_send()


def branch(masks, counts, gain, qk_gain, patches, cotangent, qkv_weight, out_weight):
    bf16, f32 = jnp.bfloat16, jnp.float32
    tok, model = patches.shape
    qkv_cols, out_cols = qkv_weight.shape[1], out_weight.shape[1]
    wide = qkv_cols + out_cols
    depth = model // 32
    share = model // 8
    head_dim = qk_gain.shape[1]
    heads = out_cols // head_dim
    slots = masks.shape[0]
    slot_rows = tok // slots
    hbm = pl.BlockSpec(memory_space=pl.ANY)
    vmem = pl.BlockSpec(memory_space=pltpu.VMEM)
    smem = pl.BlockSpec(memory_space=pltpu.SMEM)
    dma = pltpu.SemaphoreType.DMA
    sems = []
    for n in (5 * slots, 7 * slots, 45, 8, 14, 9, 12, 2, 7):
        sems += [dma((n,)), dma((n,))]
    return pl.pallas_call(
        branch_kernel,
        out_shape=(
            jax.ShapeDtypeStruct((tok, share), bf16),
            jax.ShapeDtypeStruct((tok, share), bf16),
            jax.ShapeDtypeStruct((depth, qkv_cols), f32),
            jax.ShapeDtypeStruct((depth, out_cols), f32),
        ),
        in_specs=[smem, smem, vmem, vmem, hbm, hbm, hbm, hbm],
        out_specs=(vmem,) * 4,
        scratch_shapes=[
            pltpu.VMEM((5, slots, slot_rows, share), bf16),
            pltpu.VMEM((5, slots, slot_rows, share), bf16),
            pltpu.VMEM((tok, model), bf16),
            pltpu.VMEM((model, wide), bf16),
            pltpu.VMEM((tok, model), bf16),
            pltpu.VMEM((tok, model), bf16),
            pltpu.VMEM((tok, 128), f32),
            pltpu.VMEM((tok, 128), f32),
            pltpu.VMEM((tok, qkv_cols), f32),
            pltpu.VMEM((heads, slots, slot_rows, slot_rows), f32),
            pltpu.VMEM((tok, out_cols), bf16),
            pltpu.VMEM((tok, out_cols), bf16),
            pltpu.VMEM((tok, qkv_cols), bf16),
            pltpu.VMEM((NZ, 2, 2, depth, wide), bf16),
            pltpu.VMEM((NZ, 2, depth, wide), bf16),
            pltpu.VMEM((7, depth - G_ROWS, wide), bf16),
            pltpu.VMEM((14, depth, wide), bf16),
            pltpu.VMEM((depth, wide), bf16),
            pltpu.VMEM((2, 8, tok, share), bf16),
            pltpu.VMEM((12, tok, share), bf16),
            pltpu.VMEM((2, tok, share), bf16),
            pltpu.VMEM((2, tok, 128), f32),
            pltpu.VMEM((8, tok), f32),
            pltpu.VMEM((7, 8, tok), f32),
        ]
        + sems
        + [dma((slots + 3,))],
        compiler_params=pltpu.CompilerParams(
            collective_id=0, has_side_effects=True, vmem_limit_bytes=60 * 2**20
        ),
        cost_estimate=pl.CostEstimate(
            flops=13 * 10**9, bytes_accessed=16 * 2**20, transcendentals=150528
        ),
    )(masks, counts, gain, qk_gain, patches, cotangent, qkv_weight, out_weight)


def settle_kernel(*refs):
    n = len(refs) // 3
    sem = refs[-1]
    arrive = [
        pltpu.make_async_copy(refs[i], refs[2 * n + i], sem.at[i]) for i in range(n)
    ]
    leave = [
        pltpu.make_async_copy(refs[2 * n + i], refs[n + i], sem.at[n + i]) for i in range(n)
    ]
    for copy in arrive:
        copy.start()
    for one, other in zip(arrive, leave):
        one.wait()
        other.start()
    for copy in leave:
        copy.wait()


def settle(arrays):
    hbm = pl.BlockSpec(memory_space=pltpu.HBM)
    return pl.pallas_call(
        settle_kernel,
        out_shape=tuple(jax.ShapeDtypeStruct(a.shape, a.dtype) for a in arrays),
        in_specs=[hbm] * len(arrays),
        out_specs=(hbm,) * len(arrays),
        scratch_shapes=[pltpu.VMEM(a.shape, a.dtype) for a in arrays]
        + [pltpu.SemaphoreType.DMA((2 * len(arrays),))],
        compiler_params=pltpu.CompilerParams(vmem_limit_bytes=60 * 2**20),
    )(*arrays)


def per_device(patches, cotangent, counts, masks, norm_gain, qk_gain, qkv_weight, out_weight):
    return settle(
        branch(
            masks, counts.T, norm_gain[None, :], qk_gain, patches, cotangent, qkv_weight, out_weight
        )
    )


def solution(mesh):
    in_specs = (
        P("fsdp", None),
        P("fsdp", None),
        P(),
        P(),
        P(),
        P(),
        P("fsdp", "tp"),
        P("fsdp", "tp"),
    )
    out_specs = (P("fsdp", "tp"), P("fsdp", "tp"), P("fsdp", "tp"), P("fsdp", "tp"))
    return jax.shard_map(
        per_device, mesh=mesh, in_specs=in_specs, out_specs=out_specs, check_vma=False
    )
```

```python
import functools
import jax
import jax.numpy as jnp
from jax import lax
from jax.experimental import pallas as pl
from jax.experimental.pallas import tpu as pltpu
from jax.sharding import PartitionSpec as P

MESH = pl.DeviceIdType.MESH
epsilon = 1e-06
NZ, NX = 8, 4
W_ROWS, G_ROWS = 48, 48


def coords():
    f = lax.axis_index("fsdp")
    t = lax.axis_index("tp")
    z, yh, c = lax.div(f, 4), lax.rem(lax.div(f, 2), 2), lax.rem(f, 2)
    x, yl = lax.div(t, 2), lax.rem(t, 2)
    return z, yh, c, x, yl


def dev(z, yh, c, x, yl):
    return (z * 4 + yh * 2 + c, x * 2 + yl)


def remote(src, dst, sems, slot, target):
    send, recv = sems
    return pltpu.make_async_remote_copy(
        src_ref=src,
        dst_ref=dst,
        send_sem=send.at[slot],
        recv_sem=recv.at[slot],
        device_id=target,
        device_id_type=MESH,
    )


def greet(partners):
    barrier = pltpu.get_barrier_semaphore()
    for partner in partners:
        pl.semaphore_signal(barrier, inc=1, device_id=partner, device_id_type=MESH)
    pl.semaphore_wait(barrier, len(partners))


def head_norm(values):
    centred = values - jnp.mean(values, axis=-1, keepdims=True)
    factor = lax.rsqrt(jnp.mean(centred * centred, axis=-1, keepdims=True) + epsilon)
    return centred * factor, factor


def head_norm_back(upstream, normed, factor):
    return factor * (
        upstream
        - jnp.mean(upstream, axis=-1, keepdims=True)
        - normed * jnp.mean(upstream * normed, axis=-1, keepdims=True)
    )


def dot_nn(a, b):
    return jnp.dot(a, b, preferred_element_type=jnp.float32)


def dot_nt(a, b):
    return lax.dot_general(a, b, (((1,), (1,)), ((), ())), preferred_element_type=jnp.float32)


def dot_tn(a, b):
    return lax.dot_general(a, b, (((0,), (0,)), ((), ())), preferred_element_type=jnp.float32)


def exact_dot(a, b, dims):
    return lax.dot_general(
        a, b, (dims, ((), ())),
        precision=lax.Precision.HIGHEST, preferred_element_type=jnp.float32,
    )


def add_into(total, other, rows_at=32):
    @pl.loop(0, total.shape[0] // rows_at, unroll=True)
    def _(i):
        at = pl.ds(pl.multiple_of(i * rows_at, rows_at), rows_at)
        total[at, :] = (
            total[at, :].astype(jnp.float32) + other[at, :].astype(jnp.float32)
        ).astype(total.dtype)


def branch_kernel(
    masks_ref, counts_ref, gain, qk_gain, patches, cotangent, qkv_w, out_w,
    attended, grad_rows, grad_qkv_w, grad_out_w,
    hold, got, rows, weights, upstream, normed, row_mean, row_factor, projected, attention,
    mixed, grad_mixed, grad_qkv, terms, theirs, y_part, z_got, y_got, parts, x_got, l_got,
    partial_sums, sums, sums_got,
    a_send, a_recv, b_send, b_recv, c_send, c_recv,
    core_send, core_recv, z_send_sem, z_recv_sem, y_send, y_recv,
    x_send, x_recv, l_send, l_recv, s_send, s_recv, local_sem,
):
    f32, bf16 = jnp.float32, jnp.bfloat16
    z, yh, c, x, yl = coords()
    me_t = x * 2 + yl
    tok, model = rows.shape
    share = attended.shape[1]
    heads = attention.shape[0]
    slots, slot_rows = attention.shape[1], attention.shape[2]
    head_dim = qk_gain.shape[1]
    qkv_cols, out_cols = grad_qkv_w.shape[1], grad_out_w.shape[1]
    depth = grad_qkv_w.shape[0]
    band = 4 * depth
    z_up, z_down = lax.rem(z + 1, NZ), lax.rem(z + NZ - 1, NZ)
    x_up, x_down = lax.rem(x + 1, NX), lax.rem(x + NX - 1, NX)
    sibling = dev(z, yh, 1 - c, x, yl)
    opposite = dev(z, 1 - yh, c, x, yl)
    beside = dev(z, yh, c, x, 1 - yl)
    up, down = dev(z_up, yh, c, x, yl), dev(z_down, yh, c, x, yl)
    right, left = dev(z, yh, c, x_up, yl), dev(z, yh, c, x_down, yl)
    across = dev(z, 1 - yh, c, x, 1 - yl)
    z7 = dev(7 - z, yh, c, x, yl)
    z3 = dev(z + 3 - 2 * lax.rem(z, 4), yh, c, x, yl)
    z1 = dev(z + 1 - 2 * lax.rem(z, 2), yh, c, x, yl)
    my_f = z * 4 + yh * 2 + c
    peers = [(my_f, lax.rem(me_t + o, 8)) for o in range(1, 8)]
    f32, bf16 = jnp.float32, jnp.bfloat16

    def live_count(k):
        return counts_ref[k, jnp.bitwise_xor(my_f, masks_ref[k])]

    def mask_bit(k, place):
        return jnp.bitwise_and(lax.shift_right_logical(masks_ref[k], place), 1)

    def takes(k, step):
        which = -1 if step == 0 else order[k][step - 1]
        if which in (-1, 7, 0):
            return mask_bit(k, {-1: 1, 7: 4, 0: 0}[which]) > 0
        places = (3, 4) if which == 3 else (2, 3)
        return mask_bit(k, places[0]) != mask_bit(k, places[1])

    def slot_at(s):
        return pl.ds(s * slot_rows, slot_rows)

    def columns(index):
        return pl.ds(pl.multiple_of(index * share, 128), share)

    def weight_at(index, first, count):
        return weights.at[pl.ds(pl.multiple_of(index * depth + first, 16), count), :]

    own = [
        pltpu.make_async_copy(patches.at[slot_at(k), columns(me_t)], hold.at[0, k], local_sem.at[k])
        for k in range(slots)
    ]
    mine = pl.ds(pl.multiple_of(my_f * depth, 16), depth)
    own_w = [
        pltpu.make_async_copy(qkv_w, weights.at[mine, pl.ds(0, qkv_cols)], local_sem.at[slots]),
        pltpu.make_async_copy(
            out_w, weights.at[mine, pl.ds(qkv_cols, out_cols)], local_sem.at[slots + 1]
        ),
    ]
    load = pltpu.make_async_copy(cotangent, upstream, local_sem.at[slots + 2])
    for copy in own_w + own + [load]:
        copy.start()
    greet([across, z7, z3, z1, sibling, opposite, up, down] + peers)
    sent = []

    def go(copy):
        copy.start()
        sent.append(copy)

    a_sems, b_sems, c_sems = (a_send, a_recv), (b_send, b_recv), (c_send, c_recv)
    core_sems, z_sems = (core_send, core_recv), (z_send_sem, z_recv_sem)
    y_sems, x_sems, l_sems = (y_send, y_recv), (x_send, x_recv), (l_send, l_recv)
    s_sems = (s_send, s_recv)
    step_rows = 16
    per_slot = slot_rows // step_rows
    qkv_part, out_part = pl.ds(0, qkv_cols), pl.ds(qkv_cols, out_cols)
    limits = {(0, 0): 4, (0, 1): 3, (1, 0): 3, (1, 1): 4}

    def z_at(distance):
        return lax.rem(z + distance + NZ, NZ)

    def y_of(kind):
        return yh if kind == 0 else 1 - yh

    w_slot = {}

    def w_index(key):
        if key not in w_slot:
            w_slot[key] = len(w_slot)
        return w_slot[key]

    def w_copy(route, piece, target, core=0):
        distance, kind, first, count = piece
        owner = z_at(distance) * 4 + y_of(kind) * 2 + (1 - c if core else c)
        view = weight_at(owner, first, count)
        return remote(view, view, c_sems, w_index((route, piece)), target)

    def w_core(piece):
        go(w_copy("core", piece, sibling))

    def w_core_take(piece):
        w_copy("core", piece, sibling, 1).wait_recv()

    def w_rows(kind):
        return (0, depth) if kind == 0 else (0, W_ROWS)

    rest = (W_ROWS, depth - W_ROWS)

    def w_route(direction):
        return "up" if direction == 0 else "down"

    def w_send(direction, kind, travelled):
        signed = -travelled if direction == 0 else travelled
        first, count = w_rows(kind)
        owner = z_at(signed) * 4 + y_of(kind) * 2 + c
        view = weight_at(owner, first, count)
        there = -travelled - 1 if direction == 0 else travelled + 1
        slot = w_index((w_route(direction), (there, kind, first, count)))
        go(remote(view, view, c_sems, slot, up if direction == 0 else down))

    def w_take(kind, d):
        for direction in range(2):
            if d <= limits[direction, kind]:
                signed = -d if direction == 0 else d
                piece = (signed, kind) + w_rows(kind)
                w_copy(w_route(direction), piece, up).wait_recv()
                if kind == 0:
                    owner = z_at(signed) * 4 + yh * 2 + c
                    view = weight_at(owner, *rest)
                    go(remote(view, view, c_sems, w_index(("y", (signed, 1) + rest)), opposite))
                w_core(piece)

    def w_pass(kind, d):
        for direction in range(2):
            if d < limits[direction, kind]:
                w_send(direction, kind, d)

    def w_across(signed):
        piece = (signed, 1) + rest
        w_copy("y", piece, opposite).wait_recv()
        w_core(piece)

    for k in range(slots):
        go(remote(patches.at[slot_at(k), columns(x * 2 + 1 - yl)], got.at[0, k], a_sems, k, across))
    for copy in own_w:
        copy.wait()
    whole = (0, depth)
    for copy in own:
        copy.wait()

    partner = {3: z3, 7: z7, 1: z1, 0: sibling}
    order = [[7, 3, 1, 0], [3, 7, 1, 0], [7, 3, 1, 0], [3, 7, 1, 0]]

    def merge(k, step):
        remote(got.at[step, k], got.at[step, k], a_sems, step * slots + k, sibling).wait_recv()
        taken = takes(k, step)
        return lax.select_n(taken, hold[step, k], got[step, k])

    def row_step(step, which_slots=(0, 1, 2, 3)):
        for k in which_slots:
            hold[step + 1, k] = merge(k, step)
            go(
                remote(
                    hold.at[step + 1, k], got.at[step + 1, k], a_sems,
                    (step + 1) * slots + k, partner[order[k][step]],
                )
            )

    def row_copy(k, xx, y_low, which, target):
        view = rows.at[slot_at(k), columns(xx * 2 + y_low)]
        return remote(view, view, b_sems, k * 7 + which, target)

    def rows_first(k):
        merged = merge(k, 4).astype(f32)
        place = lax.broadcasted_iota(jnp.int32, (slot_rows, share), 0)
        live = place < live_count(k)
        rows[slot_at(k), columns(me_t)] = jnp.where(live, merged, 0.0).astype(bf16)
        go(row_copy(k, x, yl, 0, beside))
        go(row_copy(k, x, yl, 1, right))
        go(row_copy(k, x, yl, 4, left))

    def rows_second(k):
        row_copy(k, x, 1 - yl, 0, beside).wait_recv()
        go(row_copy(k, x, 1 - yl, 3, right))
        go(row_copy(k, x, 1 - yl, 5, left))

    def rows_third(k):
        row_copy(k, x_down, yl, 1, right).wait_recv()
        go(row_copy(k, x_down, yl, 2, right))
        row_copy(k, x_up, 1 - yl, 5, left).wait_recv()
        go(row_copy(k, x_up, 1 - yl, 6, left))

    def rows_last(k):
        row_copy(k, lax.rem(x + 2, NX), yl, 2, right).wait_recv()
        row_copy(k, x_down, 1 - yl, 3, right).wait_recv()
        row_copy(k, x_up, yl, 4, left).wait_recv()
        row_copy(k, lax.rem(x + 2, NX), 1 - yl, 6, left).wait_recv()

    def norm_slot(k):
        @pl.loop(0, per_slot, unroll=True)
        def _(i):
            at = pl.ds(pl.multiple_of(k * slot_rows + i * step_rows, step_rows), step_rows)
            values = rows[at, :].astype(f32)
            mean = jnp.mean(values, axis=-1, keepdims=True)
            centred = values - mean
            factor = lax.rsqrt(jnp.mean(centred * centred, axis=-1, keepdims=True) + epsilon)
            normed[at, :] = (centred * factor * gain[...]).astype(bf16)
            row_mean[at, :] = jnp.broadcast_to(mean, (step_rows, 128))
            row_factor[at, :] = jnp.broadcast_to(factor, (step_rows, 128))

    def project(distance):
        if distance == 0:
            for kind in range(2):
                w_core_take((0, kind) + whole)
        else:
            for kind, part in ((0, whole), (1, (0, W_ROWS)), (1, rest)):
                signed = distance
                if abs(distance) == 4:
                    signed = 4 if (kind, part) == (1, (0, W_ROWS)) else -4
                w_core_take((signed, kind) + part)
        at = pl.ds(pl.multiple_of(z_at(distance) * band, band), band)
        part = dot_nn(normed[:, at], weights[at, qkv_part])
        if distance == 0:
            projected[...] = part
        else:
            projected[...] += part

    def live_rows(i, shape):
        place = lax.broadcasted_iota(jnp.int32, shape, 0) + lax.rem(i, per_slot) * step_rows
        return place < live_count(lax.div(i, per_slot))

    w_pass(0, 0)
    row_step(0, (0, 1, 2, 3))
    view = weight_at(my_f, *whole)
    go(remote(view, view, c_sems, w_index(("y", (0, 1) + whole)), opposite))
    w_core((0, 0) + whole)
    w_take(0, 1)
    row_step(1, (0, 1, 2, 3))
    load.wait()

    @pl.loop(0, tok // step_rows)
    def _(i):
        at = pl.ds(pl.multiple_of(i * step_rows, step_rows), step_rows)
        values = upstream[at, :].astype(f32)
        upstream[at, :] = jnp.where(live_rows(i, values.shape), values, 0.0).astype(bf16)
    w_copy("y", (0, 1) + whole, opposite).wait_recv()
    w_core((0, 1) + whole)
    row_step(2, (0, 1, 2, 3))
    w_pass(0, 1)
    w_pass(1, 0)
    w_across(-1)
    w_across(1)
    row_step(3, (0, 1, 2, 3))
    rows_first(0)
    rows_first(1)
    rows_first(2)
    rows_first(3)
    w_take(0, 2)
    w_pass(0, 2)
    rows_second(0)
    rows_second(1)
    rows_second(2)
    rows_second(3)
    w_take(1, 1)
    w_pass(1, 1)
    rows_third(0)
    rows_third(1)
    rows_third(2)
    rows_third(3)
    w_across(-2)
    w_across(2)
    w_take(0, 3)
    w_pass(0, 3)
    w_take(1, 2)
    w_pass(1, 2)
    rows_last(0)
    norm_slot(0)
    rows_last(1)
    norm_slot(1)
    w_across(-3)
    w_across(3)
    rows_last(2)
    norm_slot(2)
    rows_last(3)
    norm_slot(3)
    w_take(0, 4)
    w_take(1, 3)
    w_pass(1, 3)
    project(0)
    project(-1)
    project(1)
    project(-2)
    project(2)
    w_take(1, 4)
    w_across(-4)
    project(-3)
    project(3)
    project(4)

    query_scale = qk_gain[0:1, :] * head_dim ** (-0.5)
    key_scale = qk_gain[1:2, :]

    def head_at(h, which):
        return pl.ds(pl.multiple_of((h * 3 + which) * head_dim, head_dim), head_dim)

    def mixed_at(h):
        return pl.ds(pl.multiple_of(h * head_dim, head_dim), head_dim)

    def head_rows(h, s):
        query_hat, query_factor = head_norm(projected[slot_at(s), head_at(h, 0)])
        key_hat, key_factor = head_norm(projected[slot_at(s), head_at(h, 1)])
        values = projected[slot_at(s), head_at(h, 2)].astype(bf16)
        return (
            (query_hat, query_factor, (query_hat * query_scale).astype(bf16)),
            (key_hat, key_factor, (key_hat * key_scale).astype(bf16)),
            values,
        )

    @pl.loop(0, heads, unroll=True)
    def _(h):
        i = lax.broadcasted_iota(jnp.int32, (slot_rows, slot_rows), 0)
        j = lax.broadcasted_iota(jnp.int32, (slot_rows, slot_rows), 1)
        for s in range(slots):
            (_, _, query), (_, _, key_rows), values = head_rows(h, s)
            count = live_count(s)
            allowed = (jnp.maximum(i, j) < count) | (i == j)
            raised = jnp.where(allowed, jnp.exp(dot_nt(query, key_rows)), 0.0)
            weight = raised / jnp.sum(raised, axis=-1, keepdims=True)
            attention[h, s] = weight
            mixed[slot_at(s), mixed_at(h)] = dot_nn(weight.astype(bf16), values).astype(bf16)

    x_limits = {(0, 0): 2, (0, 1): 1, (1, 0): 1, (1, 1): 2}
    x_slot = {}
    for p in range(2):
        for direction in range(2):
            for kind in range(2):
                for d in range(x_limits[direction, kind], 0, -1):
                    x_slot[p, direction, kind, d] = len(x_slot)

    def x_shard(direction, kind, d):
        xx = lax.rem(x + (d if direction == 0 else NX - d), NX)
        return xx * 2 + (yl if kind == 0 else 1 - yl)

    def x_go(p, direction, kind, d):
        slot = x_slot[p, direction, kind, d]
        go(
            remote(
                parts.at[p, x_shard(direction, kind, d)], x_got.at[slot], x_sems, slot,
                right if direction == 0 else left,
            )
        )

    def x_take(p, direction, kind, d):
        slot = x_slot[p, direction, kind, d]
        shard = x_shard(direction, kind, d - 1)
        remote(parts.at[p, shard], x_got.at[slot], x_sems, slot, right).wait_recv()
        add_into(parts.at[p, shard], x_got.at[slot])

    def x_first(p):
        x_go(p, 0, 0, 2)
        x_go(p, 1, 1, 2)

    def x_second(p):
        x_take(p, 1, 1, 2)
        x_go(p, 1, 1, 1)
        x_go(p, 0, 1, 1)
        x_take(p, 0, 0, 2)

    def x_third(p):
        x_take(p, 0, 1, 1)
        x_take(p, 1, 1, 1)
        go(remote(parts.at[p, x * 2 + 1 - yl], l_got.at[p], l_sems, p, beside))
        x_go(p, 0, 0, 1)
        x_go(p, 1, 0, 1)

    def x_last(p):
        x_take(p, 1, 0, 1)
        x_take(p, 0, 0, 1)

    def l_take(p):
        remote(parts.at[p, me_t], l_got.at[p], l_sems, p, beside).wait_recv()

    def shard_rows(shard):
        return pl.ds(pl.multiple_of(shard * share, share), share)

    @pl.loop(0, 8, unroll=2)
    def _(shard):
        parts[0, shard] = dot_nt(mixed[...], weights[shard_rows(shard), out_part]).astype(bf16)

    x_first(0)

    grad_mixed[...] = dot_nn(upstream[...], weights[:, out_part]).astype(bf16)

    @pl.loop(0, heads, unroll=True)
    def _(h):
        for s in range(slots):
            (query_hat, query_factor, query), (key_hat, key_factor, key_rows), values = head_rows(
                h, s
            )
            weight = attention[h, s]
            rounded = weight.astype(bf16)
            above = grad_mixed[slot_at(s), mixed_at(h)]
            grad_value = dot_tn(rounded, above)
            grad_weight = dot_nt(above, values)
            grad_scores = weight * (
                grad_weight - jnp.sum(weight * grad_weight, axis=-1, keepdims=True)
            )
            grad_scores = grad_scores.astype(bf16)
            grad_query = dot_nn(grad_scores, key_rows)
            grad_key = dot_tn(grad_scores, query)
            grad_qkv[slot_at(s), head_at(h, 0)] = head_norm_back(
                grad_query * query_scale, query_hat, query_factor
            ).astype(bf16)
            grad_qkv[slot_at(s), head_at(h, 1)] = head_norm_back(
                grad_key * key_scale, key_hat, key_factor
            ).astype(bf16)
            grad_qkv[slot_at(s), head_at(h, 2)] = grad_value.astype(bf16)

    distances = [4, 3, -3, 2, -2, 1, -1, 0]
    kept = pl.ds(0, G_ROWS)
    crossing = pl.ds(G_ROWS, depth - G_ROWS)

    def compute(distance):
        zz = z_at(distance)
        at = pl.ds(pl.multiple_of(zz * band, band), band)
        left_term = dot_tn(normed[:, at], grad_qkv[...]).astype(bf16)
        for q in range(4):
            terms[zz, q // 2, q % 2, :, 0:qkv_cols] = left_term[q * depth : (q + 1) * depth]
        right_term = dot_tn(upstream[:, at], mixed[...]).astype(bf16)
        for q in range(4):
            terms[zz, q // 2, q % 2, :, qkv_cols:] = right_term[q * depth : (q + 1) * depth]
        go(
            remote(
                terms.at[zz, :, 1 - c], theirs.at[zz], core_sems, distances.index(distance), sibling
            )
        )

    def have(distance):
        zz = z_at(distance)
        remote(
            terms.at[zz, :, c], theirs.at[zz], core_sems, distances.index(distance), sibling
        ).wait_recv()
        for y in range(2):
            add_into(terms.at[zz, y, c], theirs.at[zz, y])

    def y_go(distance):
        i = distances.index(distance)
        zz = z_at(distance)
        target = y_got.at[crossing] if distance == 0 else y_part.at[i]
        go(remote(terms.at[zz, 1 - yh, c, crossing], target, y_sems, i, opposite))

    def y_take(distance):
        i = distances.index(distance)
        zz = z_at(distance)
        remote(terms.at[zz, yh, c, crossing], y_part.at[i], y_sems, i, opposite).wait_recv()
        add_into(terms.at[zz, yh, c, crossing], y_part.at[i], 16)

    z_slot = {}
    for direction in range(2):
        for kind in range(2):
            for d in range(limits[direction, kind], 0, -1):
                z_slot[direction, kind, d] = len(z_slot)

    def z_views(kind, zz, slot):
        if kind == 0:
            return terms.at[zz, yh, c], z_got.at[slot]
        return terms.at[zz, 1 - yh, c, kept], z_got.at[slot, kept]

    def z_go(direction, kind, d):
        zz = z_at(d if direction == 0 else -d)
        slot = z_slot[direction, kind, d]
        here, there = z_views(kind, zz, slot)
        go(remote(here, there, z_sems, slot, up if direction == 0 else down))

    def z_take(direction, kind, d):
        zz = z_at(d - 1 if direction == 0 else 1 - d)
        slot = z_slot[direction, kind, d]
        here, arrived = z_views(kind, zz, slot)
        remote(here, arrived, z_sems, slot, up).wait_recv()
        add_into(here, arrived, 16)

    def z_pass(direction, kind, d):
        z_take(direction, kind, d)
        z_go(direction, kind, d - 1)

    partial_sums[...] = jnp.zeros(partial_sums.shape, f32)

    def back_part(distance):
        @pl.loop(0, 2, unroll=True)
        def _(low):
            shard = lax.rem(x + distance, NX) * 2 + low
            at = shard_rows(shard)
            part = dot_nt(grad_qkv[...], weights[at, qkv_part]).astype(bf16)
            parts[1, shard] = part
            scaled = part.astype(f32) * gain[:, at]
            for q in range(share // 128):
                lanes = slice(q * 128, (q + 1) * 128)
                own = pl.ds(pl.multiple_of(shard * share + q * 128, 128), 128)
                centred = (rows[:, own].astype(f32) - row_mean[...]) * row_factor[...]
                partial_sums[0] += scaled[:, lanes]
                partial_sums[1] += scaled[:, lanes] * centred
    compute(4)
    compute(-3)
    compute(3)
    x_second(0)
    have(4)
    y_go(4)
    compute(2)
    have(-3)
    have(3)
    back_part(2)
    z_go(1, 1, 4)
    z_go(0, 1, 3)
    y_go(-3)
    x_first(1)
    back_part(1)
    have(2)
    y_go(2)
    y_take(4)
    z_go(0, 0, 4)
    compute(-2)
    z_pass(0, 1, 3)
    compute(1)
    y_take(-3)
    z_pass(1, 1, 4)
    y_go(3)
    back_part(0)
    x_third(0)
    z_go(1, 0, 3)
    have(-2)
    compute(0)
    back_part(3)
    y_take(3)
    have(0)
    y_go(-2)
    z_pass(0, 0, 4)
    have(1)
    z_pass(0, 1, 2)
    z_pass(1, 1, 3)
    x_second(1)
    compute(-1)
    have(-1)
    y_go(1)
    y_go(-1)
    z_pass(1, 1, 2)
    z_take(1, 1, 1)
    z_take(0, 1, 1)
    y_take(2)
    z_pass(0, 0, 3)
    y_take(-2)
    z_pass(1, 0, 3)
    x_third(1)
    ones = jnp.ones((8, 128), f32)
    upper = lax.broadcasted_iota(jnp.int32, (8, tok), 0) < 4
    sums[...] = jnp.where(
        upper,
        exact_dot(ones, partial_sums[0], ((1,), (1,))),
        exact_dot(ones, partial_sums[1], ((1,), (1,))),
    )
    for o, peer in enumerate(peers):
        go(remote(sums, sums_got.at[o], s_sems, o, peer))
    y_take(1)
    x_last(0)
    total_sums = sums[...]
    for o, peer in enumerate(peers):
        remote(sums, sums_got.at[o], s_sems, o, peer).wait_recv()
        total_sums += sums_got[o]
    pick = lax.broadcasted_iota(jnp.int32, (8, 128), 0)
    partial_sums[0] = exact_dot(
        total_sums, jnp.where(pick == 0, 1.0 / model, 0.0).astype(f32), ((0,), (0,))
    )
    partial_sums[1] = exact_dot(
        total_sums, jnp.where(pick == 4, 1.0 / model, 0.0).astype(f32), ((0,), (0,))
    )
    y_take(-1)
    l_take(0)

    @pl.loop(0, tok // step_rows)
    def _(i):
        at = pl.ds(pl.multiple_of(i * step_rows, step_rows), step_rows)
        total = parts[0, me_t, at, :].astype(f32) + l_got[0, at, :].astype(f32)
        attended[at, :] = jnp.where(live_rows(i, total.shape), total, 0.0).astype(bf16)
    z_pass(0, 0, 2)
    go(remote(terms.at[z, 1 - yh, c, kept], y_got.at[kept], y_sems, 8, opposite))
    z_pass(1, 0, 2)
    x_last(1)
    y_go(0)
    l_take(1)

    @pl.loop(0, tok // step_rows)
    def _(i):
        at = pl.ds(pl.multiple_of(i * step_rows, step_rows), step_rows)
        for q in range(share // 128):
            lanes = slice(q * 128, (q + 1) * 128)
            own = pl.ds(pl.multiple_of(me_t * share + q * 128, 128), 128)
            total = parts[1, me_t, at, lanes].astype(f32) + l_got[1, at, lanes].astype(f32)
            centred = (rows[at, own].astype(f32) - row_mean[at, :]) * row_factor[at, :]
            grad_rows[at, lanes] = (
                row_factor[at, :]
                * (total * gain[:, own] - partial_sums[0, at, :] - centred * partial_sums[1, at, :])
            ).astype(bf16)
    z_take(0, 0, 1)
    z_take(1, 0, 1)
    remote(terms.at[z, yh, c, crossing], y_got.at[crossing], y_sems, 7, opposite).wait_recv()
    remote(terms.at[z, yh, c, kept], y_got.at[kept], y_sems, 8, opposite).wait_recv()

    @pl.loop(0, depth // step_rows)
    def _(i):
        at = pl.ds(pl.multiple_of(i * step_rows, step_rows), step_rows)
        total = terms[z, yh, c, at, :].astype(f32) + y_got[at, :].astype(f32)
        grad_qkv_w[at, :] = total[:, :qkv_cols]
        grad_out_w[at, :] = total[:, qkv_cols:]

    for copy in sent:
        copy.wait_send()


def branch(masks, counts, gain, qk_gain, patches, cotangent, qkv_weight, out_weight):
    bf16, f32 = jnp.bfloat16, jnp.float32
    tok, model = patches.shape
    qkv_cols, out_cols = qkv_weight.shape[1], out_weight.shape[1]
    wide = qkv_cols + out_cols
    depth = model // 32
    share = model // 8
    head_dim = qk_gain.shape[1]
    heads = out_cols // head_dim
    slots = masks.shape[0]
    slot_rows = tok // slots
    hbm = pl.BlockSpec(memory_space=pl.ANY)
    vmem = pl.BlockSpec(memory_space=pltpu.VMEM)
    smem = pl.BlockSpec(memory_space=pltpu.SMEM)
    dma = pltpu.SemaphoreType.DMA
    sems = []
    for n in (5 * slots, 7 * slots, 45, 8, 14, 9, 12, 2, 7):
        sems += [dma((n,)), dma((n,))]
    return pl.pallas_call(
        branch_kernel,
        out_shape=(
            jax.ShapeDtypeStruct((tok, share), bf16),
            jax.ShapeDtypeStruct((tok, share), bf16),
            jax.ShapeDtypeStruct((depth, qkv_cols), f32),
            jax.ShapeDtypeStruct((depth, out_cols), f32),
        ),
        in_specs=[smem, smem, vmem, vmem, hbm, hbm, hbm, hbm],
        out_specs=(vmem,) * 4,
        scratch_shapes=[
            pltpu.VMEM((5, slots, slot_rows, share), bf16),
            pltpu.VMEM((5, slots, slot_rows, share), bf16),
            pltpu.VMEM((tok, model), bf16),
            pltpu.VMEM((model, wide), bf16),
            pltpu.VMEM((tok, model), bf16),
            pltpu.VMEM((tok, model), bf16),
            pltpu.VMEM((tok, 128), f32),
            pltpu.VMEM((tok, 128), f32),
            pltpu.VMEM((tok, qkv_cols), f32),
            pltpu.VMEM((heads, slots, slot_rows, slot_rows), f32),
            pltpu.VMEM((tok, out_cols), bf16),
            pltpu.VMEM((tok, out_cols), bf16),
            pltpu.VMEM((tok, qkv_cols), bf16),
            pltpu.VMEM((NZ, 2, 2, depth, wide), bf16),
            pltpu.VMEM((NZ, 2, depth, wide), bf16),
            pltpu.VMEM((7, depth - G_ROWS, wide), bf16),
            pltpu.VMEM((14, depth, wide), bf16),
            pltpu.VMEM((depth, wide), bf16),
            pltpu.VMEM((2, 8, tok, share), bf16),
            pltpu.VMEM((12, tok, share), bf16),
            pltpu.VMEM((2, tok, share), bf16),
            pltpu.VMEM((2, tok, 128), f32),
            pltpu.VMEM((8, tok), f32),
            pltpu.VMEM((7, 8, tok), f32),
        ]
        + sems
        + [dma((slots + 3,))],
        compiler_params=pltpu.CompilerParams(
            collective_id=0, has_side_effects=True, vmem_limit_bytes=60 * 2**20
        ),
        cost_estimate=pl.CostEstimate(
            flops=13 * 10**9, bytes_accessed=16 * 2**20, transcendentals=150528
        ),
    )(masks, counts, gain, qk_gain, patches, cotangent, qkv_weight, out_weight)


def settle_kernel(*refs):
    n = len(refs) // 3
    sem = refs[-1]
    arrive = [
        pltpu.make_async_copy(refs[i], refs[2 * n + i], sem.at[i]) for i in range(n)
    ]
    leave = [
        pltpu.make_async_copy(refs[2 * n + i], refs[n + i], sem.at[n + i]) for i in range(n)
    ]
    for copy in arrive:
        copy.start()
    for one, other in zip(arrive, leave):
        one.wait()
        other.start()
    for copy in leave:
        copy.wait()


def settle(arrays):
    hbm = pl.BlockSpec(memory_space=pltpu.HBM)
    return pl.pallas_call(
        settle_kernel,
        out_shape=tuple(jax.ShapeDtypeStruct(a.shape, a.dtype) for a in arrays),
        in_specs=[hbm] * len(arrays),
        out_specs=(hbm,) * len(arrays),
        scratch_shapes=[pltpu.VMEM(a.shape, a.dtype) for a in arrays]
        + [pltpu.SemaphoreType.DMA((2 * len(arrays),))],
        compiler_params=pltpu.CompilerParams(vmem_limit_bytes=60 * 2**20),
    )(*arrays)


def per_device(patches, cotangent, counts, masks, norm_gain, qk_gain, qkv_weight, out_weight):
    return settle(
        branch(
            masks, counts.T, norm_gain[None, :], qk_gain, patches, cotangent, qkv_weight, out_weight
        )
    )


def solution(mesh):
    in_specs = (
        P("fsdp", None),
        P("fsdp", None),
        P(),
        P(),
        P(),
        P(),
        P("fsdp", "tp"),
        P("fsdp", "tp"),
    )
    out_specs = (P("fsdp", "tp"), P("fsdp", "tp"), P("fsdp", "tp"), P("fsdp", "tp"))
    return jax.shard_map(
        per_device, mesh=mesh, in_specs=in_specs, out_specs=out_specs, check_vma=False
    )
```

```python
import functools
import jax
import jax.numpy as jnp
from jax import lax
from jax.experimental import pallas as pl
from jax.experimental.pallas import tpu as pltpu
from jax.sharding import PartitionSpec as P

MESH = pl.DeviceIdType.MESH
epsilon = 1e-06
NZ, NX = 8, 4
W_ROWS, G_ROWS = 48, 48


def coords():
    f = lax.axis_index("fsdp")
    t = lax.axis_index("tp")
    z, yh, c = lax.div(f, 4), lax.rem(lax.div(f, 2), 2), lax.rem(f, 2)
    x, yl = lax.div(t, 2), lax.rem(t, 2)
    return z, yh, c, x, yl


def dev(z, yh, c, x, yl):
    return (z * 4 + yh * 2 + c, x * 2 + yl)


def remote(src, dst, sems, slot, target):
    send, recv = sems
    return pltpu.make_async_remote_copy(
        src_ref=src,
        dst_ref=dst,
        send_sem=send.at[slot],
        recv_sem=recv.at[slot],
        device_id=target,
        device_id_type=MESH,
    )


def greet(partners):
    barrier = pltpu.get_barrier_semaphore()
    for partner in partners:
        pl.semaphore_signal(barrier, inc=1, device_id=partner, device_id_type=MESH)
    pl.semaphore_wait(barrier, len(partners))


def head_norm(values):
    centred = values - jnp.mean(values, axis=-1, keepdims=True)
    factor = lax.rsqrt(jnp.mean(centred * centred, axis=-1, keepdims=True) + epsilon)
    return centred * factor, factor


def head_norm_back(upstream, normed, factor):
    return factor * (
        upstream
        - jnp.mean(upstream, axis=-1, keepdims=True)
        - normed * jnp.mean(upstream * normed, axis=-1, keepdims=True)
    )


def dot_nn(a, b):
    return jnp.dot(a, b, preferred_element_type=jnp.float32)


def dot_nt(a, b):
    return lax.dot_general(a, b, (((1,), (1,)), ((), ())), preferred_element_type=jnp.float32)


def dot_tn(a, b):
    return lax.dot_general(a, b, (((0,), (0,)), ((), ())), preferred_element_type=jnp.float32)


def exact_dot(a, b, dims):
    return lax.dot_general(
        a, b, (dims, ((), ())),
        precision=lax.Precision.HIGHEST, preferred_element_type=jnp.float32,
    )


def add_into(total, other, rows_at=32):
    @pl.loop(0, total.shape[0] // rows_at, unroll=True)
    def _(i):
        at = pl.ds(pl.multiple_of(i * rows_at, rows_at), rows_at)
        total[at, :] = (
            total[at, :].astype(jnp.float32) + other[at, :].astype(jnp.float32)
        ).astype(total.dtype)


def branch_kernel(
    masks_ref, counts_ref, gain, qk_gain, patches, cotangent, qkv_w, out_w,
    attended, grad_rows, grad_qkv_w, grad_out_w,
    hold, got, rows, weights, upstream, normed, row_mean, row_factor, projected, attention,
    mixed, grad_mixed, grad_qkv, terms, theirs, y_part, z_got, y_got, parts, x_got, l_got,
    partial_sums, sums, sums_got,
    a_send, a_recv, b_send, b_recv, c_send, c_recv,
    core_send, core_recv, z_send_sem, z_recv_sem, y_send, y_recv,
    x_send, x_recv, l_send, l_recv, s_send, s_recv, local_sem,
):
    f32, bf16 = jnp.float32, jnp.bfloat16
    z, yh, c, x, yl = coords()
    me_t = x * 2 + yl
    tok, model = rows.shape
    share = attended.shape[1]
    heads = attention.shape[0]
    slots, slot_rows = attention.shape[1], attention.shape[2]
    head_dim = qk_gain.shape[1]
    qkv_cols, out_cols = grad_qkv_w.shape[1], grad_out_w.shape[1]
    depth = grad_qkv_w.shape[0]
    band = 4 * depth
    z_up, z_down = lax.rem(z + 1, NZ), lax.rem(z + NZ - 1, NZ)
    x_up, x_down = lax.rem(x + 1, NX), lax.rem(x + NX - 1, NX)
    sibling = dev(z, yh, 1 - c, x, yl)
    opposite = dev(z, 1 - yh, c, x, yl)
    beside = dev(z, yh, c, x, 1 - yl)
    up, down = dev(z_up, yh, c, x, yl), dev(z_down, yh, c, x, yl)
    right, left = dev(z, yh, c, x_up, yl), dev(z, yh, c, x_down, yl)
    across = dev(z, 1 - yh, c, x, 1 - yl)
    z7 = dev(7 - z, yh, c, x, yl)
    z3 = dev(z + 3 - 2 * lax.rem(z, 4), yh, c, x, yl)
    z1 = dev(z + 1 - 2 * lax.rem(z, 2), yh, c, x, yl)
    my_f = z * 4 + yh * 2 + c
    peers = [(my_f, lax.rem(me_t + o, 8)) for o in range(1, 8)]
    f32, bf16 = jnp.float32, jnp.bfloat16

    def live_count(k):
        return counts_ref[k, jnp.bitwise_xor(my_f, masks_ref[k])]

    def mask_bit(k, place):
        return jnp.bitwise_and(lax.shift_right_logical(masks_ref[k], place), 1)

    def takes(k, step):
        which = -1 if step == 0 else order[k][step - 1]
        if which in (-1, 7, 0):
            return mask_bit(k, {-1: 1, 7: 4, 0: 0}[which]) > 0
        places = (3, 4) if which == 3 else (2, 3)
        return mask_bit(k, places[0]) != mask_bit(k, places[1])

    def slot_at(s):
        return pl.ds(s * slot_rows, slot_rows)

    def columns(index):
        return pl.ds(pl.multiple_of(index * share, 128), share)

    def weight_at(index, first, count):
        return weights.at[pl.ds(pl.multiple_of(index * depth + first, 16), count), :]

    own = [
        pltpu.make_async_copy(patches.at[slot_at(k), columns(me_t)], hold.at[0, k], local_sem.at[k])
        for k in range(slots)
    ]
    mine = pl.ds(pl.multiple_of(my_f * depth, 16), depth)
    own_w = [
        pltpu.make_async_copy(qkv_w, weights.at[mine, pl.ds(0, qkv_cols)], local_sem.at[slots]),
        pltpu.make_async_copy(
            out_w, weights.at[mine, pl.ds(qkv_cols, out_cols)], local_sem.at[slots + 1]
        ),
    ]
    load = pltpu.make_async_copy(cotangent, upstream, local_sem.at[slots + 2])
    for copy in own_w + own + [load]:
        copy.start()
    greet([across, z7, z3, z1, sibling, opposite, up, down] + peers)
    sent = []

    def go(copy):
        copy.start()
        sent.append(copy)

    a_sems, b_sems, c_sems = (a_send, a_recv), (b_send, b_recv), (c_send, c_recv)
    core_sems, z_sems = (core_send, core_recv), (z_send_sem, z_recv_sem)
    y_sems, x_sems, l_sems = (y_send, y_recv), (x_send, x_recv), (l_send, l_recv)
    s_sems = (s_send, s_recv)
    step_rows = 16
    per_slot = slot_rows // step_rows
    qkv_part, out_part = pl.ds(0, qkv_cols), pl.ds(qkv_cols, out_cols)
    limits = {(0, 0): 4, (0, 1): 3, (1, 0): 3, (1, 1): 4}

    def z_at(distance):
        return lax.rem(z + distance + NZ, NZ)

    def y_of(kind):
        return yh if kind == 0 else 1 - yh

    w_slot = {}

    def w_index(key):
        if key not in w_slot:
            w_slot[key] = len(w_slot)
        return w_slot[key]

    def w_copy(route, piece, target, core=0):
        distance, kind, first, count = piece
        owner = z_at(distance) * 4 + y_of(kind) * 2 + (1 - c if core else c)
        view = weight_at(owner, first, count)
        return remote(view, view, c_sems, w_index((route, piece)), target)

    def w_core(piece):
        go(w_copy("core", piece, sibling))

    def w_core_take(piece):
        w_copy("core", piece, sibling, 1).wait_recv()

    def w_rows(kind):
        return (0, depth) if kind == 0 else (0, W_ROWS)

    rest = (W_ROWS, depth - W_ROWS)

    def w_route(direction):
        return "up" if direction == 0 else "down"

    def w_send(direction, kind, travelled):
        signed = -travelled if direction == 0 else travelled
        first, count = w_rows(kind)
        owner = z_at(signed) * 4 + y_of(kind) * 2 + c
        view = weight_at(owner, first, count)
        there = -travelled - 1 if direction == 0 else travelled + 1
        slot = w_index((w_route(direction), (there, kind, first, count)))
        go(remote(view, view, c_sems, slot, up if direction == 0 else down))

    def w_take(kind, d):
        for direction in range(2):
            if d <= limits[direction, kind]:
                signed = -d if direction == 0 else d
                piece = (signed, kind) + w_rows(kind)
                w_copy(w_route(direction), piece, up).wait_recv()
                if kind == 0:
                    owner = z_at(signed) * 4 + yh * 2 + c
                    view = weight_at(owner, *rest)
                    go(remote(view, view, c_sems, w_index(("y", (signed, 1) + rest)), opposite))
                w_core(piece)

    def w_pass(kind, d):
        for direction in range(2):
            if d < limits[direction, kind]:
                w_send(direction, kind, d)

    def w_across(signed):
        piece = (signed, 1) + rest
        w_copy("y", piece, opposite).wait_recv()
        w_core(piece)

    for k in range(slots):
        go(remote(patches.at[slot_at(k), columns(x * 2 + 1 - yl)], got.at[0, k], a_sems, k, across))
    for copy in own_w:
        copy.wait()
    whole = (0, depth)
    for copy in own:
        copy.wait()

    partner = {3: z3, 7: z7, 1: z1, 0: sibling}
    order = [[7, 3, 1, 0], [3, 7, 1, 0], [7, 3, 1, 0], [3, 7, 1, 0]]

    def merge(k, step):
        remote(got.at[step, k], got.at[step, k], a_sems, step * slots + k, sibling).wait_recv()
        taken = takes(k, step)
        return lax.select_n(taken, hold[step, k], got[step, k])

    def row_step(step, which_slots=(0, 1, 2, 3)):
        for k in which_slots:
            hold[step + 1, k] = merge(k, step)
            go(
                remote(
                    hold.at[step + 1, k], got.at[step + 1, k], a_sems,
                    (step + 1) * slots + k, partner[order[k][step]],
                )
            )

    def row_copy(k, xx, y_low, which, target):
        view = rows.at[slot_at(k), columns(xx * 2 + y_low)]
        return remote(view, view, b_sems, k * 7 + which, target)

    def rows_first(k):
        merged = merge(k, 4).astype(f32)
        place = lax.broadcasted_iota(jnp.int32, (slot_rows, share), 0)
        live = place < live_count(k)
        rows[slot_at(k), columns(me_t)] = jnp.where(live, merged, 0.0).astype(bf16)
        go(row_copy(k, x, yl, 0, beside))
        go(row_copy(k, x, yl, 1, right))
        go(row_copy(k, x, yl, 4, left))

    def rows_second(k):
        row_copy(k, x, 1 - yl, 0, beside).wait_recv()
        go(row_copy(k, x, 1 - yl, 3, right))
        go(row_copy(k, x, 1 - yl, 5, left))

    def rows_third(k):
        row_copy(k, x_down, yl, 1, right).wait_recv()
        go(row_copy(k, x_down, yl, 2, right))
        row_copy(k, x_up, 1 - yl, 5, left).wait_recv()
        go(row_copy(k, x_up, 1 - yl, 6, left))

    def rows_last(k):
        row_copy(k, lax.rem(x + 2, NX), yl, 2, right).wait_recv()
        row_copy(k, x_down, 1 - yl, 3, right).wait_recv()
        row_copy(k, x_up, yl, 4, left).wait_recv()
        row_copy(k, lax.rem(x + 2, NX), 1 - yl, 6, left).wait_recv()

    def norm_slot(k):
        @pl.loop(0, per_slot, unroll=True)
        def _(i):
            at = pl.ds(pl.multiple_of(k * slot_rows + i * step_rows, step_rows), step_rows)
            values = rows[at, :].astype(f32)
            mean = jnp.mean(values, axis=-1, keepdims=True)
            centred = values - mean
            factor = lax.rsqrt(jnp.mean(centred * centred, axis=-1, keepdims=True) + epsilon)
            normed[at, :] = (centred * factor * gain[...]).astype(bf16)
            row_mean[at, :] = jnp.broadcast_to(mean, (step_rows, 128))
            row_factor[at, :] = jnp.broadcast_to(factor, (step_rows, 128))

    def project(distance):
        if distance == 0:
            for kind in range(2):
                w_core_take((0, kind) + whole)
        else:
            for kind, part in ((0, whole), (1, (0, W_ROWS)), (1, rest)):
                signed = distance
                if abs(distance) == 4:
                    signed = 4 if (kind, part) == (1, (0, W_ROWS)) else -4
                w_core_take((signed, kind) + part)
        at = pl.ds(pl.multiple_of(z_at(distance) * band, band), band)
        part = dot_nn(normed[:, at], weights[at, qkv_part])
        if distance == 0:
            projected[...] = part
        else:
            projected[...] += part

    def live_rows(i, shape):
        place = lax.broadcasted_iota(jnp.int32, shape, 0) + lax.rem(i, per_slot) * step_rows
        return place < live_count(lax.div(i, per_slot))

    w_pass(0, 0)
    row_step(0, (0, 1, 2, 3))
    view = weight_at(my_f, *whole)
    go(remote(view, view, c_sems, w_index(("y", (0, 1) + whole)), opposite))
    w_core((0, 0) + whole)
    w_take(0, 1)
    row_step(1, (0, 1, 2, 3))
    load.wait()

    @pl.loop(0, tok // step_rows)
    def _(i):
        at = pl.ds(pl.multiple_of(i * step_rows, step_rows), step_rows)
        values = upstream[at, :].astype(f32)
        upstream[at, :] = jnp.where(live_rows(i, values.shape), values, 0.0).astype(bf16)
    w_copy("y", (0, 1) + whole, opposite).wait_recv()
    w_core((0, 1) + whole)
    row_step(2, (0, 1, 2, 3))
    w_pass(0, 1)
    w_pass(1, 0)
    w_across(-1)
    w_across(1)
    row_step(3, (0, 1, 2, 3))
    rows_first(0)
    rows_first(1)
    rows_first(2)
    rows_first(3)
    w_take(0, 2)
    w_pass(0, 2)
    rows_second(0)
    rows_second(1)
    rows_second(2)
    rows_second(3)
    w_take(1, 1)
    w_pass(1, 1)
    rows_third(0)
    rows_third(1)
    rows_third(2)
    rows_third(3)
    w_across(-2)
    w_across(2)
    w_take(0, 3)
    w_pass(0, 3)
    w_take(1, 2)
    w_pass(1, 2)
    rows_last(0)
    norm_slot(0)
    rows_last(1)
    norm_slot(1)
    w_across(-3)
    w_across(3)
    rows_last(2)
    norm_slot(2)
    rows_last(3)
    norm_slot(3)
    w_take(0, 4)
    w_take(1, 3)
    w_pass(1, 3)
    project(0)
    project(-1)
    project(1)
    project(-2)
    project(2)
    w_take(1, 4)
    w_across(-4)
    project(-3)
    project(3)
    project(4)

    gathered = len(sent)
    query_scale = qk_gain[0:1, :] * head_dim ** (-0.5)
    key_scale = qk_gain[1:2, :]

    def head_at(h, which):
        return pl.ds(pl.multiple_of((h * 3 + which) * head_dim, head_dim), head_dim)

    def mixed_at(h):
        return pl.ds(pl.multiple_of(h * head_dim, head_dim), head_dim)

    def head_rows(h, s):
        query_hat, query_factor = head_norm(projected[slot_at(s), head_at(h, 0)])
        key_hat, key_factor = head_norm(projected[slot_at(s), head_at(h, 1)])
        values = projected[slot_at(s), head_at(h, 2)].astype(bf16)
        return (
            (query_hat, query_factor, (query_hat * query_scale).astype(bf16)),
            (key_hat, key_factor, (key_hat * key_scale).astype(bf16)),
            values,
        )

    @pl.loop(0, heads, unroll=True)
    def _(h):
        i = lax.broadcasted_iota(jnp.int32, (slot_rows, slot_rows), 0)
        j = lax.broadcasted_iota(jnp.int32, (slot_rows, slot_rows), 1)
        for s in range(slots):
            (_, _, query), (_, _, key_rows), values = head_rows(h, s)
            count = live_count(s)
            allowed = (jnp.maximum(i, j) < count) | (i == j)
            raised = jnp.where(allowed, jnp.exp(dot_nt(query, key_rows)), 0.0)
            weight = raised / jnp.sum(raised, axis=-1, keepdims=True)
            attention[h, s] = weight
            mixed[slot_at(s), mixed_at(h)] = dot_nn(weight.astype(bf16), values).astype(bf16)

    x_limits = {(0, 0): 2, (0, 1): 1, (1, 0): 1, (1, 1): 2}
    x_slot = {}
    for p in range(2):
        for direction in range(2):
            for kind in range(2):
                for d in range(x_limits[direction, kind], 0, -1):
                    x_slot[p, direction, kind, d] = len(x_slot)

    def x_shard(direction, kind, d):
        xx = lax.rem(x + (d if direction == 0 else NX - d), NX)
        return xx * 2 + (yl if kind == 0 else 1 - yl)

    def x_go(p, direction, kind, d):
        slot = x_slot[p, direction, kind, d]
        go(
            remote(
                parts.at[p, x_shard(direction, kind, d)], x_got.at[slot], x_sems, slot,
                right if direction == 0 else left,
            )
        )

    def x_take(p, direction, kind, d):
        slot = x_slot[p, direction, kind, d]
        shard = x_shard(direction, kind, d - 1)
        remote(parts.at[p, shard], x_got.at[slot], x_sems, slot, right).wait_recv()
        add_into(parts.at[p, shard], x_got.at[slot])

    def x_first(p):
        x_go(p, 0, 0, 2)
        x_go(p, 1, 1, 2)

    def x_second(p):
        x_take(p, 1, 1, 2)
        x_go(p, 1, 1, 1)
        x_go(p, 0, 1, 1)
        x_take(p, 0, 0, 2)

    def x_third(p):
        x_take(p, 0, 1, 1)
        x_take(p, 1, 1, 1)
        go(remote(parts.at[p, x * 2 + 1 - yl], l_got.at[p], l_sems, p, beside))
        x_go(p, 0, 0, 1)
        x_go(p, 1, 0, 1)

    def x_last(p):
        x_take(p, 1, 0, 1)
        x_take(p, 0, 0, 1)

    def l_take(p):
        remote(parts.at[p, me_t], l_got.at[p], l_sems, p, beside).wait_recv()

    def shard_rows(shard):
        return pl.ds(pl.multiple_of(shard * share, share), share)

    @pl.loop(0, 8, unroll=2)
    def _(shard):
        parts[0, shard] = dot_nt(mixed[...], weights[shard_rows(shard), out_part]).astype(bf16)

    x_first(0)

    grad_mixed[...] = dot_nn(upstream[...], weights[:, out_part]).astype(bf16)

    @pl.loop(0, heads, unroll=True)
    def _(h):
        for s in range(slots):
            (query_hat, query_factor, query), (key_hat, key_factor, key_rows), values = head_rows(
                h, s
            )
            weight = attention[h, s]
            rounded = weight.astype(bf16)
            above = grad_mixed[slot_at(s), mixed_at(h)]
            grad_value = dot_tn(rounded, above)
            grad_weight = dot_nt(above, values)
            grad_scores = weight * (
                grad_weight - jnp.sum(weight * grad_weight, axis=-1, keepdims=True)
            )
            grad_scores = grad_scores.astype(bf16)
            grad_query = dot_nn(grad_scores, key_rows)
            grad_key = dot_tn(grad_scores, query)
            grad_qkv[slot_at(s), head_at(h, 0)] = head_norm_back(
                grad_query * query_scale, query_hat, query_factor
            ).astype(bf16)
            grad_qkv[slot_at(s), head_at(h, 1)] = head_norm_back(
                grad_key * key_scale, key_hat, key_factor
            ).astype(bf16)
            grad_qkv[slot_at(s), head_at(h, 2)] = grad_value.astype(bf16)

    distances = [4, 3, -3, 2, -2, 1, -1, 0]
    kept = pl.ds(0, G_ROWS)
    crossing = pl.ds(G_ROWS, depth - G_ROWS)

    def compute(distance):
        zz = z_at(distance)
        at = pl.ds(pl.multiple_of(zz * band, band), band)
        left_term = dot_tn(normed[:, at], grad_qkv[...]).astype(bf16)
        for q in range(4):
            terms[zz, q // 2, q % 2, :, 0:qkv_cols] = left_term[q * depth : (q + 1) * depth]
        right_term = dot_tn(upstream[:, at], mixed[...]).astype(bf16)
        for q in range(4):
            terms[zz, q // 2, q % 2, :, qkv_cols:] = right_term[q * depth : (q + 1) * depth]
        go(
            remote(
                terms.at[zz, :, 1 - c], theirs.at[zz], core_sems, distances.index(distance), sibling
            )
        )

    def have(distance):
        zz = z_at(distance)
        remote(
            terms.at[zz, :, c], theirs.at[zz], core_sems, distances.index(distance), sibling
        ).wait_recv()
        for y in range(2):
            add_into(terms.at[zz, y, c], theirs.at[zz, y])

    def y_go(distance):
        i = distances.index(distance)
        zz = z_at(distance)
        target = y_got.at[crossing] if distance == 0 else y_part.at[i]
        go(remote(terms.at[zz, 1 - yh, c, crossing], target, y_sems, i, opposite))

    def y_take(distance):
        i = distances.index(distance)
        zz = z_at(distance)
        remote(terms.at[zz, yh, c, crossing], y_part.at[i], y_sems, i, opposite).wait_recv()
        add_into(terms.at[zz, yh, c, crossing], y_part.at[i], 16)

    z_slot = {}
    for direction in range(2):
        for kind in range(2):
            for d in range(limits[direction, kind], 0, -1):
                z_slot[direction, kind, d] = len(z_slot)

    def z_views(kind, zz, slot):
        if kind == 0:
            return terms.at[zz, yh, c], z_got.at[slot]
        return terms.at[zz, 1 - yh, c, kept], z_got.at[slot, kept]

    def z_go(direction, kind, d):
        zz = z_at(d if direction == 0 else -d)
        slot = z_slot[direction, kind, d]
        here, there = z_views(kind, zz, slot)
        go(remote(here, there, z_sems, slot, up if direction == 0 else down))

    def z_take(direction, kind, d):
        zz = z_at(d - 1 if direction == 0 else 1 - d)
        slot = z_slot[direction, kind, d]
        here, arrived = z_views(kind, zz, slot)
        remote(here, arrived, z_sems, slot, up).wait_recv()
        add_into(here, arrived, 16)

    def z_pass(direction, kind, d):
        z_take(direction, kind, d)
        z_go(direction, kind, d - 1)

    partial_sums[...] = jnp.zeros(partial_sums.shape, f32)

    def back_part(distance):
        @pl.loop(0, 2, unroll=True)
        def _(low):
            shard = lax.rem(x + distance, NX) * 2 + low
            at = shard_rows(shard)
            part = dot_nt(grad_qkv[...], weights[at, qkv_part]).astype(bf16)
            parts[1, shard] = part
            scaled = part.astype(f32) * gain[:, at]
            for q in range(share // 128):
                lanes = slice(q * 128, (q + 1) * 128)
                own = pl.ds(pl.multiple_of(shard * share + q * 128, 128), 128)
                centred = (rows[:, own].astype(f32) - row_mean[...]) * row_factor[...]
                partial_sums[0] += scaled[:, lanes]
                partial_sums[1] += scaled[:, lanes] * centred
    compute(4)
    compute(-3)
    compute(3)
    x_second(0)
    have(4)
    y_go(4)
    compute(2)
    have(-3)
    have(3)
    back_part(2)
    z_go(1, 1, 4)
    z_go(0, 1, 3)
    y_go(-3)
    x_first(1)
    back_part(1)
    have(2)
    y_go(2)
    y_take(4)
    z_go(0, 0, 4)
    compute(-2)
    z_pass(0, 1, 3)
    compute(1)
    y_take(-3)
    z_pass(1, 1, 4)
    y_go(3)
    back_part(0)
    x_third(0)
    z_go(1, 0, 3)
    have(-2)
    compute(0)
    back_part(3)
    y_take(3)
    have(0)
    y_go(-2)
    z_pass(0, 0, 4)
    have(1)
    z_pass(0, 1, 2)
    z_pass(1, 1, 3)
    x_second(1)
    compute(-1)
    have(-1)
    y_go(1)
    y_go(-1)
    for copy in sent[:gathered]:
        copy.wait_send()
    del sent[:gathered]
    z_pass(1, 1, 2)
    z_take(1, 1, 1)
    z_take(0, 1, 1)
    y_take(2)
    z_pass(0, 0, 3)
    y_take(-2)
    z_pass(1, 0, 3)
    x_third(1)
    ones = jnp.ones((8, 128), f32)
    upper = lax.broadcasted_iota(jnp.int32, (8, tok), 0) < 4
    sums[...] = jnp.where(
        upper,
        exact_dot(ones, partial_sums[0], ((1,), (1,))),
        exact_dot(ones, partial_sums[1], ((1,), (1,))),
    )
    for o, peer in enumerate(peers):
        go(remote(sums, sums_got.at[o], s_sems, o, peer))
    y_take(1)
    x_last(0)
    total_sums = sums[...]
    for o, peer in enumerate(peers):
        remote(sums, sums_got.at[o], s_sems, o, peer).wait_recv()
        total_sums += sums_got[o]
    pick = lax.broadcasted_iota(jnp.int32, (8, 128), 0)
    partial_sums[0] = exact_dot(
        total_sums, jnp.where(pick == 0, 1.0 / model, 0.0).astype(f32), ((0,), (0,))
    )
    partial_sums[1] = exact_dot(
        total_sums, jnp.where(pick == 4, 1.0 / model, 0.0).astype(f32), ((0,), (0,))
    )
    y_take(-1)
    l_take(0)

    @pl.loop(0, tok // step_rows)
    def _(i):
        at = pl.ds(pl.multiple_of(i * step_rows, step_rows), step_rows)
        total = parts[0, me_t, at, :].astype(f32) + l_got[0, at, :].astype(f32)
        attended[at, :] = jnp.where(live_rows(i, total.shape), total, 0.0).astype(bf16)
    z_pass(0, 0, 2)
    go(remote(terms.at[z, 1 - yh, c, kept], y_got.at[kept], y_sems, 8, opposite))
    z_pass(1, 0, 2)
    x_last(1)
    y_go(0)
    l_take(1)

    @pl.loop(0, tok // step_rows)
    def _(i):
        at = pl.ds(pl.multiple_of(i * step_rows, step_rows), step_rows)
        for q in range(share // 128):
            lanes = slice(q * 128, (q + 1) * 128)
            own = pl.ds(pl.multiple_of(me_t * share + q * 128, 128), 128)
            total = parts[1, me_t, at, lanes].astype(f32) + l_got[1, at, lanes].astype(f32)
            centred = (rows[at, own].astype(f32) - row_mean[at, :]) * row_factor[at, :]
            grad_rows[at, lanes] = (
                row_factor[at, :]
                * (total * gain[:, own] - partial_sums[0, at, :] - centred * partial_sums[1, at, :])
            ).astype(bf16)
    z_take(0, 0, 1)
    z_take(1, 0, 1)
    remote(terms.at[z, yh, c, crossing], y_got.at[crossing], y_sems, 7, opposite).wait_recv()
    remote(terms.at[z, yh, c, kept], y_got.at[kept], y_sems, 8, opposite).wait_recv()

    @pl.loop(0, depth // step_rows)
    def _(i):
        at = pl.ds(pl.multiple_of(i * step_rows, step_rows), step_rows)
        total = terms[z, yh, c, at, :].astype(f32) + y_got[at, :].astype(f32)
        grad_qkv_w[at, :] = total[:, :qkv_cols]
        grad_out_w[at, :] = total[:, qkv_cols:]

    for copy in sent:
        copy.wait_send()


def branch(masks, counts, gain, qk_gain, patches, cotangent, qkv_weight, out_weight):
    bf16, f32 = jnp.bfloat16, jnp.float32
    tok, model = patches.shape
    qkv_cols, out_cols = qkv_weight.shape[1], out_weight.shape[1]
    wide = qkv_cols + out_cols
    depth = model // 32
    share = model // 8
    head_dim = qk_gain.shape[1]
    heads = out_cols // head_dim
    slots = masks.shape[0]
    slot_rows = tok // slots
    hbm = pl.BlockSpec(memory_space=pl.ANY)
    vmem = pl.BlockSpec(memory_space=pltpu.VMEM)
    smem = pl.BlockSpec(memory_space=pltpu.SMEM)
    dma = pltpu.SemaphoreType.DMA
    sems = []
    for n in (5 * slots, 7 * slots, 45, 8, 14, 9, 12, 2, 7):
        sems += [dma((n,)), dma((n,))]
    return pl.pallas_call(
        branch_kernel,
        out_shape=(
            jax.ShapeDtypeStruct((tok, share), bf16),
            jax.ShapeDtypeStruct((tok, share), bf16),
            jax.ShapeDtypeStruct((depth, qkv_cols), f32),
            jax.ShapeDtypeStruct((depth, out_cols), f32),
        ),
        in_specs=[smem, smem, vmem, vmem, hbm, hbm, hbm, hbm],
        out_specs=(vmem,) * 4,
        scratch_shapes=[
            pltpu.VMEM((5, slots, slot_rows, share), bf16),
            pltpu.VMEM((5, slots, slot_rows, share), bf16),
            pltpu.VMEM((tok, model), bf16),
            pltpu.VMEM((model, wide), bf16),
            pltpu.VMEM((tok, model), bf16),
            pltpu.VMEM((tok, model), bf16),
            pltpu.VMEM((tok, 128), f32),
            pltpu.VMEM((tok, 128), f32),
            pltpu.VMEM((tok, qkv_cols), f32),
            pltpu.VMEM((heads, slots, slot_rows, slot_rows), f32),
            pltpu.VMEM((tok, out_cols), bf16),
            pltpu.VMEM((tok, out_cols), bf16),
            pltpu.VMEM((tok, qkv_cols), bf16),
            pltpu.VMEM((NZ, 2, 2, depth, wide), bf16),
            pltpu.VMEM((NZ, 2, depth, wide), bf16),
            pltpu.VMEM((7, depth - G_ROWS, wide), bf16),
            pltpu.VMEM((14, depth, wide), bf16),
            pltpu.VMEM((depth, wide), bf16),
            pltpu.VMEM((2, 8, tok, share), bf16),
            pltpu.VMEM((12, tok, share), bf16),
            pltpu.VMEM((2, tok, share), bf16),
            pltpu.VMEM((2, tok, 128), f32),
            pltpu.VMEM((8, tok), f32),
            pltpu.VMEM((7, 8, tok), f32),
        ]
        + sems
        + [dma((slots + 3,))],
        compiler_params=pltpu.CompilerParams(
            collective_id=0, has_side_effects=True, vmem_limit_bytes=60 * 2**20
        ),
        cost_estimate=pl.CostEstimate(
            flops=13 * 10**9, bytes_accessed=16 * 2**20, transcendentals=150528
        ),
    )(masks, counts, gain, qk_gain, patches, cotangent, qkv_weight, out_weight)


def settle_kernel(*refs):
    n = len(refs) // 3
    sem = refs[-1]
    arrive = [
        pltpu.make_async_copy(refs[i], refs[2 * n + i], sem.at[i]) for i in range(n)
    ]
    leave = [
        pltpu.make_async_copy(refs[2 * n + i], refs[n + i], sem.at[n + i]) for i in range(n)
    ]
    for copy in arrive:
        copy.start()
    for one, other in zip(arrive, leave):
        one.wait()
        other.start()
    for copy in leave:
        copy.wait()


def settle(arrays):
    hbm = pl.BlockSpec(memory_space=pltpu.HBM)
    return pl.pallas_call(
        settle_kernel,
        out_shape=tuple(jax.ShapeDtypeStruct(a.shape, a.dtype) for a in arrays),
        in_specs=[hbm] * len(arrays),
        out_specs=(hbm,) * len(arrays),
        scratch_shapes=[pltpu.VMEM(a.shape, a.dtype) for a in arrays]
        + [pltpu.SemaphoreType.DMA((2 * len(arrays),))],
        compiler_params=pltpu.CompilerParams(vmem_limit_bytes=60 * 2**20),
    )(*arrays)


def per_device(patches, cotangent, counts, masks, norm_gain, qk_gain, qkv_weight, out_weight):
    return settle(
        branch(
            masks, counts.T, norm_gain[None, :], qk_gain, patches, cotangent, qkv_weight, out_weight
        )
    )


def solution(mesh):
    in_specs = (
        P("fsdp", None),
        P("fsdp", None),
        P(),
        P(),
        P(),
        P(),
        P("fsdp", "tp"),
        P("fsdp", "tp"),
    )
    out_specs = (P("fsdp", "tp"), P("fsdp", "tp"), P("fsdp", "tp"), P("fsdp", "tp"))
    return jax.shard_map(
        per_device, mesh=mesh, in_specs=in_specs, out_specs=out_specs, check_vma=False
    )
```
